256 devices in a mesh: pix: 32 (over z, y), ang: 8 (over x, core).
Axes of the slice: x: 4, y: 4, z: 8, core: 2. Of those that a mesh axis runs over, the one named last changes fastest.
Arguments:
- tiles: float32 [32, 8, 512, 4096], P('pix', 'ang'), may hold values from 0.01 to 1
- tile_ray: int32 [32, 8, 512], P('pix', 'ang'), may hold values from 0 to 127, as said below
- tile_pix: int32 [32, 8, 512], P('pix', 'ang'), may hold values from 0 to 15, as said below
- tile_count: int32 [32, 8], P('pix', 'ang'), may hold values from 128 to 512, as said below
- ray_slot: int32 [8, 128], P('ang'), may hold values from 0 to 127, as said below
- image: float32 [32768, 128], P(('pix', 'ang')), may hold values from 0 to 2
- measured: float32 [8, 8192, 128], P('ang', 'pix'), may hold values from -6144 to 6144
Outputs:
- new_image: float32 [32768, 128], P(('pix', 'ang'))
- scaled_resid: float32 [8, 8192, 128], P('ang', 'pix')
The draws below stay inside these ranges and needn't reach their ends.
Inputs may be any that keep to these rules, and one draw needn't show every extreme that they name: Device (p, a) uses only its first tile_count[p, a] tiles; some device uses all 512. `tile_ray`: the used tiles of the devices of one angle group a together name every ray block of that group. `tile_pix`: the used tiles of the devices of one region p together name every pixel block of that region. `ray_slot`: each row is a permutation; slot s lies on the device with pix index s // 4.
All inputs are finite; a program needn't handle non-finite values.
Results may differ from the reference program's by a relative error of at most 0.0003.
Values sent between devices are 32-bit elements; how exact they have to be, the bound alone decides.
A program may use at most 64 MiB of HBM per device.

```python
import math
import jax
import jax.numpy as jnp
from jax import lax

BLK = 64
S = 128
SLOTS = 512
RBD = 4
PXB_DEV = 2
RB_A = 128
RAYS_A = 8192
PB = 16
NPIX = 32768
N_PIX = 32
N_ANG = 8


def draw_tile_count(key, part):
    first_key, second_key = jax.random.split(jax.random.fold_in(key, 7))
    counts = jax.random.randint(first_key, (N_PIX * N_ANG,), SLOTS // 4, SLOTS + 1)
    busiest = jax.random.randint(second_key, (), 0, N_PIX * N_ANG)
    counts = counts.at[busiest].set(SLOTS)
    return counts.reshape(N_PIX, N_ANG).astype(jnp.int32)


def draw_tile_ray(key, part):
    first_key, second_key = jax.random.split(jax.random.fold_in(key, 11))
    random_rays = jax.random.randint(first_key, (N_PIX, N_ANG, SLOTS), 0, RB_A)
    shifts = jax.random.randint(second_key, (N_PIX, N_ANG, 1), 0, RBD)
    positions = jnp.arange(SLOTS)[None, None, :]
    owners = jnp.arange(N_PIX)[:, None, None]
    covering = owners * RBD + (positions + shifts) % RBD
    return jnp.where(positions < RBD, covering, random_rays).astype(jnp.int32)


def draw_tile_pix(key, part):
    first_key, second_key = jax.random.split(jax.random.fold_in(key, 13))
    random_pixels = jax.random.randint(first_key, (N_PIX, N_ANG, SLOTS), 0, PB)
    shifts = jax.random.randint(second_key, (N_PIX, N_ANG, 1), 0, PXB_DEV)
    positions = jnp.arange(SLOTS)[None, None, :]
    angles = jnp.arange(N_ANG)[None, :, None]
    covering = angles * PXB_DEV + (positions + shifts) % PXB_DEV
    return jnp.where(positions < PXB_DEV, covering, random_pixels).astype(jnp.int32)


def draw_ray_slot(key, part):
    keys = jax.random.split(jax.random.fold_in(key, 17), N_ANG)
    return jax.vmap(lambda single_key: jax.random.permutation(single_key, RB_A))(keys).astype(jnp.int32)


def block_scale(key, dims, shards, low, largest):
    def one(dim, shards_of):
        steps = jax.random.uniform(jax.random.fold_in(jax.random.fold_in(key, 6), dim), (shards_of,), jnp.float32, low / len(shards), largest / len(shards))
        return jnp.repeat(jnp.exp(steps), dims[dim] // shards_of).reshape((-1,) + (1,) * (len(dims) - dim - 1))

    gain = one(*shards[0])
    for cut in shards[1:]:
        gain = gain * one(*cut)
    return gain


def normal_values(rng, shape, deviation, most, cuts=(), kind=jnp.bfloat16):
    array = jax.random.normal(rng, shape, jnp.float32) * deviation
    if len(cuts) > 0:
        array = block_scale(rng, shape, cuts, -0.22, 0.18) * array
    return jnp.clip(array, min=-most, max=most).astype(kind)


def setup_inputs(seed: int = 0) -> dict:
    key_of = jax.random.split(jax.random.key(seed), 8)
    return {
        "tiles": jnp.clip(jnp.exp(math.log(1.0) - 4.6051702 * jax.random.uniform(key_of[0], (N_PIX, N_ANG, SLOTS, BLK * BLK), jnp.float32) ** block_scale(key_of[0], (N_PIX, N_ANG, SLOTS, BLK * BLK), ((0, 32), (1, 8)), -0.2, 0.2)), 0.01, 1.0),
        "tile_ray": draw_tile_ray(jax.random.fold_in(key_of[7], 71), 0),
        "tile_pix": draw_tile_pix(jax.random.fold_in(key_of[7], 71), 0),
        "tile_count": draw_tile_count(jax.random.fold_in(key_of[7], 71), 0),
        "ray_slot": draw_ray_slot(jax.random.fold_in(key_of[7], 71), 0),
        "image": jnp.clip(2.0 * jax.random.uniform(key_of[5], (NPIX, S), jnp.float32) ** block_scale(key_of[5], (NPIX, S), ((0, 256),), -0.2, 0.2), 0.0, 2.0),
        "measured": normal_values(key_of[6], (N_ANG, RAYS_A, S), (SLOTS * BLK // (8 * RBD)), 6144.0, ((0, 8), (1, 32)), jnp.float32),
    }


relax_factor = 0.9


def reference(tiles, tile_ray, tile_pix, tile_count, ray_slot, image, measured):
    group_image = image.reshape(N_PIX, PB, BLK, S)
    positions = jnp.arange(SLOTS, dtype=jnp.int32)

    def device_tiles(device):
        region = device // N_ANG
        angle = device % N_ANG
        active = (positions < tile_count[region, angle]).astype(jnp.float32)
        matrices = tiles[region, angle].reshape(SLOTS, BLK, BLK) * active[:, None, None]
        return region, angle, matrices

    def forward(device, state_tuple):
        proj, row_sums, col_sums = state_tuple
        region, angle, matrices = device_tiles(device)
        pixel_blocks = group_image[region][tile_pix[region, angle]]
        contrib = jnp.einsum("tij,tjs->tis", matrices, pixel_blocks, precision=lax.Precision.HIGHEST)
        proj = proj.at[angle, tile_ray[region, angle]].add(contrib)
        row_sums = row_sums.at[angle, tile_ray[region, angle]].add(jnp.sum(matrices, axis=2))
        col_sums = col_sums.at[region, tile_pix[region, angle]].add(jnp.sum(matrices, axis=1))
        return proj, row_sums, col_sums

    start_state = (jnp.zeros((N_ANG, RB_A, BLK, S), jnp.float32),
                   jnp.zeros((N_ANG, RB_A, BLK), jnp.float32),
                   jnp.zeros((N_PIX, PB, BLK), jnp.float32))
    proj, row_sums, col_sums = lax.fori_loop(0, N_PIX * N_ANG, forward, start_state)
    measured_blocks = measured.reshape(N_ANG, RB_A, BLK, S)
    measured_rays = jnp.take_along_axis(measured_blocks, ray_slot[:, :, None, None], axis=1)
    resid = (measured_rays - proj) / row_sums[..., None]

    def backward(device, back):
        region, angle, matrices = device_tiles(device)
        ray_blocks = resid[angle][tile_ray[region, angle]]
        contrib = jnp.einsum("tij,tis->tjs", matrices, ray_blocks, precision=lax.Precision.HIGHEST)
        return back.at[region, tile_pix[region, angle]].add(contrib)

    back = lax.fori_loop(0, N_PIX * N_ANG, backward, jnp.zeros((N_PIX, PB, BLK, S), jnp.float32))
    new_image = image + relax_factor * (back / col_sums[..., None]).reshape(NPIX, S)
    angles = jnp.arange(N_ANG, dtype=jnp.int32)[:, None]
    slot_resid = jnp.zeros((N_ANG, RB_A, BLK, S), jnp.float32).at[angles, ray_slot].set(resid)
    return new_image, slot_resid.reshape(N_ANG, RAYS_A, S)
```

```python
import functools

import jax
import jax.numpy as jnp
from jax import lax
from jax.experimental import pallas as pl
from jax.experimental.pallas import tpu as pltpu
from jax.sharding import PartitionSpec as P

MESH = pl.DeviceIdType.MESH
BLK, S, SLOTS, RB, QB = 64, 128, 512, 128, 16
RELAX = 0.9
NZ, NY, NA = 8, 4, 8
GRP = 4
NPOS = SLOTS + QB * (GRP - 1)
NPOS_PAD = 640
OWN = 256
CH = OWN + 8
VM = pl.BlockSpec(memory_space=pltpu.VMEM)
SM = pl.BlockSpec(memory_space=pltpu.SMEM)
MIB = 1024 * 1024


def vmem(*shape, dtype=jnp.float32):
    return pltpu.VMEM(shape, dtype)


def gather_kernel(img_ref, out_ref, send_sem, recv_sem):
    me = lax.axis_index("ang")
    pix = lax.axis_index("pix")
    barrier = pltpu.get_barrier_semaphore()
    for d in range(1, NA):
        pl.semaphore_signal(barrier, inc=1, device_id=(pix, lax.rem(me + d, NA)), device_id_type=MESH)
    pl.semaphore_wait(barrier, NA - 1)
    rows = pl.ds(pl.multiple_of(me * 128, 128), 128)
    copies = []
    for d in (4, 3, 5, 2, 6, 1, 7):
        copy = pltpu.make_async_remote_copy(
            src_ref=img_ref,
            dst_ref=out_ref.at[rows],
            send_sem=send_sem.at[d - 1],
            recv_sem=recv_sem.at[d - 1],
            device_id=(pix, lax.rem(me + d, NA)),
            device_id_type=MESH,
        )
        copy.start()
        copies.append(copy)
    out_ref[rows, :] = img_ref[...]
    for copy in copies:
        copy.wait()


def gather_image(image):
    return pl.pallas_call(
        gather_kernel,
        out_shape=jax.ShapeDtypeStruct((NA * 128, S), jnp.float32),
        in_specs=[VM],
        out_specs=VM,
        scratch_shapes=[pltpu.SemaphoreType.DMA((NA - 1,)), pltpu.SemaphoreType.DMA((NA - 1,))],
        compiler_params=pltpu.CompilerParams(collective_id=0, has_side_effects=True),
        name="gather_image",
    )(image)


def tile_rows(tiles_ref, code):
    t = lax.shift_right_logical(code, 7) & (SLOTS - 1)
    start = lax.shift_right_logical(t, 3) * 256 + (t & 7)
    used = lax.shift_right_logical(code, 20).astype(jnp.float32)
    return tiles_ref[pl.ds(start, 32, stride=8), :] * used


def forward_kernel(code_ref, count_ref, tiles_ref, img_ref, p_ref, col_ref, w_ref, rowacc, colacc):
    lane_low = lax.broadcasted_iota(jnp.int32, (32, 128), 1) < BLK

    def weights(q, _):
        x = img_ref[pl.ds(pl.multiple_of(q * BLK, BLK), BLK), :]
        hi = x.astype(jnp.bfloat16)
        lo = (x - hi.astype(jnp.float32)).astype(jnp.bfloat16)
        w_ref[q] = jnp.concatenate([hi, hi, lo, lo], axis=0)
        return _

    lax.fori_loop(0, QB, weights, 0)
    rowacc[...] = jnp.zeros_like(rowacc)
    colacc[...] = jnp.zeros_like(colacc)

    def clear(o, _):
        p_ref[o] = jnp.zeros((CH, S), jnp.float32)
        return _

    lax.fori_loop(0, NZ * NY, clear, 0)

    def group(g, _):
        codes = [code_ref[g * GRP + i] for i in range(GRP)]
        q = lax.shift_right_logical(codes[0], 16) & (QB - 1)
        tiles = [tile_rows(tiles_ref, c) for c in codes]
        parts = []
        for m in tiles:
            hi = m.astype(jnp.bfloat16).astype(jnp.float32)
            lo = m - hi
            parts.append(jnp.where(lane_low, hi, pltpu.roll(lo, BLK, 1)))
            parts.append(jnp.where(lane_low, pltpu.roll(hi, BLK, 1), lo))
        x = jnp.concatenate(parts, axis=0).astype(jnp.bfloat16)
        out = jnp.dot(jnp.concatenate([x, x], axis=1), w_ref[q], preferred_element_type=jnp.float32)
        for i, (c, m) in enumerate(zip(codes, tiles)):
            slot = c & (RB - 1)
            rows = pl.ds(pl.multiple_of((slot & 3) * BLK, BLK), BLK)
            owner = lax.shift_right_logical(slot, 2)
            p_ref[owner, rows, :] += out[BLK * i : BLK * (i + 1)]
            rowacc[slot] += m
        colacc[q] += (tiles[0] + tiles[1]) + (tiles[2] + tiles[3])
        return _

    lax.fori_loop(0, count_ref[0], group, 0)

    pick = lax.broadcasted_iota(jnp.int32, (8, 128), 0) == (lax.broadcasted_iota(jnp.int32, (8, 128), 1) // BLK)
    pick = pick.astype(jnp.float32).astype(jnp.bfloat16)

    def row_sums(o, _):
        x = rowacc[pl.ds(o * 4, 4)].reshape(128, 128)
        hi = x.astype(jnp.bfloat16)
        lo = (x - hi.astype(jnp.float32)).astype(jnp.bfloat16)
        dims = (((1,), (1,)), ((), ()))
        sums = lax.dot_general(pick, hi, dims, preferred_element_type=jnp.float32)
        sums += lax.dot_general(pick, lo, dims, preferred_element_type=jnp.float32)
        p_ref[o, OWN:CH, :] = sums
        return _

    lax.fori_loop(0, NZ * NY, row_sums, 0)
    low = lax.broadcasted_iota(jnp.int32, (1, 128), 1) < BLK
    for o in range(NA):
        a = jnp.sum(colacc[2 * o], axis=0, keepdims=True)
        b = jnp.sum(colacc[2 * o + 1], axis=0, keepdims=True)
        a = a + pltpu.roll(a, BLK, 1)
        b = b + pltpu.roll(b, BLK, 1)
        col_ref[o] = jnp.broadcast_to(jnp.where(low, a, b), (8, 128))


def forward(code, count, tiles, img):
    return pl.pallas_call(
        forward_kernel,
        out_shape=(
            jax.ShapeDtypeStruct((NZ * NY, CH, S), jnp.float32),
            jax.ShapeDtypeStruct((NA, 8, 128), jnp.float32),
        ),
        in_specs=[SM, SM, VM, VM],
        out_specs=(VM, VM),
        scratch_shapes=[
            vmem(QB, 4 * BLK, S, dtype=jnp.bfloat16),
            vmem(RB, 32, 128),
            vmem(QB, 32, 128),
        ],
        compiler_params=pltpu.CompilerParams(vmem_limit_bytes=40 * MIB),
        name="forward_tiles",
    )(code, count, tiles, img)


def ring_steps(n, sign):
    return ((sign, n // 2), (-sign, n // 2 - 1))


class Task:
    def __init__(self, key, link, rows, needs):
        self.key, self.link, self.rows, self.needs = key, link, rows, needs


def schedule(tasks, latency, rate):
    by_key = {t.key: t for t in tasks}
    follow = {t.key: [] for t in tasks}
    for t in tasks:
        for k in t.needs:
            follow[k].append(t.key)
    tail = {}

    def tail_of(k):
        if k not in tail:
            t = by_key[k]
            tail[k] = t.rows / rate + latency + max([tail_of(f) for f in follow[k]], default=0.0)
        return tail[k]

    left, done, free, order = list(tasks), {}, {}, []
    while left:
        best = None
        for t in left:
            if all(k in done for k in t.needs):
                at = max([done[k] for k in t.needs], default=0.0)
                start = max(at, free.get(t.link, 0.0))
                rank = (start, -tail_of(t.key))
                if best is None or rank < best[0]:
                    best = (rank, t)
        (start, _), t = best
        free[t.link] = start + t.rows / rate
        done[t.key] = start + t.rows / rate + latency
        order.append((start, t.key))
        left.remove(t)
    return [k for _, k in sorted(order, key=lambda e: e[0])]


RATE = 95.0
LATENCY = 1.5

SUM_A = (0, 104)
SUM_B = (104, 264)
ALL_A = (0, 104)
ALL_B = (104, 256)


def halves(span):
    lo, hi = span
    mid = lo + ((hi - lo) // 2 + 7) // 8 * 8
    return ((lo, mid), (mid, hi))


def sign_of(i):
    return 1 if i % 2 == 0 else -1


def sum_tasks():
    tasks = []

    def ring(stage, n, axis, piece, sign, rows, local_needs):
        for chain, (d, steps) in enumerate(ring_steps(n, sign)):
            for s in range(1, steps + 1):
                off = (d * (steps - s + 1)) % n
                needs = [(stage, piece, chain, s - 1)] if s > 1 else []
                tasks.append(Task((stage, piece, chain, s), (axis, d), rows, needs + local_needs(off)))

    def last(stage, n, piece):
        return [(stage, piece, 0, n // 2), (stage, piece, 1, n // 2 - 1)]

    for yo in range(NY):
        ring("a1", NZ, "z", yo, sign_of(yo), SUM_A[1] - SUM_A[0], lambda off: [])
    for h, (lo, hi) in enumerate(halves(SUM_A)):
        ring("a2", NY, "y", h, sign_of(h), hi - lo, lambda off: last("a1", NZ, off))
    for zo in range(NZ):
        ring("b1", NY, "y", zo, sign_of(zo), SUM_B[1] - SUM_B[0], lambda off: [])
    for h, (lo, hi) in enumerate(halves(SUM_B)):
        ring("b2", NZ, "z", h, sign_of(h), hi - lo, lambda off: last("b1", NY, off))
    return tasks


def all_tasks():
    tasks = []

    def ring(stage, n, axis, piece, sign, rows, first_needs):
        for chain, (d, steps) in enumerate(ring_steps(n, sign)):
            for s in range(1, steps + 1):
                needs = [(stage, piece, chain, s - 1)] if s > 1 else first_needs
                tasks.append(Task((stage, piece, chain, s), (axis, d), rows, needs))

    def arrives(stage, n, piece, sign, off):
        for chain, (d, steps) in enumerate(ring_steps(n, sign)):
            for s in range(1, steps + 1):
                if (-d * s) % n == off:
                    return (stage, piece, chain, s)

    for h, (lo, hi) in enumerate(halves(ALL_A)):
        ring("c1", NY, "y", h, sign_of(h), hi - lo, [])
    for yo in range(NY):
        needs = [arrives("c1", NY, h, sign_of(h), yo) for h in range(2)] if yo else []
        ring("c2", NZ, "z", yo, sign_of(yo), ALL_A[1] - ALL_A[0], needs)
    for h, (lo, hi) in enumerate(halves(ALL_B)):
        ring("d1", NZ, "z", h, sign_of(h), hi - lo, [])
    for zo in range(NZ):
        needs = [arrives("d1", NZ, h, sign_of(h), zo) for h in range(2)] if zo else []
        ring("d2", NY, "y", zo, sign_of(zo), ALL_B[1] - ALL_B[0], needs)
    return tasks


AHEAD = 3


def exchange_kernel(p_ref, meas_ref, resid_ref, all_ref, ra1, ra2, rb1, rb2, own, send_sem, recv_sem):
    pix, ang = lax.axis_index("pix"), lax.axis_index("ang")
    z, y = pix // NY, lax.rem(pix, NY)

    def at(zo, yo):
        return lax.rem(z + zo % NZ, NZ) * NY + lax.rem(y + yo % NY, NY)

    def device(link):
        axis, d = link
        return (at(d, 0) if axis == "z" else at(0, d), ang)

    barrier = pltpu.get_barrier_semaphore()
    for link in (("z", 1), ("z", -1), ("y", 1), ("y", -1)):
        pl.semaphore_signal(barrier, inc=1, device_id=device(link), device_id_type=MESH)
    pl.semaphore_wait(barrier, 4)

    tasks = sum_tasks() + all_tasks()
    number = {t.key: i for i, t in enumerate(tasks)}
    by_key = {t.key: t for t in tasks}
    sums = schedule(sum_tasks(), LATENCY, RATE)
    alls = schedule(all_tasks(), LATENCY, RATE)

    a_rows, b_rows = pl.ds(SUM_A[0], SUM_A[1] - SUM_A[0]), pl.ds(SUM_B[0], SUM_B[1] - SUM_B[0])
    slot_of = {}
    for stage, ref in (("a1", ra1), ("a2", ra2), ("b1", rb1), ("b2", rb2)):
        keys = [t.key for t in tasks if t.key[0] == stage]
        for i, k in enumerate(keys):
            slot_of[k] = ref.at[i, pl.ds(0, by_key[k].rows)]

    def chain_of(n, piece, chain):
        return ring_steps(n, sign_of(piece))[chain]

    def origin(key):
        stage, piece, chain, s = key
        if stage in ("c1", "d1"):
            n = NY if stage == "c1" else NZ
            d, _ = chain_of(n, piece, chain)
            off = -d * (s - 1)
            lo, hi = halves(ALL_A if stage == "c1" else ALL_B)[piece]
            return (at(0, off) if stage == "c1" else at(off, 0)), pl.ds(lo, hi - lo)
        n = NZ if stage == "c2" else NY
        d, _ = chain_of(n, piece, chain)
        off = -d * (s - 1)
        lo, hi = ALL_A if stage == "c2" else ALL_B
        return (at(off, piece) if stage == "c2" else at(piece, off)), pl.ds(lo, hi - lo)

    def source(key):
        stage, piece, chain, s = key
        if stage in ("c1", "c2", "d1", "d2"):
            owner, rows = origin(key)
            ref = all_ref.at[owner, rows]
            return ref, ref
        dst = slot_of[key]
        if s > 1:
            return slot_of[(stage, piece, chain, s - 1)], dst
        return local(key), dst

    def local(key):
        stage, piece, chain, s = key
        if stage in ("a1", "b1"):
            n = NZ if stage == "a1" else NY
            d, steps = chain_of(n, piece, chain)
            off = d * (steps - s + 1)
            return p_ref.at[at(off, piece), a_rows] if stage == "a1" else p_ref.at[at(piece, off), b_rows]
        n = NY if stage == "a2" else NZ
        d, steps = chain_of(n, piece, chain)
        off = (d * (steps - s + 1)) % n
        span = SUM_A if stage == "a2" else SUM_B
        lo, hi = halves(span)[piece]
        first = ("a1" if stage == "a2" else "b1", off, 0, n_first(stage) // 2)
        return slot_of[first].at[pl.ds(lo - span[0], hi - lo)]

    def n_first(stage):
        return NZ if stage == "a2" else NY

    copies = {}

    def copy_of(key):
        if key not in copies:
            src, dst = source(key)
            i = number[key]
            copies[key] = pltpu.make_async_remote_copy(
                src_ref=src,
                dst_ref=dst,
                send_sem=send_sem.at[i],
                recv_sem=recv_sem.at[i],
                device_id=device(by_key[key].link),
                device_id_type=MESH,
            )
        return copies[key]

    received, sent, waited, finished = set(), {}, set(), set()

    def receive(key):
        if key not in received:
            received.add(key)
            copy_of(key).wait_recv()

    def finish(stage, off):
        if (stage, off) in finished:
            return
        finished.add((stage, off))
        n = NZ if stage == "a1" else NY
        one, two = (stage, off, 0, n // 2), (stage, off, 1, n // 2 - 1)
        receive(one)
        receive(two)
        mine = p_ref.at[at(0, off), a_rows] if stage == "a1" else p_ref.at[at(off, 0), b_rows]
        slot_of[one][...] = slot_of[one][...] + slot_of[two][...] + mine[...]

    def issue(key):
        stage, piece, chain, s = key
        task = by_key[key]
        queue = sent.setdefault(task.link, [])
        if len(queue) >= AHEAD:
            old = queue[-AHEAD]
            if old not in waited:
                waited.add(old)
                copy_of(old).wait_send()
        for k in task.needs:
            if stage in ("a2", "b2") and k[0] in ("a1", "b1"):
                finish(k[0], k[1])
            else:
                receive(k)
        if s > 1 and stage in ("a1", "a2", "b1", "b2"):
            ref = slot_of[(stage, piece, chain, s - 1)]
            ref[...] = ref[...] + local(key)[...]
        copy_of(key).start()
        queue.append(key)

    for key in sums:
        issue(key)
    for stage, span, n, n1 in (("a2", SUM_A, NY, NZ), ("b2", SUM_B, NZ, NY)):
        first = "a1" if stage == "a2" else "b1"
        finish(first, 0)
        for h, (lo, hi) in enumerate(halves(span)):
            one, two = (stage, h, 0, n // 2), (stage, h, 1, n // 2 - 1)
            receive(one)
            receive(two)
            mine = slot_of[(first, 0, 0, n1 // 2)].at[pl.ds(lo - span[0], hi - lo)]
            own[lo:hi, :] = slot_of[one][...] + slot_of[two][...] + mine[...]

    norms = [jnp.broadcast_to(own[OWN + h : OWN + h + 1, :], (128, 128)).T for h in range(2)]
    for b in range(4):
        for h in range(2):
            natural = pl.ds(b * BLK + h, 32, stride=2)
            mine = slice(b * BLK + 32 * h, b * BLK + 32 * h + 32)
            value = (meas_ref[natural, :] - own[mine, :]) / norms[h][32 * b : 32 * b + 32]
            resid_ref[natural, :] = value
            all_ref[at(0, 0), mine, :] = value

    for key in alls:
        issue(key)
    for t in tasks:
        receive(t.key)
    for t in tasks:
        if t.key not in waited:
            copy_of(t.key).wait_send()


def exchange(p, measured):
    tasks = sum_tasks() + all_tasks()
    count = {}
    for t in tasks:
        count[t.key[0]] = count.get(t.key[0], 0) + 1
    most = {k: max(t.rows for t in tasks if t.key[0] == k) for k in count}
    return pl.pallas_call(
        exchange_kernel,
        out_shape=(
            jax.ShapeDtypeStruct((OWN, S), jnp.float32),
            jax.ShapeDtypeStruct((NZ * NY, OWN, S), jnp.float32),
        ),
        in_specs=[VM, VM],
        out_specs=(VM, VM),
        scratch_shapes=[vmem(count[k], most[k], S) for k in ("a1", "a2", "b1", "b2")]
        + [
            vmem(CH, S),
            pltpu.SemaphoreType.DMA((len(tasks),)),
            pltpu.SemaphoreType.DMA((len(tasks),)),
        ],
        compiler_params=pltpu.CompilerParams(
            collective_id=1, has_side_effects=True, vmem_limit_bytes=32 * MIB
        ),
        name="sum_and_spread",
    )(p, measured)


def backward_kernel(code_ref, count_ref, tiles_ref, all_ref, col_ref, b_ref, hi_ref, lo_ref):
    def split(o, _):
        x = all_ref[o]
        hi = x.astype(jnp.bfloat16)
        rows = pl.ds(pl.multiple_of(o * OWN, OWN), OWN)
        hi_ref[rows, :] = hi
        lo_ref[rows, :] = (x - hi.astype(jnp.float32)).astype(jnp.bfloat16)
        return _

    lax.fori_loop(0, NZ * NY, split, 0)
    for o in range(NA):
        b_ref[o, 0:128, :] = jnp.zeros((128, S), jnp.float32)
        b_ref[o, 128:136, :] = col_ref[o]

    def group(g, _):
        codes = [code_ref[g * GRP + i] for i in range(GRP)]
        q = lax.shift_right_logical(codes[0], 16) & (QB - 1)
        x = jnp.concatenate([tile_rows(tiles_ref, c) for c in codes], axis=0).T
        hi = x.astype(jnp.bfloat16)
        lo = (x - hi.astype(jnp.float32)).astype(jnp.bfloat16)
        starts = [(c & (RB - 1)) * BLK for c in codes]

        def rays(ref):
            return [
                ref[pl.ds(pl.multiple_of(start + 32 * h, 32), 32), :] for h in range(2) for start in starts
            ]

        r_hi, r_lo = rays(hi_ref), rays(lo_ref)
        left = jnp.concatenate([hi[:BLK], hi[BLK:], lo[:BLK], lo[BLK:], hi[:BLK], hi[BLK:]], axis=1)
        right = jnp.concatenate(r_hi + r_hi + r_lo, axis=0)
        out = jnp.dot(left, right, preferred_element_type=jnp.float32)
        rows = pl.ds(pl.multiple_of((q & 1) * BLK, BLK), BLK)
        b_ref[lax.shift_right_logical(q, 1), rows, :] += out
        return _

    lax.fori_loop(0, count_ref[0], group, 0)


def backward(code, count, tiles, everyone, col):
    return pl.pallas_call(
        backward_kernel,
        out_shape=jax.ShapeDtypeStruct((NA, 136, S), jnp.float32),
        in_specs=[SM, SM, VM, VM, VM],
        out_specs=VM,
        scratch_shapes=[
            vmem(RB * BLK, S, dtype=jnp.bfloat16),
            vmem(RB * BLK, S, dtype=jnp.bfloat16),
        ],
        compiler_params=pltpu.CompilerParams(vmem_limit_bytes=40 * MIB),
        name="backward_tiles",
    )(code, count, tiles, everyone, col)


def update_kernel(b_ref, img_ref, out_ref, got, send_sem, recv_sem):
    me = lax.axis_index("ang")
    pix = lax.axis_index("pix")
    barrier = pltpu.get_barrier_semaphore()
    for d in range(1, NA):
        pl.semaphore_signal(barrier, inc=1, device_id=(pix, lax.rem(me + d, NA)), device_id_type=MESH)
    pl.semaphore_wait(barrier, NA - 1)
    copies = []
    for d in (4, 3, 5, 2, 6, 1, 7):
        to = lax.rem(me + d, NA)
        copy = pltpu.make_async_remote_copy(
            src_ref=b_ref.at[to],
            dst_ref=got.at[d - 1],
            send_sem=send_sem.at[d - 1],
            recv_sem=recv_sem.at[d - 1],
            device_id=(pix, to),
            device_id_type=MESH,
        )
        copy.start()
        copies.append(copy)
    for copy in copies:
        copy.wait()
    total = b_ref[me]
    for d in range(NA - 1):
        total = total + got[d]
    norm = jnp.broadcast_to(total[128:129], (128, 128)).T
    out_ref[...] = img_ref[...] + RELAX * (total[:128] / norm)


def update(b, image):
    return pl.pallas_call(
        update_kernel,
        out_shape=jax.ShapeDtypeStruct((128, S), jnp.float32),
        in_specs=[VM, VM],
        out_specs=VM,
        scratch_shapes=[
            vmem(NA - 1, 136, S),
            pltpu.SemaphoreType.DMA((NA - 1,)),
            pltpu.SemaphoreType.DMA((NA - 1,)),
        ],
        compiler_params=pltpu.CompilerParams(collective_id=2, has_side_effects=True),
        name="sum_and_update",
    )(b, image)


def sort_tiles(tile_ray, tile_pix, tile_count, slot_table):
    t = jnp.arange(SLOTS, dtype=jnp.int32)
    used = t < tile_count
    slot = jnp.sum(
        jnp.where(tile_ray[:, None] == jnp.arange(RB, dtype=jnp.int32)[None, :], slot_table[None, :], 0), axis=1
    )
    q = jnp.where(used, tile_pix, QB)
    before = jnp.sum(((q[None, :] == q[:, None]) & (t[None, :] < t[:, None])).astype(jnp.int32), axis=1)
    blocks = jnp.arange(QB, dtype=jnp.int32)
    counts = jnp.sum((q[None, :] == blocks[:, None]).astype(jnp.int32), axis=1)
    whole = (counts + GRP - 1) // GRP * GRP
    first = jnp.sum(jnp.where(blocks[None, :] < q[:, None], whole[None, :], 0), axis=1)
    place = jnp.where(used, first + before, -1)
    code = (1 << 20) | (q << 16) | (t << 7) | slot
    places = jnp.arange(NPOS_PAD, dtype=jnp.int32)
    listed = jnp.sum(jnp.where(place[None, :] == places[:, None], code[None, :], 0), axis=1)
    return listed, jnp.sum(whole, keepdims=True) // GRP


def shards(tiles, tile_ray, tile_pix, tile_count, ray_slot, image, measured):
    code, count = sort_tiles(tile_ray[0, 0], tile_pix[0, 0], tile_count[0, 0], ray_slot[0])
    rows = tiles[0, 0].reshape(SLOTS // 8, 8, 32, 128).transpose(0, 2, 1, 3).reshape(SLOTS * 32, 128)
    img = gather_image(image)
    p, col = forward(code, count, rows, img)
    resid, everyone = exchange(p, measured[0])
    b = backward(code, count, rows, everyone, col)
    new_image = update(b, image)
    return (new_image, resid[None])


def solution(mesh):
    in_specs = (
        P("pix", "ang", None, None),
        P("pix", "ang", None),
        P("pix", "ang", None),
        P("pix", "ang"),
        P("ang", None),
        P(("pix", "ang"), None),
        P("ang", "pix", None),
    )
    out_specs = (P(("pix", "ang"), None), P("ang", "pix", None))
    return jax.shard_map(shards, mesh=mesh, in_specs=in_specs, out_specs=out_specs, check_vma=False)
```

```python
import functools

import jax
import jax.numpy as jnp
from jax import lax
from jax.experimental import pallas as pl
from jax.experimental.pallas import tpu as pltpu
from jax.sharding import PartitionSpec as P

MESH = pl.DeviceIdType.MESH
BLK, S, SLOTS, RB, QB = 64, 128, 512, 128, 16
RELAX = 0.9
NZ, NY, NX, NA = 8, 4, 4, 8
GRP = 4
NPOS = SLOTS + QB * (GRP - 1)
NPOS_PAD = 640
OWN = 256
CH = OWN + 8
VM = pl.BlockSpec(memory_space=pltpu.VMEM)
SM = pl.BlockSpec(memory_space=pltpu.SMEM)
MIB = 1024 * 1024


def cost(us):
    return pl.CostEstimate(flops=int(us * 1.15e9), bytes_accessed=0, transcendentals=0)


def vmem(*shape, dtype=jnp.float32):
    return pltpu.VMEM(shape, dtype)


def split_bf16(x):
    hi = x.astype(jnp.bfloat16)
    return hi, (x - hi.astype(jnp.float32)).astype(jnp.bfloat16)


def sign_of(i):
    return 1 if i % 2 == 0 else -1


class Ang:
    def __init__(self):
        self.pix, me = lax.axis_index("pix"), lax.axis_index("ang")
        self.me, self.x, self.core = me, me // 2, lax.rem(me, 2)

    def index(self, dx):
        return lax.rem(self.x + dx % NX, NX) * 2 + self.core

    def twin(self, dx=0):
        return lax.rem(self.x + dx % NX, NX) * 2 + (1 - self.core)

    def device(self, to):
        return (self.pix, self.twin() if to == "twin" else self.index(to))

    def meet(self):
        barrier = pltpu.get_barrier_semaphore()
        for to in ("twin", 1, -1):
            pl.semaphore_signal(barrier, inc=1, device_id=self.device(to), device_id_type=MESH)
        pl.semaphore_wait(barrier, 3)


def sort_tiles(ray, pix, used_tiles, table):
    f32 = jnp.float32
    both = jnp.broadcast_to((pix * RB + ray).astype(f32), (128, SLOTS)).T.astype(jnp.int32)
    lane = lax.broadcasted_iota(jnp.int32, (SLOTS, 128), 1)
    t = lax.broadcasted_iota(jnp.int32, (SLOTS, 128), 0)
    q = lax.shift_right_logical(both, 7)
    mine = jnp.where((q == lane) & (t < used_tiles), 1.0, 0.0).astype(f32)
    slot = jnp.sum(jnp.where((both & (RB - 1)) == lane, table.astype(f32), 0.0), axis=1, keepdims=True)
    earlier = lax.broadcasted_iota(jnp.int32, (SLOTS, SLOTS), 1) < lax.broadcasted_iota(jnp.int32, (SLOTS, SLOTS), 0)
    earlier = jnp.where(earlier, 1.0, 0.0).astype(jnp.bfloat16)
    before = jnp.dot(earlier, mine.astype(jnp.bfloat16), preferred_element_type=f32)
    counts = jnp.sum(mine, axis=0, keepdims=True).astype(jnp.int32)
    groups = lax.shift_right_logical(counts + (GRP - 1), 2).astype(f32)
    left_of = lax.broadcasted_iota(jnp.int32, (128, 128), 0) < lax.broadcasted_iota(jnp.int32, (128, 128), 1)
    left_of = jnp.where(left_of, 1.0, 0.0).astype(jnp.bfloat16)
    first = jnp.dot(jnp.broadcast_to(groups, (8, 128)).astype(jnp.bfloat16), left_of, preferred_element_type=f32)
    place = jnp.sum(mine * (before + GRP * first[:1]), axis=1, keepdims=True)
    place = jnp.where(t < used_tiles, place, -1.0)
    code = ((1 << 20) + q * (1 << 16) + t * RB).astype(f32) + slot
    parts = []
    for c in range(NPOS_PAD // 128):
        at = (lax.broadcasted_iota(jnp.int32, (1, 128), 1) + c * 128).astype(f32)
        part = jnp.sum(jnp.where(place == at, code, 0.0), axis=0, keepdims=True)
        parts.append(jnp.where(at == NPOS_PAD - 1, jnp.sum(groups, axis=1, keepdims=True), part))
    return jnp.concatenate(parts, axis=1).astype(jnp.int32)


def gather_kernel(
    count_ref, ray_ref, pix_ref, table_ref, img_ref, out_ref, code_ref, send_sem, recv_sem
):
    here = Ang()
    here.meet()
    number = iter(range(13))

    def send(to, dx, half, src=None):
        lo, size = (0, 128) if half is None else (64 * half, 64)
        rows = out_ref.at[pl.ds(pl.multiple_of(here.index(dx) * 128 + lo, 64), size)]
        i = next(number)
        copy = pltpu.make_async_remote_copy(
            src_ref=rows if src is None else src.at[pl.ds(lo, size)],
            dst_ref=rows,
            send_sem=send_sem.at[i],
            recv_sem=recv_sem.at[i],
            device_id=here.device(to),
            device_id_type=MESH,
        )
        copy.start()
        return copy

    far = [send(sign_of(h), 0, h, img_ref) for h in range(2)]
    near = [send(-sign_of(h), 0, h, img_ref) for h in range(2)]
    across = [send("twin", 0, None, img_ref)]
    out_ref[pl.ds(pl.multiple_of(here.me * 128, 128), 128), :] = img_ref[...]
    code_ref[...] = sort_tiles(ray_ref[...], pix_ref[...], count_ref[0, 0], table_ref[...])
    second = []
    for h in range(2):
        far[h].wait_recv()
        second.append(send(sign_of(h), -sign_of(h), h))
    for h in range(2):
        across.append(send("twin", -sign_of(h), h))
    for h in range(2):
        near[h].wait_recv()
        across.append(send("twin", sign_of(h), h))
    for h in range(2):
        second[h].wait_recv()
        across.append(send("twin", 2, h))
    for copy in across:
        copy.wait_recv()
    for copy in far + near + second + across:
        copy.wait_send()


def gather_image(count, ray, pix, table, image):
    return pl.pallas_call(
        gather_kernel,
        out_shape=(
            jax.ShapeDtypeStruct((NA * 128, S), jnp.float32),
            jax.ShapeDtypeStruct((1, NPOS_PAD), jnp.int32),
        ),
        in_specs=[SM, VM, VM, VM, VM],
        out_specs=(VM, VM),
        scratch_shapes=[
            pltpu.SemaphoreType.DMA((13,)),
            pltpu.SemaphoreType.DMA((13,)),
        ],
        compiler_params=pltpu.CompilerParams(
            collective_id=0, has_side_effects=True, vmem_limit_bytes=24 * MIB
        ),
        cost_estimate=cost(8),
        name="gather_image",
    )(count, ray, pix, table, image)


def tile_rows(tiles_ref, code):
    t = lax.shift_right_logical(code, 7) & (SLOTS - 1)
    start = lax.shift_right_logical(t, 3) * 256 + (t & 7)
    used = lax.shift_right_logical(code, 20).astype(jnp.float32)
    return tiles_ref[pl.ds(start, 32, stride=8), :] * used


FWD = 12


def forward_kernel(code_ref, tiles_ref, img_ref, p_ref, col_ref, w_ref, rowacc, colacc):
    zero = jnp.zeros((BLK, S), jnp.bfloat16)

    def weights(q, _):
        hi, lo = split_bf16(img_ref[pl.ds(pl.multiple_of(q * BLK, BLK), BLK), :])
        both = [jnp.concatenate([jnp.concatenate([x, zero], 1), jnp.concatenate([zero, x], 1)], 0) for x in (hi, lo)]
        w_ref[q] = jnp.concatenate([both[0], both[0], both[1]], axis=0)
        return _

    lax.fori_loop(0, QB, weights, 0, unroll=4)
    rowacc[...] = jnp.zeros_like(rowacc)
    colacc[...] = jnp.zeros_like(colacc)

    def clear(o, _):
        p_ref[o] = jnp.zeros((CH, S), jnp.float32)
        return _

    lax.fori_loop(0, NZ * NY, clear, 0, unroll=4)

    def place(slot):
        rows = pl.ds(pl.multiple_of((slot & 3) * BLK, BLK), BLK)
        return lax.shift_right_logical(slot, 2), rows, slice(None)

    def read(slot):
        return p_ref[place(slot)]

    def write(slot, value):
        p_ref[place(slot)] = value

    def read_rows(slot):
        return rowacc[slot]

    def write_rows(slot, value):
        rowacc[slot] = value

    def step(b, _):
        for i in range(FWD):
            codes = [code_ref[0, (b * FWD + i) * GRP + j] for j in range(GRP)]
            q = lax.shift_right_logical(codes[0], 16) & (QB - 1)
            slots = [c & (RB - 1) for c in codes]
            tiles = [tile_rows(tiles_ref, c) for c in codes]
            hi, lo = split_bf16(jnp.concatenate(tiles, axis=0))
            out = jnp.dot(jnp.concatenate([hi, lo, hi], axis=1), w_ref[q], preferred_element_type=jnp.float32)
            terms = [
                jnp.concatenate([out[32 * j : 32 * j + 32, h * S : h * S + S] for h in range(2)], axis=0)
                for j in range(GRP)
            ]
            for k, v in zip(slots, tiles):
                rowacc[k] += v
            colacc[q] += (tiles[0] + tiles[1]) + (tiles[2] + tiles[3])
            for k, v in zip(slots, terms):
                write(k, read(k) + v)
        return _

    lax.fori_loop(0, (code_ref[0, NPOS_PAD - 1] + FWD - 1) // FWD, step, 0)

    pick = lax.broadcasted_iota(jnp.int32, (8, 128), 0) == (lax.broadcasted_iota(jnp.int32, (8, 128), 1) // BLK)
    pick = pick.astype(jnp.float32).astype(jnp.bfloat16)

    def row_sums(o, _):
        hi, lo = split_bf16(rowacc[pl.ds(o * 4, 4)].reshape(128, 128))
        dims = (((1,), (1,)), ((), ()))
        sums = lax.dot_general(pick, hi, dims, preferred_element_type=jnp.float32)
        sums += lax.dot_general(pick, lo, dims, preferred_element_type=jnp.float32)
        p_ref[o, OWN:CH, :] = sums
        return _

    lax.fori_loop(0, NZ * NY, row_sums, 0, unroll=16)
    low = lax.broadcasted_iota(jnp.int32, (1, 128), 1) < BLK
    for o in range(NA):
        a = jnp.sum(colacc[2 * o], axis=0, keepdims=True)
        b = jnp.sum(colacc[2 * o + 1], axis=0, keepdims=True)
        a = a + pltpu.roll(a, BLK, 1)
        b = b + pltpu.roll(b, BLK, 1)
        col_ref[o] = jnp.broadcast_to(jnp.where(low, a, b), (8, 128))


def forward(code, tiles, img):
    return pl.pallas_call(
        forward_kernel,
        out_shape=(
            jax.ShapeDtypeStruct((NZ * NY, CH, S), jnp.float32),
            jax.ShapeDtypeStruct((NA, 8, 128), jnp.float32),
        ),
        in_specs=[SM, VM, VM],
        out_specs=(VM, VM),
        scratch_shapes=[
            vmem(QB, 6 * BLK, 2 * S, dtype=jnp.bfloat16),
            vmem(RB, 32, 128),
            vmem(QB, 32, 128),
        ],
        compiler_params=pltpu.CompilerParams(vmem_limit_bytes=32 * MIB),
        cost_estimate=cost(13),
        name="forward_tiles",
    )(code, tiles, img)


def ring_steps(n, sign):
    return ((sign, n // 2), (-sign, n // 2 - 1))


class Task:
    def __init__(self, key, link, rows, needs):
        self.key, self.link, self.rows, self.needs = key, link, rows, needs


def schedule(tasks, latency, rate):
    by_key = {t.key: t for t in tasks}
    follow = {t.key: [] for t in tasks}
    for t in tasks:
        for k in t.needs:
            follow[k].append(t.key)
    tail = {}

    def tail_of(k):
        if k not in tail:
            t = by_key[k]
            tail[k] = t.rows / rate + latency + max([tail_of(f) for f in follow[k]], default=0.0)
        return tail[k]

    left, done, free, order = list(tasks), {}, {}, []
    while left:
        best = None
        for t in left:
            if all(k in done for k in t.needs):
                at = max([done[k] for k in t.needs], default=0.0)
                start = max(at, free.get(t.link, 0.0))
                rank = (start, -tail_of(t.key))
                if best is None or rank < best[0]:
                    best = (rank, t)
        (start, _), t = best
        free[t.link] = start + t.rows / rate
        done[t.key] = start + t.rows / rate + latency
        order.append((start, t.key))
        left.remove(t)
    return [k for _, k in sorted(order, key=lambda e: e[0])]


RATE = 95.0
LATENCY = 1.5

SUM_A = (0, 104)
SUM_B = (104, 264)
ALL_A = (0, 104)
ALL_B = (104, 256)


def halves(span):
    lo, hi = span
    mid = lo + ((hi - lo) // 2 + 7) // 8 * 8
    return ((lo, mid), (mid, hi))


def sum_tasks():
    tasks = []

    def ring(stage, n, axis, piece, sign, rows, local_needs):
        for chain, (d, steps) in enumerate(ring_steps(n, sign)):
            for s in range(1, steps + 1):
                off = (d * (steps - s + 1)) % n
                needs = [(stage, piece, chain, s - 1)] if s > 1 else []
                tasks.append(Task((stage, piece, chain, s), (axis, d), rows, needs + local_needs(off)))

    def last(stage, n, piece):
        return [(stage, piece, 0, n // 2), (stage, piece, 1, n // 2 - 1)]

    for yo in range(NY):
        ring("a1", NZ, "z", yo, sign_of(yo), SUM_A[1] - SUM_A[0], lambda off: [])
    for h, (lo, hi) in enumerate(halves(SUM_A)):
        ring("a2", NY, "y", h, sign_of(h), hi - lo, lambda off: last("a1", NZ, off))
    for zo in range(NZ):
        ring("b1", NY, "y", zo, sign_of(zo), SUM_B[1] - SUM_B[0], lambda off: [])
    for h, (lo, hi) in enumerate(halves(SUM_B)):
        ring("b2", NZ, "z", h, sign_of(h), hi - lo, lambda off: last("b1", NY, off))
    return tasks


def all_tasks():
    tasks = []

    def ring(stage, n, axis, piece, sign, rows, first_needs):
        for chain, (d, steps) in enumerate(ring_steps(n, sign)):
            for s in range(1, steps + 1):
                needs = [(stage, piece, chain, s - 1)] if s > 1 else first_needs
                tasks.append(Task((stage, piece, chain, s), (axis, d), rows, needs))

    def arrives(stage, n, piece, sign, off):
        for chain, (d, steps) in enumerate(ring_steps(n, sign)):
            for s in range(1, steps + 1):
                if (-d * s) % n == off:
                    return (stage, piece, chain, s)

    for h, (lo, hi) in enumerate(halves(ALL_A)):
        ring("c1", NY, "y", h, sign_of(h), hi - lo, [])
    for yo in range(NY):
        needs = [arrives("c1", NY, h, sign_of(h), yo) for h in range(2)] if yo else []
        ring("c2", NZ, "z", yo, sign_of(yo), ALL_A[1] - ALL_A[0], needs)
    for h, (lo, hi) in enumerate(halves(ALL_B)):
        ring("d1", NZ, "z", h, sign_of(h), hi - lo, [])
    for zo in range(NZ):
        needs = [arrives("d1", NZ, h, sign_of(h), zo) for h in range(2)] if zo else []
        ring("d2", NY, "y", zo, sign_of(zo), ALL_B[1] - ALL_B[0], needs)
    return tasks


AHEAD = 3


def exchange_kernel(p_ref, meas_ref, resid_ref, all_ref, ra1, ra2, rb1, rb2, own, send_sem, recv_sem):
    pix, ang = lax.axis_index("pix"), lax.axis_index("ang")
    z, y = pix // NY, lax.rem(pix, NY)

    def at(zo, yo):
        return lax.rem(z + zo % NZ, NZ) * NY + lax.rem(y + yo % NY, NY)

    def device(link):
        axis, d = link
        return (at(d, 0) if axis == "z" else at(0, d), ang)

    barrier = pltpu.get_barrier_semaphore()
    for link in (("z", 1), ("z", -1), ("y", 1), ("y", -1)):
        pl.semaphore_signal(barrier, inc=1, device_id=device(link), device_id_type=MESH)
    pl.semaphore_wait(barrier, 4)

    tasks = sum_tasks() + all_tasks()
    number = {t.key: i for i, t in enumerate(tasks)}
    by_key = {t.key: t for t in tasks}
    sums = schedule(sum_tasks(), LATENCY, RATE)
    alls = schedule(all_tasks(), LATENCY, RATE)

    a_rows, b_rows = pl.ds(SUM_A[0], SUM_A[1] - SUM_A[0]), pl.ds(SUM_B[0], SUM_B[1] - SUM_B[0])
    slot_of = {}
    for stage, ref in (("a1", ra1), ("a2", ra2), ("b1", rb1), ("b2", rb2)):
        keys = [t.key for t in tasks if t.key[0] == stage]
        for i, k in enumerate(keys):
            slot_of[k] = ref.at[i, pl.ds(0, by_key[k].rows)]

    def chain_of(n, piece, chain):
        return ring_steps(n, sign_of(piece))[chain]

    def origin(key):
        stage, piece, chain, s = key
        if stage in ("c1", "d1"):
            n = NY if stage == "c1" else NZ
            d, _ = chain_of(n, piece, chain)
            off = -d * (s - 1)
            lo, hi = halves(ALL_A if stage == "c1" else ALL_B)[piece]
            return (at(0, off) if stage == "c1" else at(off, 0)), pl.ds(lo, hi - lo)
        n = NZ if stage == "c2" else NY
        d, _ = chain_of(n, piece, chain)
        off = -d * (s - 1)
        lo, hi = ALL_A if stage == "c2" else ALL_B
        return (at(off, piece) if stage == "c2" else at(piece, off)), pl.ds(lo, hi - lo)

    def source(key):
        stage, piece, chain, s = key
        if stage in ("c1", "c2", "d1", "d2"):
            owner, rows = origin(key)
            ref = all_ref.at[owner, rows]
            return ref, ref
        dst = slot_of[key]
        if s > 1:
            return slot_of[(stage, piece, chain, s - 1)], dst
        return local(key), dst

    def local(key):
        stage, piece, chain, s = key
        if stage in ("a1", "b1"):
            n = NZ if stage == "a1" else NY
            d, steps = chain_of(n, piece, chain)
            off = d * (steps - s + 1)
            return p_ref.at[at(off, piece), a_rows] if stage == "a1" else p_ref.at[at(piece, off), b_rows]
        n = NY if stage == "a2" else NZ
        d, steps = chain_of(n, piece, chain)
        off = (d * (steps - s + 1)) % n
        span = SUM_A if stage == "a2" else SUM_B
        lo, hi = halves(span)[piece]
        first = ("a1" if stage == "a2" else "b1", off, 0, n_first(stage) // 2)
        return slot_of[first].at[pl.ds(lo - span[0], hi - lo)]

    def n_first(stage):
        return NZ if stage == "a2" else NY

    copies = {}

    def copy_of(key):
        if key not in copies:
            src, dst = source(key)
            i = number[key]
            copies[key] = pltpu.make_async_remote_copy(
                src_ref=src,
                dst_ref=dst,
                send_sem=send_sem.at[i],
                recv_sem=recv_sem.at[i],
                device_id=device(by_key[key].link),
                device_id_type=MESH,
            )
        return copies[key]

    received, sent, waited, finished = set(), {}, set(), set()

    def receive(key):
        if key not in received:
            received.add(key)
            copy_of(key).wait_recv()

    def finish(stage, off):
        if (stage, off) in finished:
            return
        finished.add((stage, off))
        n = NZ if stage == "a1" else NY
        one, two = (stage, off, 0, n // 2), (stage, off, 1, n // 2 - 1)
        receive(one)
        receive(two)
        mine = p_ref.at[at(0, off), a_rows] if stage == "a1" else p_ref.at[at(off, 0), b_rows]
        slot_of[one][...] = slot_of[one][...] + slot_of[two][...] + mine[...]

    def issue(key):
        stage, piece, chain, s = key
        task = by_key[key]
        queue = sent.setdefault(task.link, [])
        if len(queue) >= AHEAD:
            old = queue[-AHEAD]
            if old not in waited:
                waited.add(old)
                copy_of(old).wait_send()
        for k in task.needs:
            if stage in ("a2", "b2") and k[0] in ("a1", "b1"):
                finish(k[0], k[1])
            else:
                receive(k)
        if s > 1 and stage in ("a1", "a2", "b1", "b2"):
            ref = slot_of[(stage, piece, chain, s - 1)]
            ref[...] = ref[...] + local(key)[...]
        copy_of(key).start()
        queue.append(key)

    for key in sums:
        issue(key)
    for stage, span, n, n1 in (("a2", SUM_A, NY, NZ), ("b2", SUM_B, NZ, NY)):
        first = "a1" if stage == "a2" else "b1"
        finish(first, 0)
        for h, (lo, hi) in enumerate(halves(span)):
            one, two = (stage, h, 0, n // 2), (stage, h, 1, n // 2 - 1)
            receive(one)
            receive(two)
            mine = slot_of[(first, 0, 0, n1 // 2)].at[pl.ds(lo - span[0], hi - lo)]
            own[lo:hi, :] = slot_of[one][...] + slot_of[two][...] + mine[...]

    norms = [jnp.broadcast_to(own[OWN + h : OWN + h + 1, :], (128, 128)).T for h in range(2)]
    for b in range(4):
        for h in range(2):
            natural = pl.ds(b * BLK + h, 32, stride=2)
            mine = slice(b * BLK + 32 * h, b * BLK + 32 * h + 32)
            value = (meas_ref[natural, :] - own[mine, :]) / norms[h][32 * b : 32 * b + 32]
            resid_ref[natural, :] = value
            all_ref[at(0, 0), mine, :] = value

    for key in alls:
        issue(key)
    for t in tasks:
        receive(t.key)
    for t in tasks:
        if t.key not in waited:
            copy_of(t.key).wait_send()


def exchange(p, measured):
    tasks = sum_tasks() + all_tasks()
    count = {}
    for t in tasks:
        count[t.key[0]] = count.get(t.key[0], 0) + 1
    most = {k: max(t.rows for t in tasks if t.key[0] == k) for k in count}
    return pl.pallas_call(
        exchange_kernel,
        out_shape=(
            jax.ShapeDtypeStruct((OWN, S), jnp.float32),
            jax.ShapeDtypeStruct((NZ * NY, OWN, S), jnp.float32),
        ),
        in_specs=[VM, VM],
        out_specs=(VM, VM),
        scratch_shapes=[vmem(count[k], most[k], S) for k in ("a1", "a2", "b1", "b2")]
        + [
            vmem(CH, S),
            pltpu.SemaphoreType.DMA((len(tasks),)),
            pltpu.SemaphoreType.DMA((len(tasks),)),
        ],
        compiler_params=pltpu.CompilerParams(
            collective_id=1, has_side_effects=True, vmem_limit_bytes=24 * MIB
        ),
        cost_estimate=cost(50),
        name="sum_and_spread",
    )(p, measured)


BWD = 12


def backward_kernel(code_ref, tiles_ref, all_ref, col_ref, own_ref, b_ref, resid_ref, hi_ref, lo_ref):
    resid_ref[...] = own_ref[...]

    def split(o, _):
        rows = pl.ds(pl.multiple_of(o * OWN, OWN), OWN)
        hi_ref[rows, :], lo_ref[rows, :] = split_bf16(all_ref[o])
        return _

    lax.fori_loop(0, NZ * NY, split, 0, unroll=2)
    for o in range(NA):
        b_ref[o, 0:128, :] = jnp.zeros((128, S), jnp.float32)
        b_ref[o, 128:136, :] = col_ref[o]

    def step(b, _):
        for i in range(BWD):
            codes = [code_ref[0, (b * BWD + i) * GRP + j] for j in range(GRP)]
            q = lax.shift_right_logical(codes[0], 16) & (QB - 1)
            hi, lo = split_bf16(jnp.concatenate([tile_rows(tiles_ref, c) for c in codes], axis=0).T)
            starts = [(c & (RB - 1)) * BLK for c in codes]

            def rays(ref):
                return [
                    ref[pl.ds(pl.multiple_of(start + 32 * h, 32), 32), :] for h in range(2) for start in starts
                ]

            r_hi, r_lo = rays(hi_ref), rays(lo_ref)
            left = jnp.concatenate([hi[:BLK], hi[BLK:], lo[:BLK], lo[BLK:], hi[:BLK], hi[BLK:]], axis=1)
            right = jnp.concatenate(r_hi + r_hi + r_lo, axis=0)
            out = jnp.dot(left, right, preferred_element_type=jnp.float32)
            rows = pl.ds(pl.multiple_of((q & 1) * BLK, BLK), BLK)
            b_ref[lax.shift_right_logical(q, 1), rows, :] += out
        return _

    lax.fori_loop(0, (code_ref[0, NPOS_PAD - 1] + BWD - 1) // BWD, step, 0)


def backward(code, tiles, everyone, col, own):
    return pl.pallas_call(
        backward_kernel,
        out_shape=(
            jax.ShapeDtypeStruct((NA, 136, S), jnp.float32),
            jax.ShapeDtypeStruct((OWN, S), jnp.float32),
        ),
        in_specs=[SM, VM, VM, VM, VM],
        out_specs=(VM, VM),
        scratch_shapes=[
            vmem(RB * BLK, S, dtype=jnp.bfloat16),
            vmem(RB * BLK, S, dtype=jnp.bfloat16),
        ],
        compiler_params=pltpu.CompilerParams(vmem_limit_bytes=32 * MIB),
        cost_estimate=cost(10),
        name="backward_tiles",
    )(code, tiles, everyone, col, own)


UPD = ((0, 72), (72, 136))


def update_kernel(b_ref, out_ref, sib, far_buf, near_buf, second_buf, send_sem, recv_sem):
    here = Ang()
    here.meet()
    number = iter(range(10))

    def send(to, src, dst):
        i = next(number)
        copy = pltpu.make_async_remote_copy(
            src_ref=src,
            dst_ref=dst,
            send_sem=send_sem.at[i],
            recv_sem=recv_sem.at[i],
            device_id=here.device(to),
            device_id_type=MESH,
        )
        copy.start()
        return copy

    across = {dx: send("twin", b_ref.at[here.twin(dx)], sib.at[dx]) for dx in (2, 1, 3, 0)}

    def arrive(dx):
        across[dx].wait_recv()
        sib[dx] = sib[dx] + b_ref[here.index(dx)]

    def rows(h):
        return pl.ds(UPD[h][0], UPD[h][1] - UPD[h][0])

    def part(buf, h):
        return buf.at[h, pl.ds(0, UPD[h][1] - UPD[h][0])]

    arrive(2)
    far = [send(sign_of(h), sib.at[2, rows(h)], part(far_buf, h)) for h in range(2)]
    arrive(1)
    arrive(3)
    near = [send(-sign_of(h), sib.at[-sign_of(h) % NX, rows(h)], part(near_buf, h)) for h in range(2)]
    arrive(0)
    second = []
    for h in range(2):
        far[h].wait_recv()
        part(far_buf, h)[...] = part(far_buf, h)[...] + sib[sign_of(h) % NX, rows(h), :]
        second.append(send(sign_of(h), part(far_buf, h), part(second_buf, h)))
    totals = []
    for h in range(2):
        near[h].wait_recv()
        totals.append(sib[0, rows(h), :] + part(near_buf, h)[...])
    for h in range(2):
        second[h].wait_recv()
        totals[h] = totals[h] + part(second_buf, h)[...]
    total = jnp.concatenate(totals, axis=0)
    norm = jnp.broadcast_to(total[128:129], (128, 128)).T
    out_ref[...] = RELAX * total[:128] / norm
    for copy in [*across.values(), *far, *near, *second]:
        copy.wait_send()


def update(b):
    size = UPD[0][1]
    return pl.pallas_call(
        update_kernel,
        out_shape=jax.ShapeDtypeStruct((128, S), jnp.float32),
        in_specs=[VM],
        out_specs=VM,
        scratch_shapes=[
            vmem(NX, 136, S),
            vmem(2, size, S),
            vmem(2, size, S),
            vmem(2, size, S),
            pltpu.SemaphoreType.DMA((10,)),
            pltpu.SemaphoreType.DMA((10,)),
        ],
        compiler_params=pltpu.CompilerParams(
            collective_id=2, has_side_effects=True, vmem_limit_bytes=24 * MIB
        ),
        cost_estimate=cost(7),
        name="sum_over_angles",
    )(b)


def shards(tiles, tile_ray, tile_pix, tile_count, ray_slot, image, measured):
    rows = tiles[0, 0].reshape(SLOTS // 8, 8, 32, 128).transpose(0, 2, 1, 3).reshape(SLOTS * 32, 128)
    img, code = gather_image(tile_count, tile_ray[0], tile_pix[0], ray_slot, image)
    p, col = forward(code, rows, img)
    own, everyone = exchange(p, measured[0])
    b, resid = backward(code, rows, everyone, col, own)
    return (image + update(b), resid[None])


def solution(mesh):
    in_specs = (
        P("pix", "ang", None, None),
        P("pix", "ang", None),
        P("pix", "ang", None),
        P("pix", "ang"),
        P("ang", None),
        P(("pix", "ang"), None),
        P("ang", "pix", None),
    )
    out_specs = (P(("pix", "ang"), None), P("ang", "pix", None))
    return jax.shard_map(shards, mesh=mesh, in_specs=in_specs, out_specs=out_specs, check_vma=False)
```

```python
import functools

import jax
import jax.numpy as jnp
from jax import lax
from jax.experimental import pallas as pl
from jax.experimental.pallas import tpu as pltpu
from jax.sharding import PartitionSpec as P

MESH = pl.DeviceIdType.MESH
BLK, S, SLOTS, RB, QB = 64, 128, 512, 128, 16
RELAX = 0.9
NZ, NY, NX, NA = 8, 4, 4, 8
GRP = 4
NPOS = SLOTS + QB * (GRP - 1)
NPOS_PAD = 640
OWN = 256
CH = OWN + 8
VM = pl.BlockSpec(memory_space=pltpu.VMEM)
SM = pl.BlockSpec(memory_space=pltpu.SMEM)
MIB = 1024 * 1024


def cost(us):
    return pl.CostEstimate(flops=int(us * 1.15e9), bytes_accessed=0, transcendentals=0)


def vmem(*shape, dtype=jnp.float32):
    return pltpu.VMEM(shape, dtype)


def split_bf16(x):
    hi = x.astype(jnp.bfloat16)
    return hi, (x - hi.astype(jnp.float32)).astype(jnp.bfloat16)


def sign_of(i):
    return 1 if i % 2 == 0 else -1


class Ang:
    def __init__(self):
        self.pix, me = lax.axis_index("pix"), lax.axis_index("ang")
        self.me, self.x, self.core = me, me // 2, lax.rem(me, 2)

    def index(self, dx):
        return lax.rem(self.x + dx % NX, NX) * 2 + self.core

    def twin(self, dx=0):
        return lax.rem(self.x + dx % NX, NX) * 2 + (1 - self.core)

    def device(self, to):
        if to == "twin":
            return (self.pix, self.twin())
        return (self.pix, self.twin(to // 2) if to % 2 == 0 else self.index(to))

    def meet(self, others):
        barrier = pltpu.get_barrier_semaphore()
        for to in others:
            pl.semaphore_signal(barrier, inc=1, device_id=self.device(to), device_id_type=MESH)
        pl.semaphore_wait(barrier, len(others))


def sort_tiles(ray, pix, used_tiles, table):
    f32 = jnp.float32
    both = jnp.broadcast_to((pix * RB + ray).astype(f32), (128, SLOTS)).T.astype(jnp.int32)
    lane = lax.broadcasted_iota(jnp.int32, (SLOTS, 128), 1)
    t = lax.broadcasted_iota(jnp.int32, (SLOTS, 128), 0)
    q = lax.shift_right_logical(both, 7)
    mine = jnp.where((q == lane) & (t < used_tiles), 1.0, 0.0).astype(f32)
    slot = jnp.sum(jnp.where((both & (RB - 1)) == lane, table.astype(f32), 0.0), axis=1, keepdims=True)
    earlier = lax.broadcasted_iota(jnp.int32, (SLOTS, SLOTS), 1) < lax.broadcasted_iota(jnp.int32, (SLOTS, SLOTS), 0)
    earlier = jnp.where(earlier, 1.0, 0.0).astype(jnp.bfloat16)
    before = jnp.dot(earlier, mine.astype(jnp.bfloat16), preferred_element_type=f32)
    counts = jnp.sum(mine, axis=0, keepdims=True).astype(jnp.int32)
    groups = lax.shift_right_logical(counts + (GRP - 1), 2).astype(f32)
    left_of = lax.broadcasted_iota(jnp.int32, (128, 128), 0) < lax.broadcasted_iota(jnp.int32, (128, 128), 1)
    left_of = jnp.where(left_of, 1.0, 0.0).astype(jnp.bfloat16)
    first = jnp.dot(jnp.broadcast_to(groups, (8, 128)).astype(jnp.bfloat16), left_of, preferred_element_type=f32)
    place = jnp.sum(mine * (before + GRP * first[:1]), axis=1, keepdims=True)
    place = jnp.where(t < used_tiles, place, -1.0)
    code = ((1 << 20) + q * (1 << 16) + t * RB).astype(f32) + slot
    parts = []
    for c in range(NPOS_PAD // 128):
        at = (lax.broadcasted_iota(jnp.int32, (1, 128), 1) + c * 128).astype(f32)
        part = jnp.sum(jnp.where(place == at, code, 0.0), axis=0, keepdims=True)
        parts.append(jnp.where(at == NPOS_PAD - 1, jnp.sum(groups, axis=1, keepdims=True), part))
    return jnp.concatenate(parts, axis=1).astype(jnp.int32)


def gather_kernel(
    index_ref, img_ref, out_ref, code_ref, send_sem, recv_sem
):
    here = Ang()
    here.meet(("twin", 1, -1, 2, -2))
    number = iter(range(13))

    def send(to, dx, half, src=None):
        lo, size = (0, 128) if half is None else (64 * half, 64)
        rows = out_ref.at[pl.ds(pl.multiple_of(here.index(dx) * 128 + lo, 64), size)]
        i = next(number)
        copy = pltpu.make_async_remote_copy(
            src_ref=rows if src is None else src.at[pl.ds(lo, size)],
            dst_ref=rows,
            send_sem=send_sem.at[i],
            recv_sem=recv_sem.at[i],
            device_id=here.device(to),
            device_id_type=MESH,
        )
        copy.start()
        return copy

    far = [send(sign_of(h), 0, h, img_ref) for h in range(2)]
    near = [send(-sign_of(h), 0, h, img_ref) for h in range(2)]
    across = [send("twin", 0, None, img_ref)]
    out_ref[pl.ds(pl.multiple_of(here.me * 128, 128), 128), :] = img_ref[...]
    ray, pix = index_ref[:, :SLOTS], index_ref[:, SLOTS : 2 * SLOTS]
    table, used_tiles = index_ref[:, 2 * SLOTS : 2 * SLOTS + RB], index_ref[:, 2 * SLOTS + RB :]
    code_ref[...] = sort_tiles(ray, pix, used_tiles, table)
    second = []
    for h in range(2):
        far[h].wait_recv()
        second += [send(sign_of(h), -sign_of(h), h), send(2 * sign_of(h), -sign_of(h), h)]
        across.append(send("twin", -sign_of(h), h))
    for h in range(2):
        near[h].wait_recv()
        across.append(send("twin", sign_of(h), h))
    across += second
    for copy in across:
        copy.wait_recv()
    for copy in far + near + across:
        copy.wait_send()


def gather_image(index, image):
    return pl.pallas_call(
        gather_kernel,
        out_shape=(
            jax.ShapeDtypeStruct((NA * 128, S), jnp.float32),
            jax.ShapeDtypeStruct((1, NPOS_PAD), jnp.int32),
        ),
        in_specs=[VM, VM],
        out_specs=(VM, VM),
        scratch_shapes=[
            pltpu.SemaphoreType.DMA((13,)),
            pltpu.SemaphoreType.DMA((13,)),
        ],
        compiler_params=pltpu.CompilerParams(
            collective_id=0, has_side_effects=True, vmem_limit_bytes=24 * MIB
        ),
        cost_estimate=cost(8),
        name="gather_image",
    )(index, image)


def tile_rows(tiles_ref, code):
    t = lax.shift_right_logical(code, 7) & (SLOTS - 1)
    start = lax.shift_right_logical(t, 3) * 256 + (t & 7)
    used = lax.shift_right_logical(code, 20).astype(jnp.float32)
    return tiles_ref[pl.ds(start, 32, stride=8), :] * used


FWD = 12


def forward_kernel(code_ref, tiles_ref, img_ref, p_ref, col_ref, w_ref, rowacc, colacc):
    zero = jnp.zeros((BLK, S), jnp.bfloat16)

    def weights(q, _):
        hi, lo = split_bf16(img_ref[pl.ds(pl.multiple_of(q * BLK, BLK), BLK), :])
        both = [jnp.concatenate([jnp.concatenate([x, zero], 1), jnp.concatenate([zero, x], 1)], 0) for x in (hi, lo)]
        w_ref[q] = jnp.concatenate([both[0], both[0], both[1]], axis=0)
        return _

    lax.fori_loop(0, QB, weights, 0, unroll=4)
    rowacc[...] = jnp.zeros_like(rowacc)
    colacc[...] = jnp.zeros_like(colacc)

    def clear(o, _):
        p_ref[o] = jnp.zeros((CH, S), jnp.float32)
        return _

    lax.fori_loop(0, NZ * NY, clear, 0, unroll=4)

    def place(slot):
        rows = pl.ds(pl.multiple_of((slot & 3) * BLK, BLK), BLK)
        return lax.shift_right_logical(slot, 2), rows, slice(None)

    def read(slot):
        return p_ref[place(slot)]

    def write(slot, value):
        p_ref[place(slot)] = value

    def read_rows(slot):
        return rowacc[slot]

    def write_rows(slot, value):
        rowacc[slot] = value

    def step(b, _):
        for i in range(FWD):
            codes = [code_ref[0, (b * FWD + i) * GRP + j] for j in range(GRP)]
            q = lax.shift_right_logical(codes[0], 16) & (QB - 1)
            slots = [c & (RB - 1) for c in codes]
            tiles = [tile_rows(tiles_ref, c) for c in codes]
            hi, lo = split_bf16(jnp.concatenate(tiles, axis=0))
            out = jnp.dot(jnp.concatenate([hi, lo, hi], axis=1), w_ref[q], preferred_element_type=jnp.float32)
            terms = [
                jnp.concatenate([out[32 * j : 32 * j + 32, h * S : h * S + S] for h in range(2)], axis=0)
                for j in range(GRP)
            ]
            for k, v in zip(slots, tiles):
                rowacc[k] += v
            colacc[q] += (tiles[0] + tiles[1]) + (tiles[2] + tiles[3])
            for k, v in zip(slots, terms):
                write(k, read(k) + v)
        return _

    lax.fori_loop(0, (code_ref[0, NPOS_PAD - 1] + FWD - 1) // FWD, step, 0)

    pick = lax.broadcasted_iota(jnp.int32, (8, 128), 0) == (lax.broadcasted_iota(jnp.int32, (8, 128), 1) // BLK)
    pick = pick.astype(jnp.float32).astype(jnp.bfloat16)

    def row_sums(o, _):
        hi, lo = split_bf16(rowacc[pl.ds(o * 4, 4)].reshape(128, 128))
        dims = (((1,), (1,)), ((), ()))
        sums = lax.dot_general(pick, hi, dims, preferred_element_type=jnp.float32)
        sums += lax.dot_general(pick, lo, dims, preferred_element_type=jnp.float32)
        p_ref[o, OWN:CH, :] = sums
        return _

    lax.fori_loop(0, NZ * NY, row_sums, 0, unroll=16)
    low = lax.broadcasted_iota(jnp.int32, (1, 128), 1) < BLK
    for o in range(NA):
        a = jnp.sum(colacc[2 * o], axis=0, keepdims=True)
        b = jnp.sum(colacc[2 * o + 1], axis=0, keepdims=True)
        a = a + pltpu.roll(a, BLK, 1)
        b = b + pltpu.roll(b, BLK, 1)
        col_ref[o] = jnp.broadcast_to(jnp.where(low, a, b), (8, 128))


def forward(code, tiles, img):
    return pl.pallas_call(
        forward_kernel,
        out_shape=(
            jax.ShapeDtypeStruct((NZ * NY, CH, S), jnp.float32),
            jax.ShapeDtypeStruct((NA, 8, 128), jnp.float32),
        ),
        in_specs=[SM, VM, VM],
        out_specs=(VM, VM),
        scratch_shapes=[
            vmem(QB, 6 * BLK, 2 * S, dtype=jnp.bfloat16),
            vmem(RB, 32, 128),
            vmem(QB, 32, 128),
        ],
        compiler_params=pltpu.CompilerParams(vmem_limit_bytes=32 * MIB),
        cost_estimate=cost(13),
        name="forward_tiles",
    )(code, tiles, img)


def ring_steps(n, sign):
    return ((sign, n // 2), (-sign, n // 2 - 1))


class Task:
    def __init__(self, key, link, rows, needs):
        self.key, self.link, self.rows, self.needs = key, link, rows, needs


def schedule(tasks, latency, rate):
    by_key = {t.key: t for t in tasks}
    follow = {t.key: [] for t in tasks}
    for t in tasks:
        for k in t.needs:
            follow[k].append(t.key)
    tail = {}

    def tail_of(k):
        if k not in tail:
            t = by_key[k]
            tail[k] = t.rows / rate + latency + max([tail_of(f) for f in follow[k]], default=0.0)
        return tail[k]

    left, done, free, order = list(tasks), {}, {}, []
    while left:
        best = None
        for t in left:
            if all(k in done for k in t.needs):
                at = max([done[k] for k in t.needs], default=0.0)
                start = max(at, free.get(t.link, 0.0))
                rank = (start, -tail_of(t.key))
                if best is None or rank < best[0]:
                    best = (rank, t)
        (start, _), t = best
        free[t.link] = start + t.rows / rate
        done[t.key] = start + t.rows / rate + latency
        order.append((start, t.key))
        left.remove(t)
    return [k for _, k in sorted(order, key=lambda e: e[0])]


RATE = 95.0
LATENCY = 2.5

SUM_A = (0, 104)
SUM_B = (104, 264)
ALL_A = (0, 104)
ALL_B = (104, 256)


def halves(span):
    lo, hi = span
    mid = lo + ((hi - lo) // 2 + 7) // 8 * 8
    return ((lo, mid), (mid, hi))


def sum_tasks():
    tasks = []

    def ring(stage, n, axis, piece, sign, rows, local_needs):
        for chain, (d, steps) in enumerate(ring_steps(n, sign)):
            for s in range(1, steps + 1):
                off = (d * (steps - s + 1)) % n
                needs = [(stage, piece, chain, s - 1)] if s > 1 else []
                tasks.append(Task((stage, piece, chain, s), (axis, d), rows, needs + local_needs(off)))

    def last(stage, n, piece):
        return [(stage, piece, 0, n // 2), (stage, piece, 1, n // 2 - 1)]

    for yo in range(NY):
        ring("a1", NZ, "z", yo, sign_of(yo), SUM_A[1] - SUM_A[0], lambda off: [])
    for h, (lo, hi) in enumerate(halves(SUM_A)):
        ring("a2", NY, "y", h, sign_of(h), hi - lo, lambda off: last("a1", NZ, off))
    for zo in range(NZ):
        ring("b1", NY, "y", zo, sign_of(zo), SUM_B[1] - SUM_B[0], lambda off: [])
    for h, (lo, hi) in enumerate(halves(SUM_B)):
        ring("b2", NZ, "z", h, sign_of(h), hi - lo, lambda off: last("b1", NY, off))
    return tasks


def all_tasks():
    tasks = []

    def ring(stage, n, axis, piece, sign, rows, first_needs):
        for chain, (d, steps) in enumerate(ring_steps(n, sign)):
            for s in range(1, steps + 1):
                needs = [(stage, piece, chain, s - 1)] if s > 1 else first_needs
                tasks.append(Task((stage, piece, chain, s), (axis, d), rows, needs))

    def arrives(stage, n, piece, sign, off):
        for chain, (d, steps) in enumerate(ring_steps(n, sign)):
            for s in range(1, steps + 1):
                if (-d * s) % n == off:
                    return (stage, piece, chain, s)

    for h, (lo, hi) in enumerate(halves(ALL_A)):
        ring("c1", NY, "y", h, sign_of(h), hi - lo, [])
    for yo in range(NY):
        needs = [arrives("c1", NY, h, sign_of(h), yo) for h in range(2)] if yo else []
        ring("c2", NZ, "z", yo, sign_of(yo), ALL_A[1] - ALL_A[0], needs)
    for h, (lo, hi) in enumerate(halves(ALL_B)):
        ring("d1", NZ, "z", h, sign_of(h), hi - lo, [])
    for zo in range(NZ):
        needs = [arrives("d1", NZ, h, sign_of(h), zo) for h in range(2)] if zo else []
        ring("d2", NY, "y", zo, sign_of(zo), ALL_B[1] - ALL_B[0], needs)
    return tasks


AHEAD = 3


def exchange_kernel(p_ref, meas_ref, resid_ref, all_ref, ra1, ra2, rb1, rb2, own, send_sem, recv_sem):
    pix, ang = lax.axis_index("pix"), lax.axis_index("ang")
    z, y = pix // NY, lax.rem(pix, NY)

    def at(zo, yo):
        return lax.rem(z + zo % NZ, NZ) * NY + lax.rem(y + yo % NY, NY)

    def device(link):
        axis, d = link
        return (at(d, 0) if axis == "z" else at(0, d), ang)

    barrier = pltpu.get_barrier_semaphore()
    for link in (("z", 1), ("z", -1), ("y", 1), ("y", -1)):
        pl.semaphore_signal(barrier, inc=1, device_id=device(link), device_id_type=MESH)
    pl.semaphore_wait(barrier, 4)

    tasks = sum_tasks() + all_tasks()
    number = {t.key: i for i, t in enumerate(tasks)}
    by_key = {t.key: t for t in tasks}
    sums = schedule(sum_tasks(), LATENCY, RATE)
    alls = schedule(all_tasks(), LATENCY, RATE)

    a_rows, b_rows = pl.ds(SUM_A[0], SUM_A[1] - SUM_A[0]), pl.ds(SUM_B[0], SUM_B[1] - SUM_B[0])
    slot_of = {}
    for stage, ref in (("a1", ra1), ("a2", ra2), ("b1", rb1), ("b2", rb2)):
        keys = [t.key for t in tasks if t.key[0] == stage]
        for i, k in enumerate(keys):
            slot_of[k] = ref.at[i, pl.ds(0, by_key[k].rows)]

    def chain_of(n, piece, chain):
        return ring_steps(n, sign_of(piece))[chain]

    def origin(key):
        stage, piece, chain, s = key
        if stage in ("c1", "d1"):
            n = NY if stage == "c1" else NZ
            d, _ = chain_of(n, piece, chain)
            off = -d * (s - 1)
            lo, hi = halves(ALL_A if stage == "c1" else ALL_B)[piece]
            return (at(0, off) if stage == "c1" else at(off, 0)), pl.ds(lo, hi - lo)
        n = NZ if stage == "c2" else NY
        d, _ = chain_of(n, piece, chain)
        off = -d * (s - 1)
        lo, hi = ALL_A if stage == "c2" else ALL_B
        return (at(off, piece) if stage == "c2" else at(piece, off)), pl.ds(lo, hi - lo)

    def source(key):
        stage, piece, chain, s = key
        if stage in ("c1", "c2", "d1", "d2"):
            owner, rows = origin(key)
            ref = all_ref.at[owner, rows]
            return ref, ref
        dst = slot_of[key]
        if s > 1:
            return slot_of[(stage, piece, chain, s - 1)], dst
        return local(key), dst

    def local(key):
        stage, piece, chain, s = key
        if stage in ("a1", "b1"):
            n = NZ if stage == "a1" else NY
            d, steps = chain_of(n, piece, chain)
            off = d * (steps - s + 1)
            return p_ref.at[at(off, piece), a_rows] if stage == "a1" else p_ref.at[at(piece, off), b_rows]
        n = NY if stage == "a2" else NZ
        d, steps = chain_of(n, piece, chain)
        off = (d * (steps - s + 1)) % n
        span = SUM_A if stage == "a2" else SUM_B
        lo, hi = halves(span)[piece]
        first = ("a1" if stage == "a2" else "b1", off, 0, n_first(stage) // 2)
        return slot_of[first].at[pl.ds(lo - span[0], hi - lo)]

    def n_first(stage):
        return NZ if stage == "a2" else NY

    copies = {}

    def copy_of(key):
        if key not in copies:
            src, dst = source(key)
            i = number[key]
            copies[key] = pltpu.make_async_remote_copy(
                src_ref=src,
                dst_ref=dst,
                send_sem=send_sem.at[i],
                recv_sem=recv_sem.at[i],
                device_id=device(by_key[key].link),
                device_id_type=MESH,
            )
        return copies[key]

    received, sent, waited, finished = set(), {}, set(), set()

    def receive(key):
        if key not in received:
            received.add(key)
            copy_of(key).wait_recv()

    def finish(stage, off):
        if (stage, off) in finished:
            return
        finished.add((stage, off))
        n = NZ if stage == "a1" else NY
        one, two = (stage, off, 0, n // 2), (stage, off, 1, n // 2 - 1)
        receive(one)
        receive(two)
        mine = p_ref.at[at(0, off), a_rows] if stage == "a1" else p_ref.at[at(off, 0), b_rows]
        slot_of[one][...] = slot_of[one][...] + slot_of[two][...] + mine[...]

    def issue(key):
        stage, piece, chain, s = key
        task = by_key[key]
        queue = sent.setdefault(task.link, [])
        if len(queue) >= AHEAD:
            old = queue[-AHEAD]
            if old not in waited:
                waited.add(old)
                copy_of(old).wait_send()
        for k in task.needs:
            if stage in ("a2", "b2") and k[0] in ("a1", "b1"):
                finish(k[0], k[1])
            else:
                receive(k)
        if s > 1 and stage in ("a1", "a2", "b1", "b2"):
            ref = slot_of[(stage, piece, chain, s - 1)]
            ref[...] = ref[...] + local(key)[...]
        copy_of(key).start()
        queue.append(key)

    for key in sums:
        issue(key)
    for stage, span, n, n1 in (("a2", SUM_A, NY, NZ), ("b2", SUM_B, NZ, NY)):
        first = "a1" if stage == "a2" else "b1"
        finish(first, 0)
        for h, (lo, hi) in enumerate(halves(span)):
            one, two = (stage, h, 0, n // 2), (stage, h, 1, n // 2 - 1)
            receive(one)
            receive(two)
            mine = slot_of[(first, 0, 0, n1 // 2)].at[pl.ds(lo - span[0], hi - lo)]
            own[lo:hi, :] = slot_of[one][...] + slot_of[two][...] + mine[...]

    norms = [jnp.broadcast_to(own[OWN + h : OWN + h + 1, :], (128, 128)).T for h in range(2)]
    for b in range(4):
        for h in range(2):
            natural = pl.ds(b * BLK + h, 32, stride=2)
            mine = slice(b * BLK + 32 * h, b * BLK + 32 * h + 32)
            value = (meas_ref[natural, :] - own[mine, :]) / norms[h][32 * b : 32 * b + 32]
            resid_ref[natural, :] = value
            all_ref[at(0, 0), mine, :] = value

    for key in alls:
        issue(key)
    for t in tasks:
        receive(t.key)
    for t in tasks:
        if t.key not in waited:
            copy_of(t.key).wait_send()


def exchange(p, measured):
    tasks = sum_tasks() + all_tasks()
    count = {}
    for t in tasks:
        count[t.key[0]] = count.get(t.key[0], 0) + 1
    most = {k: max(t.rows for t in tasks if t.key[0] == k) for k in count}
    return pl.pallas_call(
        exchange_kernel,
        out_shape=(
            jax.ShapeDtypeStruct((OWN, S), jnp.float32),
            jax.ShapeDtypeStruct((NZ * NY, OWN, S), jnp.float32),
        ),
        in_specs=[VM, VM],
        out_specs=(VM, VM),
        scratch_shapes=[vmem(count[k], most[k], S) for k in ("a1", "a2", "b1", "b2")]
        + [
            vmem(CH, S),
            pltpu.SemaphoreType.DMA((len(tasks),)),
            pltpu.SemaphoreType.DMA((len(tasks),)),
        ],
        compiler_params=pltpu.CompilerParams(
            collective_id=1, has_side_effects=True, vmem_limit_bytes=24 * MIB
        ),
        cost_estimate=cost(50),
        name="sum_and_spread",
    )(p, measured)


BWD = 12


def backward_kernel(code_ref, tiles_ref, all_ref, col_ref, own_ref, b_ref, resid_ref, hi_ref, lo_ref):
    resid_ref[...] = own_ref[...]

    def split(o, _):
        rows = pl.ds(pl.multiple_of(o * OWN, OWN), OWN)
        hi_ref[rows, :], lo_ref[rows, :] = split_bf16(all_ref[o])
        return _

    lax.fori_loop(0, NZ * NY, split, 0, unroll=2)
    for o in range(NA):
        b_ref[o, 0:128, :] = jnp.zeros((128, S), jnp.float32)
        b_ref[o, 128:136, :] = col_ref[o]

    def step(b, _):
        for i in range(BWD):
            codes = [code_ref[0, (b * BWD + i) * GRP + j] for j in range(GRP)]
            q = lax.shift_right_logical(codes[0], 16) & (QB - 1)
            hi, lo = split_bf16(jnp.concatenate([tile_rows(tiles_ref, c) for c in codes], axis=0).T)
            starts = [(c & (RB - 1)) * BLK for c in codes]

            def rays(ref):
                return [
                    ref[pl.ds(pl.multiple_of(start + 32 * h, 32), 32), :] for h in range(2) for start in starts
                ]

            r_hi, r_lo = rays(hi_ref), rays(lo_ref)
            left = jnp.concatenate([hi[:BLK], hi[BLK:], lo[:BLK], lo[BLK:], hi[:BLK], hi[BLK:]], axis=1)
            right = jnp.concatenate(r_hi + r_hi + r_lo, axis=0)
            out = jnp.dot(left, right, preferred_element_type=jnp.float32)
            rows = pl.ds(pl.multiple_of((q & 1) * BLK, BLK), BLK)
            b_ref[lax.shift_right_logical(q, 1), rows, :] += out
        return _

    lax.fori_loop(0, (code_ref[0, NPOS_PAD - 1] + BWD - 1) // BWD, step, 0)


def backward(code, tiles, everyone, col, own):
    return pl.pallas_call(
        backward_kernel,
        out_shape=(
            jax.ShapeDtypeStruct((NA, 136, S), jnp.float32),
            jax.ShapeDtypeStruct((OWN, S), jnp.float32),
        ),
        in_specs=[SM, VM, VM, VM, VM],
        out_specs=(VM, VM),
        scratch_shapes=[
            vmem(RB * BLK, S, dtype=jnp.bfloat16),
            vmem(RB * BLK, S, dtype=jnp.bfloat16),
        ],
        compiler_params=pltpu.CompilerParams(vmem_limit_bytes=32 * MIB),
        cost_estimate=cost(10),
        name="backward_tiles",
    )(code, tiles, everyone, col, own)


UPD = ((0, 72), (72, 136))


def update_kernel(b_ref, out_ref, sib, far_buf, near_buf, second_buf, send_sem, recv_sem):
    here = Ang()
    here.meet(("twin", 1, -1))
    number = iter(range(10))

    def send(to, src, dst):
        i = next(number)
        copy = pltpu.make_async_remote_copy(
            src_ref=src,
            dst_ref=dst,
            send_sem=send_sem.at[i],
            recv_sem=recv_sem.at[i],
            device_id=here.device(to),
            device_id_type=MESH,
        )
        copy.start()
        return copy

    across = {dx: send("twin", b_ref.at[here.twin(dx)], sib.at[dx]) for dx in (2, 1, 3, 0)}

    def arrive(dx):
        across[dx].wait_recv()
        sib[dx] = sib[dx] + b_ref[here.index(dx)]

    def rows(h):
        return pl.ds(UPD[h][0], UPD[h][1] - UPD[h][0])

    def part(buf, h):
        return buf.at[h, pl.ds(0, UPD[h][1] - UPD[h][0])]

    arrive(2)
    far = [send(sign_of(h), sib.at[2, rows(h)], part(far_buf, h)) for h in range(2)]
    arrive(1)
    arrive(3)
    near = [send(-sign_of(h), sib.at[-sign_of(h) % NX, rows(h)], part(near_buf, h)) for h in range(2)]
    arrive(0)
    second = []
    for h in range(2):
        far[h].wait_recv()
        part(far_buf, h)[...] = part(far_buf, h)[...] + sib[sign_of(h) % NX, rows(h), :]
        second.append(send(sign_of(h), part(far_buf, h), part(second_buf, h)))
    totals = []
    for h in range(2):
        near[h].wait_recv()
        totals.append(sib[0, rows(h), :] + part(near_buf, h)[...])
    for h in range(2):
        second[h].wait_recv()
        totals[h] = totals[h] + part(second_buf, h)[...]
    total = jnp.concatenate(totals, axis=0)
    norm = jnp.broadcast_to(total[128:129], (128, 128)).T
    out_ref[...] = RELAX * total[:128] / norm
    for copy in [*across.values(), *far, *near, *second]:
        copy.wait_send()


def update(b):
    size = UPD[0][1]
    return pl.pallas_call(
        update_kernel,
        out_shape=jax.ShapeDtypeStruct((128, S), jnp.float32),
        in_specs=[VM],
        out_specs=VM,
        scratch_shapes=[
            vmem(NX, 136, S),
            vmem(2, size, S),
            vmem(2, size, S),
            vmem(2, size, S),
            pltpu.SemaphoreType.DMA((10,)),
            pltpu.SemaphoreType.DMA((10,)),
        ],
        compiler_params=pltpu.CompilerParams(
            collective_id=2, has_side_effects=True, vmem_limit_bytes=24 * MIB
        ),
        cost_estimate=cost(7),
        name="sum_over_angles",
    )(b)


def shards(tiles, tile_ray, tile_pix, tile_count, ray_slot, image, measured):
    rows = tiles[0, 0].reshape(SLOTS // 8, 8, 32, 128).transpose(0, 2, 1, 3).reshape(SLOTS * 32, 128)
    used_tiles = jnp.broadcast_to(tile_count[0], (RB,))
    index = jnp.concatenate([tile_ray[0, 0], tile_pix[0, 0], ray_slot[0], used_tiles])[None]
    img, code = gather_image(index, image)
    p, col = forward(code, rows, img)
    own, everyone = exchange(p, measured[0])
    b, resid = backward(code, rows, everyone, col, own)
    return (image + update(b), resid[None])


def solution(mesh):
    in_specs = (
        P("pix", "ang", None, None),
        P("pix", "ang", None),
        P("pix", "ang", None),
        P("pix", "ang"),
        P("ang", None),
        P(("pix", "ang"), None),
        P("ang", "pix", None),
    )
    out_specs = (P(("pix", "ang"), None), P("ang", "pix", None))
    return jax.shard_map(shards, mesh=mesh, in_specs=in_specs, out_specs=out_specs, check_vma=False)
```

```python
import functools

import jax
import jax.numpy as jnp
from jax import lax
from jax.experimental import pallas as pl
from jax.experimental.pallas import tpu as pltpu
from jax.sharding import PartitionSpec as P

MESH = pl.DeviceIdType.MESH
BLK, S, SLOTS, RB, QB = 64, 128, 512, 128, 16
RELAX = 0.9
NZ, NY, NX, NA = 8, 4, 4, 8
GRP = 4
NPOS = SLOTS + QB * (GRP - 1)
NPOS_PAD = 640
LIST = NPOS_PAD + 128
BWD = 12
STEPS = NPOS // GRP // BWD + 1
OWN = 256
CH = OWN + 8
VM = pl.BlockSpec(memory_space=pltpu.VMEM)
SM = pl.BlockSpec(memory_space=pltpu.SMEM)
MIB = 1024 * 1024


def cost(us):
    return pl.CostEstimate(flops=int(us * 1.15e9), bytes_accessed=0, transcendentals=0)


def vmem(*shape, dtype=jnp.float32):
    return pltpu.VMEM(shape, dtype)


def split_bf16(x):
    hi = x.astype(jnp.bfloat16)
    return hi, (x - hi.astype(jnp.float32)).astype(jnp.bfloat16)


def sign_of(i):
    return 1 if i % 2 == 0 else -1


class Ang:
    def __init__(self):
        self.pix, me = lax.axis_index("pix"), lax.axis_index("ang")
        self.me, self.x, self.core = me, me // 2, lax.rem(me, 2)

    def index(self, dx):
        return lax.rem(self.x + dx % NX, NX) * 2 + self.core

    def twin(self, dx=0):
        return lax.rem(self.x + dx % NX, NX) * 2 + (1 - self.core)

    def device(self, to):
        if to == "twin":
            return (self.pix, self.twin())
        return (self.pix, self.twin(to // 2) if to % 2 == 0 else self.index(to))

    def meet(self, others):
        barrier = pltpu.get_barrier_semaphore()
        for to in others:
            pl.semaphore_signal(barrier, inc=1, device_id=self.device(to), device_id_type=MESH)
        return lambda: pl.semaphore_wait(barrier, len(others))


def sort_tiles(ray, pix, used_tiles, table):
    f32 = jnp.float32
    both = jnp.broadcast_to((pix * RB + ray).astype(f32), (128, SLOTS)).T.astype(jnp.int32)
    lane = lax.broadcasted_iota(jnp.int32, (SLOTS, 128), 1)
    t = lax.broadcasted_iota(jnp.int32, (SLOTS, 128), 0)
    q = lax.shift_right_logical(both, 7)
    mine = jnp.where((q == lane) & (t < used_tiles), 1.0, 0.0).astype(f32)
    slot = jnp.sum(jnp.where((both & (RB - 1)) == lane, table.astype(f32), 0.0), axis=1, keepdims=True)
    earlier = lax.broadcasted_iota(jnp.int32, (SLOTS, SLOTS), 1) < lax.broadcasted_iota(jnp.int32, (SLOTS, SLOTS), 0)
    earlier = jnp.where(earlier, 1.0, 0.0).astype(jnp.bfloat16)
    before = jnp.dot(earlier, mine.astype(jnp.bfloat16), preferred_element_type=f32)
    counts = jnp.sum(mine, axis=0, keepdims=True).astype(jnp.int32)
    groups = lax.shift_right_logical(counts + (GRP - 1), 2).astype(f32)
    left_of = lax.broadcasted_iota(jnp.int32, (128, 128), 0) < lax.broadcasted_iota(jnp.int32, (128, 128), 1)
    left_of = jnp.where(left_of, 1.0, 0.0).astype(jnp.bfloat16)
    first = jnp.dot(jnp.broadcast_to(groups, (8, 128)).astype(jnp.bfloat16), left_of, preferred_element_type=f32)
    place = jnp.sum(mine * (before + GRP * first[:1]), axis=1, keepdims=True)
    place = jnp.where(t < used_tiles, place, -1.0)
    code = ((1 << 20) + q * (1 << 16) + t * RB).astype(f32) + slot
    parts = []
    for c in range(NPOS_PAD // 128):
        at = (lax.broadcasted_iota(jnp.int32, (1, 128), 1) + c * 128).astype(f32)
        part = jnp.sum(jnp.where(place == at, code, 0.0), axis=0, keepdims=True)
        parts.append(jnp.where(at == NPOS_PAD - 1, jnp.sum(groups, axis=1, keepdims=True), part))
    parts.append(jnp.where(groups > 0.0, first[:1] + groups - 1.0, -1.0))
    return jnp.concatenate(parts, axis=1).astype(jnp.int32)


def gather_kernel(
    index_ref, img_ref, out_ref, code_ref, send_sem, recv_sem
):
    here = Ang()
    here.meet(("twin", 1, -1, 2, -2))()
    number = iter(range(13))

    def send(to, dx, half, src=None):
        lo, size = (0, 128) if half is None else (64 * half, 64)
        rows = out_ref.at[pl.ds(pl.multiple_of(here.index(dx) * 128 + lo, 64), size)]
        i = next(number)
        copy = pltpu.make_async_remote_copy(
            src_ref=rows if src is None else src.at[pl.ds(lo, size)],
            dst_ref=rows,
            send_sem=send_sem.at[i],
            recv_sem=recv_sem.at[i],
            device_id=here.device(to),
            device_id_type=MESH,
        )
        copy.start()
        return copy

    far = [send(sign_of(h), 0, h, img_ref) for h in range(2)]
    near = [send(-sign_of(h), 0, h, img_ref) for h in range(2)]
    across = [send("twin", 0, None, img_ref)]
    out_ref[pl.ds(pl.multiple_of(here.me * 128, 128), 128), :] = img_ref[...]
    ray, pix = index_ref[:, :SLOTS], index_ref[:, SLOTS : 2 * SLOTS]
    table, used_tiles = index_ref[:, 2 * SLOTS : 2 * SLOTS + RB], index_ref[:, 2 * SLOTS + RB :]
    code_ref[...] = sort_tiles(ray, pix, used_tiles, table)
    second = []
    for h in range(2):
        far[h].wait_recv()
        second += [send(sign_of(h), -sign_of(h), h), send(2 * sign_of(h), -sign_of(h), h)]
        across.append(send("twin", -sign_of(h), h))
    for h in range(2):
        near[h].wait_recv()
        across.append(send("twin", sign_of(h), h))
    across += second
    for copy in across:
        copy.wait_recv()
    for copy in far + near + across:
        copy.wait_send()


def gather_image(index, image):
    return pl.pallas_call(
        gather_kernel,
        out_shape=(
            jax.ShapeDtypeStruct((NA * 128, S), jnp.float32),
            jax.ShapeDtypeStruct((1, LIST), jnp.int32),
        ),
        in_specs=[VM, VM],
        out_specs=(VM, VM),
        scratch_shapes=[
            pltpu.SemaphoreType.DMA((13,)),
            pltpu.SemaphoreType.DMA((13,)),
        ],
        compiler_params=pltpu.CompilerParams(
            collective_id=0, has_side_effects=True, vmem_limit_bytes=24 * MIB
        ),
        cost_estimate=cost(8),
        name="gather_image",
    )(index, image)


def tile_rows(tiles_ref, code):
    t = lax.shift_right_logical(code, 7) & (SLOTS - 1)
    start = lax.shift_right_logical(t, 3) * 256 + (t & 7)
    used = lax.shift_right_logical(code, 20).astype(jnp.float32)
    return tiles_ref[pl.ds(start, 32, stride=8), :] * used


FWD = 12


def forward_kernel(code_ref, tiles_ref, img_ref, p_ref, col_ref, turned_ref, w_ref, rowacc, colacc):
    zero = jnp.zeros((BLK, S), jnp.bfloat16)

    def weights(q, _):
        hi, lo = split_bf16(img_ref[pl.ds(pl.multiple_of(q * BLK, BLK), BLK), :])
        both = [jnp.concatenate([jnp.concatenate([x, zero], 1), jnp.concatenate([zero, x], 1)], 0) for x in (hi, lo)]
        w_ref[q] = jnp.concatenate([both[0], both[0], both[1]], axis=0)
        return _

    lax.fori_loop(0, QB, weights, 0, unroll=4)
    rowacc[...] = jnp.zeros_like(rowacc)
    colacc[...] = jnp.zeros_like(colacc)

    def clear(o, _):
        p_ref[o] = jnp.zeros((CH, S), jnp.float32)
        return _

    lax.fori_loop(0, NZ * NY, clear, 0, unroll=4)

    def place(slot):
        rows = pl.ds(pl.multiple_of((slot & 3) * BLK, BLK), BLK)
        return lax.shift_right_logical(slot, 2), rows, slice(None)

    def read(slot):
        return p_ref[place(slot)]

    def write(slot, value):
        p_ref[place(slot)] = value

    def read_rows(slot):
        return rowacc[slot]

    def write_rows(slot, value):
        rowacc[slot] = value

    def step(b, _):
        for i in range(FWD):
            codes = [code_ref[0, (b * FWD + i) * GRP + j] for j in range(GRP)]
            q = lax.shift_right_logical(codes[0], 16) & (QB - 1)
            slots = [c & (RB - 1) for c in codes]
            tiles = [tile_rows(tiles_ref, c) for c in codes]
            hi, lo = split_bf16(jnp.concatenate(tiles, axis=0))
            turned_ref[b * FWD + i] = jnp.concatenate([hi.T, lo.T], axis=1)
            out = jnp.dot(jnp.concatenate([hi, lo, hi], axis=1), w_ref[q], preferred_element_type=jnp.float32)
            terms = [
                jnp.concatenate([out[32 * j : 32 * j + 32, h * S : h * S + S] for h in range(2)], axis=0)
                for j in range(GRP)
            ]
            for k, v in zip(slots, tiles):
                rowacc[k] += v
            colacc[q] += (tiles[0] + tiles[1]) + (tiles[2] + tiles[3])
            for k, v in zip(slots, terms):
                write(k, read(k) + v)
        return _

    lax.fori_loop(0, (code_ref[0, NPOS_PAD - 1] + FWD - 1) // FWD, step, 0)

    pick = lax.broadcasted_iota(jnp.int32, (8, 128), 0) == (lax.broadcasted_iota(jnp.int32, (8, 128), 1) // BLK)
    pick = pick.astype(jnp.float32).astype(jnp.bfloat16)

    def row_sums(o, _):
        hi, lo = split_bf16(rowacc[pl.ds(o * 4, 4)].reshape(128, 128))
        dims = (((1,), (1,)), ((), ()))
        sums = lax.dot_general(pick, hi, dims, preferred_element_type=jnp.float32)
        sums += lax.dot_general(pick, lo, dims, preferred_element_type=jnp.float32)
        p_ref[o, OWN:CH, :] = sums
        return _

    lax.fori_loop(0, NZ * NY, row_sums, 0, unroll=16)
    low = lax.broadcasted_iota(jnp.int32, (1, 128), 1) < BLK
    for o in range(NA):
        a = jnp.sum(colacc[2 * o], axis=0, keepdims=True)
        b = jnp.sum(colacc[2 * o + 1], axis=0, keepdims=True)
        a = a + pltpu.roll(a, BLK, 1)
        b = b + pltpu.roll(b, BLK, 1)
        col_ref[o] = jnp.broadcast_to(jnp.where(low, a, b), (8, 128))


def forward(code, tiles, img):
    return pl.pallas_call(
        forward_kernel,
        out_shape=(
            jax.ShapeDtypeStruct((NZ * NY, CH, S), jnp.float32),
            jax.ShapeDtypeStruct((NA, 8, 128), jnp.float32),
            jax.ShapeDtypeStruct((STEPS * BWD, 128, 2 * 128), jnp.bfloat16),
        ),
        in_specs=[SM, VM, VM],
        out_specs=(VM, VM, VM),
        scratch_shapes=[
            vmem(QB, 6 * BLK, 2 * S, dtype=jnp.bfloat16),
            vmem(RB, 32, 128),
            vmem(QB, 32, 128),
        ],
        compiler_params=pltpu.CompilerParams(vmem_limit_bytes=32 * MIB),
        cost_estimate=cost(13),
        name="forward_tiles",
    )(code, tiles, img)


def ring_steps(n, sign):
    return ((sign, n // 2), (-sign, n // 2 - 1))


class Task:
    def __init__(self, key, link, rows, needs):
        self.key, self.link, self.rows, self.needs = key, link, rows, needs


def schedule(tasks, latency, rate):
    by_key = {t.key: t for t in tasks}
    follow = {t.key: [] for t in tasks}
    for t in tasks:
        for k in t.needs:
            follow[k].append(t.key)
    tail = {}

    def tail_of(k):
        if k not in tail:
            t = by_key[k]
            tail[k] = t.rows / rate + latency + max([tail_of(f) for f in follow[k]], default=0.0)
        return tail[k]

    left, done, free, order = list(tasks), {}, {}, []
    while left:
        best = None
        for t in left:
            if all(k in done for k in t.needs):
                at = max([done[k] for k in t.needs], default=0.0)
                start = max(at, free.get(t.link, 0.0))
                rank = (start, -tail_of(t.key))
                if best is None or rank < best[0]:
                    best = (rank, t)
        (start, _), t = best
        free[t.link] = start + t.rows / rate
        done[t.key] = start + t.rows / rate + latency
        order.append((start, t.key))
        left.remove(t)
    return [k for _, k in sorted(order, key=lambda e: e[0])]


RATE = 95.0
LATENCY = 2.5

SUM_A = (0, 104)
SUM_B = (104, 264)
ALL_A = (0, 104)
ALL_B = (104, 256)


def halves(span):
    lo, hi = span
    mid = lo + ((hi - lo) // 2 + 7) // 8 * 8
    return ((lo, mid), (mid, hi))


def sum_tasks():
    tasks = []

    def ring(stage, n, axis, piece, sign, rows, local_needs):
        for chain, (d, steps) in enumerate(ring_steps(n, sign)):
            for s in range(1, steps + 1):
                off = (d * (steps - s + 1)) % n
                needs = [(stage, piece, chain, s - 1)] if s > 1 else []
                tasks.append(Task((stage, piece, chain, s), (axis, d), rows, needs + local_needs(off)))

    def last(stage, n, piece):
        return [(stage, piece, 0, n // 2), (stage, piece, 1, n // 2 - 1)]

    for yo in range(NY):
        ring("a1", NZ, "z", yo, sign_of(yo), SUM_A[1] - SUM_A[0], lambda off: [])
    for h, (lo, hi) in enumerate(halves(SUM_A)):
        ring("a2", NY, "y", h, sign_of(h), hi - lo, lambda off: last("a1", NZ, off))
    for zo in range(NZ):
        ring("b1", NY, "y", zo, sign_of(zo), SUM_B[1] - SUM_B[0], lambda off: [])
    for h, (lo, hi) in enumerate(halves(SUM_B)):
        ring("b2", NZ, "z", h, sign_of(h), hi - lo, lambda off: last("b1", NY, off))
    return tasks


def all_tasks():
    tasks = []

    def ring(stage, n, axis, piece, sign, rows, first_needs):
        for chain, (d, steps) in enumerate(ring_steps(n, sign)):
            for s in range(1, steps + 1):
                needs = [(stage, piece, chain, s - 1)] if s > 1 else first_needs
                tasks.append(Task((stage, piece, chain, s), (axis, d), rows, needs))

    def arrives(stage, n, piece, sign, off):
        for chain, (d, steps) in enumerate(ring_steps(n, sign)):
            for s in range(1, steps + 1):
                if (-d * s) % n == off:
                    return (stage, piece, chain, s)

    for h, (lo, hi) in enumerate(halves(ALL_A)):
        ring("c1", NY, "y", h, sign_of(h), hi - lo, [])
    for yo in range(NY):
        needs = [arrives("c1", NY, h, sign_of(h), yo) for h in range(2)] if yo else []
        ring("c2", NZ, "z", yo, sign_of(yo), ALL_A[1] - ALL_A[0], needs)
    for h, (lo, hi) in enumerate(halves(ALL_B)):
        ring("d1", NZ, "z", h, sign_of(h), hi - lo, [])
    for zo in range(NZ):
        needs = [arrives("d1", NZ, h, sign_of(h), zo) for h in range(2)] if zo else []
        ring("d2", NY, "y", zo, sign_of(zo), ALL_B[1] - ALL_B[0], needs)
    return tasks


AHEAD = 3


def exchange_kernel(p_ref, meas_ref, resid_ref, all_ref, ra1, ra2, rb1, rb2, own, send_sem, recv_sem):
    pix, ang = lax.axis_index("pix"), lax.axis_index("ang")
    z, y = pix // NY, lax.rem(pix, NY)

    def at(zo, yo):
        return lax.rem(z + zo % NZ, NZ) * NY + lax.rem(y + yo % NY, NY)

    def device(link):
        axis, d = link
        return (at(d, 0) if axis == "z" else at(0, d), ang)

    barrier = pltpu.get_barrier_semaphore()
    for link in (("z", 1), ("z", -1), ("y", 1), ("y", -1)):
        pl.semaphore_signal(barrier, inc=1, device_id=device(link), device_id_type=MESH)
    pl.semaphore_wait(barrier, 4)

    tasks = sum_tasks() + all_tasks()
    number = {t.key: i for i, t in enumerate(tasks)}
    by_key = {t.key: t for t in tasks}
    sums = schedule(sum_tasks(), LATENCY, RATE)
    alls = schedule(all_tasks(), LATENCY, RATE)

    a_rows, b_rows = pl.ds(SUM_A[0], SUM_A[1] - SUM_A[0]), pl.ds(SUM_B[0], SUM_B[1] - SUM_B[0])
    slot_of = {}
    for stage, ref in (("a1", ra1), ("a2", ra2), ("b1", rb1), ("b2", rb2)):
        keys = [t.key for t in tasks if t.key[0] == stage]
        for i, k in enumerate(keys):
            slot_of[k] = ref.at[i, pl.ds(0, by_key[k].rows)]

    def chain_of(n, piece, chain):
        return ring_steps(n, sign_of(piece))[chain]

    def origin(key):
        stage, piece, chain, s = key
        if stage in ("c1", "d1"):
            n = NY if stage == "c1" else NZ
            d, _ = chain_of(n, piece, chain)
            off = -d * (s - 1)
            lo, hi = halves(ALL_A if stage == "c1" else ALL_B)[piece]
            return (at(0, off) if stage == "c1" else at(off, 0)), pl.ds(lo, hi - lo)
        n = NZ if stage == "c2" else NY
        d, _ = chain_of(n, piece, chain)
        off = -d * (s - 1)
        lo, hi = ALL_A if stage == "c2" else ALL_B
        return (at(off, piece) if stage == "c2" else at(piece, off)), pl.ds(lo, hi - lo)

    def source(key):
        stage, piece, chain, s = key
        if stage in ("c1", "c2", "d1", "d2"):
            owner, rows = origin(key)
            ref = all_ref.at[owner, rows]
            return ref, ref
        dst = slot_of[key]
        if s > 1:
            return slot_of[(stage, piece, chain, s - 1)], dst
        return local(key), dst

    def local(key):
        stage, piece, chain, s = key
        if stage in ("a1", "b1"):
            n = NZ if stage == "a1" else NY
            d, steps = chain_of(n, piece, chain)
            off = d * (steps - s + 1)
            return p_ref.at[at(off, piece), a_rows] if stage == "a1" else p_ref.at[at(piece, off), b_rows]
        n = NY if stage == "a2" else NZ
        d, steps = chain_of(n, piece, chain)
        off = (d * (steps - s + 1)) % n
        span = SUM_A if stage == "a2" else SUM_B
        lo, hi = halves(span)[piece]
        first = ("a1" if stage == "a2" else "b1", off, 0, n_first(stage) // 2)
        return slot_of[first].at[pl.ds(lo - span[0], hi - lo)]

    def n_first(stage):
        return NZ if stage == "a2" else NY

    copies = {}

    def copy_of(key):
        if key not in copies:
            src, dst = source(key)
            i = number[key]
            copies[key] = pltpu.make_async_remote_copy(
                src_ref=src,
                dst_ref=dst,
                send_sem=send_sem.at[i],
                recv_sem=recv_sem.at[i],
                device_id=device(by_key[key].link),
                device_id_type=MESH,
            )
        return copies[key]

    received, sent, waited, finished = set(), {}, set(), set()

    def receive(key):
        if key not in received:
            received.add(key)
            copy_of(key).wait_recv()

    def finish(stage, off):
        if (stage, off) in finished:
            return
        finished.add((stage, off))
        n = NZ if stage == "a1" else NY
        one, two = (stage, off, 0, n // 2), (stage, off, 1, n // 2 - 1)
        receive(one)
        receive(two)
        mine = p_ref.at[at(0, off), a_rows] if stage == "a1" else p_ref.at[at(off, 0), b_rows]
        slot_of[one][...] = slot_of[one][...] + slot_of[two][...] + mine[...]

    def issue(key):
        stage, piece, chain, s = key
        task = by_key[key]
        queue = sent.setdefault(task.link, [])
        if len(queue) >= AHEAD:
            old = queue[-AHEAD]
            if old not in waited:
                waited.add(old)
                copy_of(old).wait_send()
        for k in task.needs:
            if stage in ("a2", "b2") and k[0] in ("a1", "b1"):
                finish(k[0], k[1])
            else:
                receive(k)
        if s > 1 and stage in ("a1", "a2", "b1", "b2"):
            ref = slot_of[(stage, piece, chain, s - 1)]
            ref[...] = ref[...] + local(key)[...]
        copy_of(key).start()
        queue.append(key)

    for key in sums:
        issue(key)
    for stage, span, n, n1 in (("a2", SUM_A, NY, NZ), ("b2", SUM_B, NZ, NY)):
        first = "a1" if stage == "a2" else "b1"
        finish(first, 0)
        for h, (lo, hi) in enumerate(halves(span)):
            one, two = (stage, h, 0, n // 2), (stage, h, 1, n // 2 - 1)
            receive(one)
            receive(two)
            mine = slot_of[(first, 0, 0, n1 // 2)].at[pl.ds(lo - span[0], hi - lo)]
            own[lo:hi, :] = slot_of[one][...] + slot_of[two][...] + mine[...]

    norms = [jnp.broadcast_to(own[OWN + h : OWN + h + 1, :], (128, 128)).T for h in range(2)]
    for b in range(4):
        for h in range(2):
            natural = pl.ds(b * BLK + h, 32, stride=2)
            mine = slice(b * BLK + 32 * h, b * BLK + 32 * h + 32)
            value = (meas_ref[natural, :] - own[mine, :]) / norms[h][32 * b : 32 * b + 32]
            resid_ref[natural, :] = value
            all_ref[at(0, 0), mine, :] = value

    for key in alls:
        issue(key)
    for t in tasks:
        receive(t.key)
    for t in tasks:
        if t.key not in waited:
            copy_of(t.key).wait_send()


def exchange(p, measured):
    tasks = sum_tasks() + all_tasks()
    count = {}
    for t in tasks:
        count[t.key[0]] = count.get(t.key[0], 0) + 1
    most = {k: max(t.rows for t in tasks if t.key[0] == k) for k in count}
    return pl.pallas_call(
        exchange_kernel,
        out_shape=(
            jax.ShapeDtypeStruct((OWN, S), jnp.float32),
            jax.ShapeDtypeStruct((NZ * NY, OWN, S), jnp.float32),
        ),
        in_specs=[VM, VM],
        out_specs=(VM, VM),
        scratch_shapes=[vmem(count[k], most[k], S) for k in ("a1", "a2", "b1", "b2")]
        + [
            vmem(CH, S),
            pltpu.SemaphoreType.DMA((len(tasks),)),
            pltpu.SemaphoreType.DMA((len(tasks),)),
        ],
        compiler_params=pltpu.CompilerParams(
            collective_id=1, has_side_effects=True, vmem_limit_bytes=24 * MIB
        ),
        cost_estimate=cost(50),
        name="sum_and_spread",
    )(p, measured)


UPD = ((0, 72), (72, 136))


def backward_kernel(
    code_ref, turned_ref, all_ref, col_ref, out_ref, hi_ref, lo_ref, run_ref, b_ref, sib, far_buf, near_buf, second_buf,
    send_sem, recv_sem,
):
    here = Ang()
    wait_for_others = here.meet(("twin", 1, -1))

    def split(o, _):
        rows = pl.ds(pl.multiple_of(o * 8, 8), 8)
        hi_ref[rows], lo_ref[rows] = split_bf16(all_ref[o].reshape(8, 32, S))
        return _

    lax.fori_loop(0, NZ * NY, split, 0, unroll=2)

    def pixel_block(g):
        return lax.shift_right_logical(code_ref[0, g * GRP], 16) & (QB - 1)

    def step(b, run):
        for i in range(BWD):
            g = b * BWD + i
            codes = [code_ref[0, g * GRP + j] for j in range(GRP)]
            hi, lo = turned_ref[g, :, :128], turned_ref[g, :, 128:]
            slots = [c & (RB - 1) for c in codes]

            def rays(ref):
                return [ref[slot * 2 + h] for h in range(2) for slot in slots]

            r_hi, r_lo = rays(hi_ref), rays(lo_ref)
            left = jnp.concatenate([hi[:BLK], hi[BLK:], lo[:BLK], lo[BLK:], hi[:BLK], hi[BLK:]], axis=1)
            right = jnp.concatenate(r_hi + r_hi + r_lo, axis=0)
            out = jnp.dot(left, right, preferred_element_type=jnp.float32)
            before = pixel_block(jnp.maximum(g - 1, 0))
            run = run * (before == pixel_block(g)).astype(jnp.float32) + out
            run_ref[g] = run
        return run

    lax.fori_loop(0, STEPS, step, jnp.zeros((BLK, S), jnp.float32))
    for q in range(QB):
        last = code_ref[0, NPOS_PAD + q]
        total = run_ref[jnp.maximum(last, 0)]
        b_ref[q // 2, q % 2 * BLK : q % 2 * BLK + BLK, :] = total * (last >= 0).astype(jnp.float32)
    for o in range(NA):
        b_ref[o, 128:136, :] = col_ref[o]

    wait_for_others()
    number = iter(range(10))

    def send(to, src, dst):
        i = next(number)
        copy = pltpu.make_async_remote_copy(
            src_ref=src,
            dst_ref=dst,
            send_sem=send_sem.at[i],
            recv_sem=recv_sem.at[i],
            device_id=here.device(to),
            device_id_type=MESH,
        )
        copy.start()
        return copy

    across = {dx: send("twin", b_ref.at[here.twin(dx)], sib.at[dx]) for dx in (2, 1, 3, 0)}

    def arrive(dx):
        across[dx].wait_recv()
        sib[dx] = sib[dx] + b_ref[here.index(dx)]

    def rows(h):
        return pl.ds(UPD[h][0], UPD[h][1] - UPD[h][0])

    def part(buf, h):
        return buf.at[h, pl.ds(0, UPD[h][1] - UPD[h][0])]

    arrive(2)
    far = [send(sign_of(h), sib.at[2, rows(h)], part(far_buf, h)) for h in range(2)]
    arrive(1)
    arrive(3)
    near = [send(-sign_of(h), sib.at[-sign_of(h) % NX, rows(h)], part(near_buf, h)) for h in range(2)]
    arrive(0)
    second = []
    for h in range(2):
        far[h].wait_recv()
        part(far_buf, h)[...] = part(far_buf, h)[...] + sib[sign_of(h) % NX, rows(h), :]
        second.append(send(sign_of(h), part(far_buf, h), part(second_buf, h)))
    totals = []
    for h in range(2):
        near[h].wait_recv()
        totals.append(sib[0, rows(h), :] + part(near_buf, h)[...])
    for h in range(2):
        second[h].wait_recv()
        totals[h] = totals[h] + part(second_buf, h)[...]
    total = jnp.concatenate(totals, axis=0)
    norm = jnp.broadcast_to(total[128:129], (128, 128)).T
    out_ref[...] = RELAX * total[:128] / norm
    for copy in [*across.values(), *far, *near, *second]:
        copy.wait_send()


def backward(code, turned, everyone, col):
    size = UPD[0][1]
    return pl.pallas_call(
        backward_kernel,
        out_shape=jax.ShapeDtypeStruct((128, S), jnp.float32),
        in_specs=[SM, VM, VM, VM],
        out_specs=VM,
        scratch_shapes=[
            vmem(RB * 2, 32, S, dtype=jnp.bfloat16),
            vmem(RB * 2, 32, S, dtype=jnp.bfloat16),
            vmem(STEPS * BWD, BLK, S),
            vmem(NA, 136, S),
            vmem(NX, 136, S),
            vmem(2, size, S),
            vmem(2, size, S),
            vmem(2, size, S),
            pltpu.SemaphoreType.DMA((10,)),
            pltpu.SemaphoreType.DMA((10,)),
        ],
        compiler_params=pltpu.CompilerParams(
            collective_id=2, has_side_effects=True, vmem_limit_bytes=32 * MIB
        ),
        cost_estimate=cost(17),
        name="backward_and_sum",
    )(code, turned, everyone, col)


def shards(tiles, tile_ray, tile_pix, tile_count, ray_slot, image, measured):
    rows = tiles[0, 0].reshape(SLOTS // 8, 8, 32, 128).transpose(0, 2, 1, 3).reshape(SLOTS * 32, 128)
    used_tiles = jnp.broadcast_to(tile_count[0], (RB,))
    index = jnp.concatenate([tile_ray[0, 0], tile_pix[0, 0], ray_slot[0], used_tiles])[None]
    img, code = gather_image(index, image)
    p, col, turned = forward(code, rows, img)
    own, everyone = exchange(p, measured[0])
    return (image + backward(code, turned, everyone, col), own[None])


def solution(mesh):
    in_specs = (
        P("pix", "ang", None, None),
        P("pix", "ang", None),
        P("pix", "ang", None),
        P("pix", "ang"),
        P("ang", None),
        P(("pix", "ang"), None),
        P("ang", "pix", None),
    )
    out_specs = (P(("pix", "ang"), None), P("ang", "pix", None))
    return jax.shard_map(shards, mesh=mesh, in_specs=in_specs, out_specs=out_specs, check_vma=False)
```

```python
import functools

import jax
import jax.numpy as jnp
from jax import lax
from jax.experimental import pallas as pl
from jax.experimental.pallas import tpu as pltpu
from jax.sharding import PartitionSpec as P

MESH = pl.DeviceIdType.MESH
BLK, S, SLOTS, RB, QB = 64, 128, 512, 128, 16
RELAX = 0.9
NZ, NY, NX, NA = 8, 4, 4, 8
GRP = 4
NPOS = SLOTS + QB * (GRP - 1)
NPOS_PAD = 640
LIST = NPOS_PAD + 128
BWD = 12
STEPS = NPOS // GRP // BWD + 1
OWN = 256
CH = OWN + 8
VM = pl.BlockSpec(memory_space=pltpu.VMEM)
SM = pl.BlockSpec(memory_space=pltpu.SMEM)
MIB = 1024 * 1024


def cost(us):
    return pl.CostEstimate(flops=int(us * 1.15e9), bytes_accessed=0, transcendentals=0)


def vmem(*shape, dtype=jnp.float32):
    return pltpu.VMEM(shape, dtype)


def split_bf16(x):
    hi = x.astype(jnp.bfloat16)
    return hi, (x - hi.astype(jnp.float32)).astype(jnp.bfloat16)


def sign_of(i):
    return 1 if i % 2 == 0 else -1


class Ang:
    def __init__(self):
        self.pix, me = lax.axis_index("pix"), lax.axis_index("ang")
        self.me, self.x, self.core = me, me // 2, lax.rem(me, 2)

    def index(self, dx):
        return lax.rem(self.x + dx % NX, NX) * 2 + self.core

    def twin(self, dx=0):
        return lax.rem(self.x + dx % NX, NX) * 2 + (1 - self.core)

    def device(self, to):
        if to == "twin":
            return (self.pix, self.twin())
        return (self.pix, self.twin(to // 2) if to % 2 == 0 else self.index(to))

    def meet(self, others):
        barrier = pltpu.get_barrier_semaphore()
        for to in others:
            pl.semaphore_signal(barrier, inc=1, device_id=self.device(to), device_id_type=MESH)
        return lambda: pl.semaphore_wait(barrier, len(others))


def sort_tiles(ray, pix, used_tiles, table):
    f32 = jnp.float32
    both = jnp.broadcast_to((pix * RB + ray).astype(f32), (128, SLOTS)).T.astype(jnp.int32)
    lane = lax.broadcasted_iota(jnp.int32, (SLOTS, 128), 1)
    t = lax.broadcasted_iota(jnp.int32, (SLOTS, 128), 0)
    q = lax.shift_right_logical(both, 7)
    mine = jnp.where((q == lane) & (t < used_tiles), 1.0, 0.0).astype(f32)
    slot = jnp.sum(jnp.where((both & (RB - 1)) == lane, table.astype(f32), 0.0), axis=1, keepdims=True)
    earlier = lax.broadcasted_iota(jnp.int32, (SLOTS, SLOTS), 1) < lax.broadcasted_iota(jnp.int32, (SLOTS, SLOTS), 0)
    earlier = jnp.where(earlier, 1.0, 0.0).astype(jnp.bfloat16)
    before = jnp.dot(earlier, mine.astype(jnp.bfloat16), preferred_element_type=f32)
    counts = jnp.sum(mine, axis=0, keepdims=True).astype(jnp.int32)
    groups = lax.shift_right_logical(counts + (GRP - 1), 2).astype(f32)
    left_of = lax.broadcasted_iota(jnp.int32, (128, 128), 0) < lax.broadcasted_iota(jnp.int32, (128, 128), 1)
    left_of = jnp.where(left_of, 1.0, 0.0).astype(jnp.bfloat16)
    first = jnp.dot(jnp.broadcast_to(groups, (8, 128)).astype(jnp.bfloat16), left_of, preferred_element_type=f32)
    place = jnp.sum(mine * (before + GRP * first[:1]), axis=1, keepdims=True)
    place = jnp.where(t < used_tiles, place, -1.0)
    code = ((1 << 20) + q * (1 << 16) + t * RB).astype(f32) + slot
    parts = []
    for c in range(NPOS_PAD // 128):
        at = (lax.broadcasted_iota(jnp.int32, (1, 128), 1) + c * 128).astype(f32)
        part = jnp.sum(jnp.where(place == at, code, 0.0), axis=0, keepdims=True)
        parts.append(jnp.where(at == NPOS_PAD - 1, jnp.sum(groups, axis=1, keepdims=True), part))
    parts.append(jnp.where(groups > 0.0, first[:1] + groups - 1.0, -1.0))
    return jnp.concatenate(parts, axis=1).astype(jnp.int32)


def gather_kernel(
    index_ref, img_ref, out_ref, code_ref, send_sem, recv_sem
):
    here = Ang()
    here.meet(("twin", 1, -1, 2, -2))()
    number = iter(range(13))

    def send(to, dx, half, src=None):
        lo, size = (0, 128) if half is None else (64 * half, 64)
        rows = out_ref.at[pl.ds(pl.multiple_of(here.index(dx) * 128 + lo, 64), size)]
        i = next(number)
        copy = pltpu.make_async_remote_copy(
            src_ref=rows if src is None else src.at[pl.ds(lo, size)],
            dst_ref=rows,
            send_sem=send_sem.at[i],
            recv_sem=recv_sem.at[i],
            device_id=here.device(to),
            device_id_type=MESH,
        )
        copy.start()
        return copy

    far = [send(sign_of(h), 0, h, img_ref) for h in range(2)]
    near = [send(-sign_of(h), 0, h, img_ref) for h in range(2)]
    across = [send("twin", 0, None, img_ref)]
    out_ref[pl.ds(pl.multiple_of(here.me * 128, 128), 128), :] = img_ref[...]
    ray, pix = index_ref[:, :SLOTS], index_ref[:, SLOTS : 2 * SLOTS]
    table, used_tiles = index_ref[:, 2 * SLOTS : 2 * SLOTS + RB], index_ref[:, 2 * SLOTS + RB :]
    code_ref[...] = sort_tiles(ray, pix, used_tiles, table)
    second = []
    for h in range(2):
        far[h].wait_recv()
        second += [send(sign_of(h), -sign_of(h), h), send(2 * sign_of(h), -sign_of(h), h)]
        across.append(send("twin", -sign_of(h), h))
    for h in range(2):
        near[h].wait_recv()
        across.append(send("twin", sign_of(h), h))
    across += second
    for copy in across:
        copy.wait_recv()
    for copy in far + near + across:
        copy.wait_send()


def gather_image(index, image):
    return pl.pallas_call(
        gather_kernel,
        out_shape=(
            jax.ShapeDtypeStruct((NA * 128, S), jnp.float32),
            jax.ShapeDtypeStruct((1, LIST), jnp.int32),
        ),
        in_specs=[VM, VM],
        out_specs=(VM, VM),
        scratch_shapes=[
            pltpu.SemaphoreType.DMA((13,)),
            pltpu.SemaphoreType.DMA((13,)),
        ],
        compiler_params=pltpu.CompilerParams(
            collective_id=0, has_side_effects=True, vmem_limit_bytes=24 * MIB
        ),
        cost_estimate=cost(8),
        name="gather_image",
    )(index, image)


def tile_rows(tiles_ref, code):
    t = lax.shift_right_logical(code, 7) & (SLOTS - 1)
    start = lax.shift_right_logical(t, 3) * 256 + (t & 7)
    used = lax.shift_right_logical(code, 20).astype(jnp.float32)
    return tiles_ref[pl.ds(start, 32, stride=8), :] * used


FWD = 12


def forward_kernel(code_ref, tiles_ref, img_ref, p_ref, col_ref, turned_ref, w_ref, rowacc, colacc):
    zero = jnp.zeros((BLK, S), jnp.bfloat16)

    def weights(q, _):
        hi, lo = split_bf16(img_ref[pl.ds(pl.multiple_of(q * BLK, BLK), BLK), :])
        both = [jnp.concatenate([jnp.concatenate([x, zero], 1), jnp.concatenate([zero, x], 1)], 0) for x in (hi, lo)]
        w_ref[q] = jnp.concatenate([both[0], both[0], both[1]], axis=0)
        return _

    lax.fori_loop(0, QB, weights, 0, unroll=4)
    rowacc[...] = jnp.zeros_like(rowacc)
    colacc[...] = jnp.zeros_like(colacc)

    def clear(o, _):
        p_ref[o] = jnp.zeros((CH, S), jnp.float32)
        return _

    lax.fori_loop(0, NZ * NY, clear, 0, unroll=4)

    def place(slot):
        rows = pl.ds(pl.multiple_of((slot & 3) * BLK, BLK), BLK)
        return lax.shift_right_logical(slot, 2), rows, slice(None)

    def read(slot):
        return p_ref[place(slot)]

    def write(slot, value):
        p_ref[place(slot)] = value

    def read_rows(slot):
        return rowacc[slot]

    def write_rows(slot, value):
        rowacc[slot] = value

    def step(b, _):
        for i in range(FWD):
            codes = [code_ref[0, (b * FWD + i) * GRP + j] for j in range(GRP)]
            q = lax.shift_right_logical(codes[0], 16) & (QB - 1)
            slots = [c & (RB - 1) for c in codes]
            tiles = [tile_rows(tiles_ref, c) for c in codes]
            hi, lo = split_bf16(jnp.concatenate(tiles, axis=0))
            turned_ref[b * FWD + i] = jnp.concatenate([hi.T, lo.T], axis=1)
            out = jnp.dot(jnp.concatenate([hi, lo, hi], axis=1), w_ref[q], preferred_element_type=jnp.float32)
            terms = [
                jnp.concatenate([out[32 * j : 32 * j + 32, h * S : h * S + S] for h in range(2)], axis=0)
                for j in range(GRP)
            ]
            for k, v in zip(slots, tiles):
                rowacc[k] += v
            colacc[q] += (tiles[0] + tiles[1]) + (tiles[2] + tiles[3])
            for k, v in zip(slots, terms):
                write(k, read(k) + v)
        return _

    lax.fori_loop(0, (code_ref[0, NPOS_PAD - 1] + FWD - 1) // FWD, step, 0)

    pick = lax.broadcasted_iota(jnp.int32, (8, 128), 0) == (lax.broadcasted_iota(jnp.int32, (8, 128), 1) // BLK)
    pick = pick.astype(jnp.float32).astype(jnp.bfloat16)

    def row_sums(o, _):
        hi, lo = split_bf16(rowacc[pl.ds(o * 4, 4)].reshape(128, 128))
        dims = (((1,), (1,)), ((), ()))
        sums = lax.dot_general(pick, hi, dims, preferred_element_type=jnp.float32)
        sums += lax.dot_general(pick, lo, dims, preferred_element_type=jnp.float32)
        p_ref[o, OWN:CH, :] = sums
        return _

    lax.fori_loop(0, NZ * NY, row_sums, 0, unroll=16)
    low = lax.broadcasted_iota(jnp.int32, (1, 128), 1) < BLK
    for o in range(NA):
        a = jnp.sum(colacc[2 * o], axis=0, keepdims=True)
        b = jnp.sum(colacc[2 * o + 1], axis=0, keepdims=True)
        a = a + pltpu.roll(a, BLK, 1)
        b = b + pltpu.roll(b, BLK, 1)
        col_ref[o] = jnp.broadcast_to(jnp.where(low, a, b), (8, 128))


def forward(code, tiles, img):
    return pl.pallas_call(
        forward_kernel,
        out_shape=(
            jax.ShapeDtypeStruct((NZ * NY, CH, S), jnp.float32),
            jax.ShapeDtypeStruct((NA, 8, 128), jnp.float32),
            jax.ShapeDtypeStruct((STEPS * BWD, 128, 2 * 128), jnp.bfloat16),
        ),
        in_specs=[SM, VM, VM],
        out_specs=(VM, VM, VM),
        scratch_shapes=[
            vmem(QB, 6 * BLK, 2 * S, dtype=jnp.bfloat16),
            vmem(RB, 32, 128),
            vmem(QB, 32, 128),
        ],
        compiler_params=pltpu.CompilerParams(vmem_limit_bytes=32 * MIB),
        cost_estimate=cost(13),
        name="forward_tiles",
    )(code, tiles, img)


def ring_steps(n, sign):
    return ((sign, n // 2), (-sign, n // 2 - 1))


class Task:
    def __init__(self, key, link, rows, needs):
        self.key, self.link, self.rows, self.needs = key, link, rows, needs


def schedule(tasks, latency, rate):
    by_key = {t.key: t for t in tasks}
    follow = {t.key: [] for t in tasks}
    for t in tasks:
        for k in t.needs:
            follow[k].append(t.key)
    tail = {}

    def tail_of(k):
        if k not in tail:
            t = by_key[k]
            tail[k] = t.rows / rate + latency + max([tail_of(f) for f in follow[k]], default=0.0)
        return tail[k]

    left, done, free, order = list(tasks), {}, {}, []
    while left:
        best = None
        for t in left:
            if all(k in done for k in t.needs):
                at = max([done[k] for k in t.needs], default=0.0)
                start = max(at, free.get(t.link, 0.0))
                rank = (start, -tail_of(t.key))
                if best is None or rank < best[0]:
                    best = (rank, t)
        (start, _), t = best
        free[t.link] = start + t.rows / rate
        done[t.key] = start + t.rows / rate + latency
        order.append((start, t.key))
        left.remove(t)
    return [k for _, k in sorted(order, key=lambda e: e[0])]


RATE = 95.0
LATENCY = 2.5

SUM_A = (0, 104)
SUM_B = (104, 264)
ALL_A = (0, 104)
ALL_B = (104, 256)


def halves(span):
    lo, hi = span
    mid = lo + ((hi - lo) // 2 + 7) // 8 * 8
    return ((lo, mid), (mid, hi))


def sum_tasks():
    tasks = []

    def ring(stage, n, axis, piece, sign, rows, local_needs):
        for chain, (d, steps) in enumerate(ring_steps(n, sign)):
            for s in range(1, steps + 1):
                off = (d * (steps - s + 1)) % n
                needs = [(stage, piece, chain, s - 1)] if s > 1 else []
                tasks.append(Task((stage, piece, chain, s), (axis, d), rows, needs + local_needs(off)))

    def last(stage, n, piece):
        return [(stage, piece, 0, n // 2), (stage, piece, 1, n // 2 - 1)]

    for yo in range(NY):
        ring("a1", NZ, "z", yo, sign_of(yo), SUM_A[1] - SUM_A[0], lambda off: [])
    for h, (lo, hi) in enumerate(halves(SUM_A)):
        ring("a2", NY, "y", h, sign_of(h), hi - lo, lambda off: last("a1", NZ, off))
    for zo in range(NZ):
        ring("b1", NY, "y", zo, sign_of(zo), SUM_B[1] - SUM_B[0], lambda off: [])
    for h, (lo, hi) in enumerate(halves(SUM_B)):
        ring("b2", NZ, "z", h, sign_of(h), hi - lo, lambda off: last("b1", NY, off))
    return tasks


def all_tasks():
    tasks = []

    def ring(stage, n, axis, piece, sign, rows, first_needs):
        for chain, (d, steps) in enumerate(ring_steps(n, sign)):
            for s in range(1, steps + 1):
                needs = [(stage, piece, chain, s - 1)] if s > 1 else first_needs
                tasks.append(Task((stage, piece, chain, s), (axis, d), rows, needs))

    def arrives(stage, n, piece, sign, off):
        for chain, (d, steps) in enumerate(ring_steps(n, sign)):
            for s in range(1, steps + 1):
                if (-d * s) % n == off:
                    return (stage, piece, chain, s)

    for h, (lo, hi) in enumerate(halves(ALL_A)):
        ring("c1", NY, "y", h, sign_of(h), hi - lo, [])
    for yo in range(NY):
        needs = [arrives("c1", NY, h, sign_of(h), yo) for h in range(2)] if yo else []
        ring("c2", NZ, "z", yo, sign_of(yo), ALL_A[1] - ALL_A[0], needs)
    for h, (lo, hi) in enumerate(halves(ALL_B)):
        ring("d1", NZ, "z", h, sign_of(h), hi - lo, [])
    for zo in range(NZ):
        needs = [arrives("d1", NZ, h, sign_of(h), zo) for h in range(2)] if zo else []
        ring("d2", NY, "y", zo, sign_of(zo), ALL_B[1] - ALL_B[0], needs)
    return tasks


AHEAD = 3


def exchange_kernel(
    p_ref, meas_ref, resid_ref, hi_ref, lo_ref, all_ref, ra1, ra2, rb1, rb2, own, send_sem, recv_sem
):
    pix, ang = lax.axis_index("pix"), lax.axis_index("ang")
    z, y = pix // NY, lax.rem(pix, NY)

    def at(zo, yo):
        return lax.rem(z + zo % NZ, NZ) * NY + lax.rem(y + yo % NY, NY)

    def device(link):
        axis, d = link
        return (at(d, 0) if axis == "z" else at(0, d), ang)

    barrier = pltpu.get_barrier_semaphore()
    for link in (("z", 1), ("z", -1), ("y", 1), ("y", -1)):
        pl.semaphore_signal(barrier, inc=1, device_id=device(link), device_id_type=MESH)
    pl.semaphore_wait(barrier, 4)

    tasks = sum_tasks() + all_tasks()
    number = {t.key: i for i, t in enumerate(tasks)}
    by_key = {t.key: t for t in tasks}
    sums = schedule(sum_tasks(), LATENCY, RATE)
    alls = schedule(all_tasks(), LATENCY, RATE)

    a_rows, b_rows = pl.ds(SUM_A[0], SUM_A[1] - SUM_A[0]), pl.ds(SUM_B[0], SUM_B[1] - SUM_B[0])
    slot_of = {}
    for stage, ref in (("a1", ra1), ("a2", ra2), ("b1", rb1), ("b2", rb2)):
        keys = [t.key for t in tasks if t.key[0] == stage]
        for i, k in enumerate(keys):
            slot_of[k] = ref.at[i, pl.ds(0, by_key[k].rows)]

    def chain_of(n, piece, chain):
        return ring_steps(n, sign_of(piece))[chain]

    def origin(key):
        stage, piece, chain, s = key
        if stage in ("c1", "d1"):
            n = NY if stage == "c1" else NZ
            d, _ = chain_of(n, piece, chain)
            off = -d * (s - 1)
            lo, hi = halves(ALL_A if stage == "c1" else ALL_B)[piece]
            return (at(0, off) if stage == "c1" else at(off, 0)), pl.ds(lo, hi - lo)
        n = NZ if stage == "c2" else NY
        d, _ = chain_of(n, piece, chain)
        off = -d * (s - 1)
        lo, hi = ALL_A if stage == "c2" else ALL_B
        return (at(off, piece) if stage == "c2" else at(piece, off)), pl.ds(lo, hi - lo)

    def source(key):
        stage, piece, chain, s = key
        if stage in ("c1", "c2", "d1", "d2"):
            owner, rows = origin(key)
            ref = all_ref.at[owner, rows]
            return ref, ref
        dst = slot_of[key]
        if s > 1:
            return slot_of[(stage, piece, chain, s - 1)], dst
        return local(key), dst

    def local(key):
        stage, piece, chain, s = key
        if stage in ("a1", "b1"):
            n = NZ if stage == "a1" else NY
            d, steps = chain_of(n, piece, chain)
            off = d * (steps - s + 1)
            return p_ref.at[at(off, piece), a_rows] if stage == "a1" else p_ref.at[at(piece, off), b_rows]
        n = NY if stage == "a2" else NZ
        d, steps = chain_of(n, piece, chain)
        off = (d * (steps - s + 1)) % n
        span = SUM_A if stage == "a2" else SUM_B
        lo, hi = halves(span)[piece]
        first = ("a1" if stage == "a2" else "b1", off, 0, n_first(stage) // 2)
        return slot_of[first].at[pl.ds(lo - span[0], hi - lo)]

    def n_first(stage):
        return NZ if stage == "a2" else NY

    copies = {}

    def copy_of(key):
        if key not in copies:
            src, dst = source(key)
            i = number[key]
            copies[key] = pltpu.make_async_remote_copy(
                src_ref=src,
                dst_ref=dst,
                send_sem=send_sem.at[i],
                recv_sem=recv_sem.at[i],
                device_id=device(by_key[key].link),
                device_id_type=MESH,
            )
        return copies[key]

    received, sent, waited, finished = set(), {}, set(), set()

    def receive(key):
        if key not in received:
            received.add(key)
            copy_of(key).wait_recv()

    def finish(stage, off):
        if (stage, off) in finished:
            return
        finished.add((stage, off))
        n = NZ if stage == "a1" else NY
        one, two = (stage, off, 0, n // 2), (stage, off, 1, n // 2 - 1)
        receive(one)
        receive(two)
        mine = p_ref.at[at(0, off), a_rows] if stage == "a1" else p_ref.at[at(off, 0), b_rows]
        slot_of[one][...] = slot_of[one][...] + slot_of[two][...] + mine[...]

    def issue(key):
        stage, piece, chain, s = key
        task = by_key[key]
        queue = sent.setdefault(task.link, [])
        if len(queue) >= AHEAD:
            old = queue[-AHEAD]
            if old not in waited:
                waited.add(old)
                copy_of(old).wait_send()
        for k in task.needs:
            if stage in ("a2", "b2") and k[0] in ("a1", "b1"):
                finish(k[0], k[1])
            else:
                receive(k)
        if s > 1 and stage in ("a1", "a2", "b1", "b2"):
            ref = slot_of[(stage, piece, chain, s - 1)]
            ref[...] = ref[...] + local(key)[...]
        copy_of(key).start()
        queue.append(key)

    for key in sums:
        issue(key)
    for stage, span, n, n1 in (("a2", SUM_A, NY, NZ), ("b2", SUM_B, NZ, NY)):
        first = "a1" if stage == "a2" else "b1"
        finish(first, 0)
        for h, (lo, hi) in enumerate(halves(span)):
            one, two = (stage, h, 0, n // 2), (stage, h, 1, n // 2 - 1)
            receive(one)
            receive(two)
            mine = slot_of[(first, 0, 0, n1 // 2)].at[pl.ds(lo - span[0], hi - lo)]
            own[lo:hi, :] = slot_of[one][...] + slot_of[two][...] + mine[...]

    norms = [jnp.broadcast_to(own[OWN + h : OWN + h + 1, :], (128, 128)).T for h in range(2)]
    for b in range(4):
        for h in range(2):
            natural = pl.ds(b * BLK + h, 32, stride=2)
            mine = slice(b * BLK + 32 * h, b * BLK + 32 * h + 32)
            value = (meas_ref[natural, :] - own[mine, :]) / norms[h][32 * b : 32 * b + 32]
            resid_ref[natural, :] = value
            all_ref[at(0, 0), mine, :] = value

    def place(key):
        stage, piece, chain, s = key
        d, _ = chain_of(NY if stage in ("c1", "d2") else NZ, piece, chain)
        off = -d * s
        if stage == "c1":
            return 0, off % NY
        if stage == "d1":
            return off % NZ, 0
        return (off % NZ, piece) if stage == "c2" else (piece, off % NY)

    parts = {}
    for key in alls:
        parts.setdefault(place(key), []).append(key)

    def split(where):
        o = at(*where)
        rows = pl.ds(pl.multiple_of(o * 8, 8), 8)
        hi_ref[rows], lo_ref[rows] = split_bf16(all_ref[o].reshape(8, 32, S))

    def split_whole():
        for where in list(parts):
            if all(k in received for k in parts[where]):
                del parts[where]
                split(where)

    for i, key in enumerate(alls):
        issue(key)
        if i == 8:
            split((0, 0))
        split_whole()
    for key in alls:
        receive(key)
        split_whole()
    for t in tasks:
        receive(t.key)
    for t in tasks:
        if t.key not in waited:
            copy_of(t.key).wait_send()


def exchange(p, measured):
    tasks = sum_tasks() + all_tasks()
    count = {}
    for t in tasks:
        count[t.key[0]] = count.get(t.key[0], 0) + 1
    most = {k: max(t.rows for t in tasks if t.key[0] == k) for k in count}
    return pl.pallas_call(
        exchange_kernel,
        out_shape=(
            jax.ShapeDtypeStruct((OWN, S), jnp.float32),
            jax.ShapeDtypeStruct((RB * 2, 32, S), jnp.bfloat16),
            jax.ShapeDtypeStruct((RB * 2, 32, S), jnp.bfloat16),
        ),
        in_specs=[VM, VM],
        out_specs=(VM, VM, VM),
        scratch_shapes=[vmem(NZ * NY, OWN, S)]
        + [vmem(count[k], most[k], S) for k in ("a1", "a2", "b1", "b2")]
        + [
            vmem(CH, S),
            pltpu.SemaphoreType.DMA((len(tasks),)),
            pltpu.SemaphoreType.DMA((len(tasks),)),
        ],
        compiler_params=pltpu.CompilerParams(
            collective_id=1, has_side_effects=True, vmem_limit_bytes=24 * MIB
        ),
        cost_estimate=cost(50),
        name="sum_and_spread",
    )(p, measured)


UPD = ((0, 72), (72, 136))


def backward_kernel(
    code_ref, turned_ref, hi_ref, lo_ref, col_ref, out_ref, run_ref, b_ref, sib, far_buf, near_buf, second_buf,
    send_sem, recv_sem,
):
    here = Ang()
    wait_for_others = here.meet(("twin", 1, -1))

    def pixel_block(g):
        return lax.shift_right_logical(code_ref[0, g * GRP], 16) & (QB - 1)

    def step(b, run):
        for i in range(BWD):
            g = b * BWD + i
            codes = [code_ref[0, g * GRP + j] for j in range(GRP)]
            hi, lo = turned_ref[g, :, :128], turned_ref[g, :, 128:]
            slots = [c & (RB - 1) for c in codes]

            def rays(ref):
                return [ref[slot * 2 + h] for h in range(2) for slot in slots]

            r_hi, r_lo = rays(hi_ref), rays(lo_ref)
            left = jnp.concatenate([hi[:BLK], hi[BLK:], lo[:BLK], lo[BLK:], hi[:BLK], hi[BLK:]], axis=1)
            right = jnp.concatenate(r_hi + r_hi + r_lo, axis=0)
            out = jnp.dot(left, right, preferred_element_type=jnp.float32)
            before = pixel_block(jnp.maximum(g - 1, 0))
            run = run * (before == pixel_block(g)).astype(jnp.float32) + out
            run_ref[g] = run
        return run

    lax.fori_loop(0, STEPS, step, jnp.zeros((BLK, S), jnp.float32))
    for q in range(QB):
        last = code_ref[0, NPOS_PAD + q]
        total = run_ref[jnp.maximum(last, 0)]
        b_ref[q // 2, q % 2 * BLK : q % 2 * BLK + BLK, :] = total * (last >= 0).astype(jnp.float32)
    for o in range(NA):
        b_ref[o, 128:136, :] = col_ref[o]

    wait_for_others()
    number = iter(range(10))

    def send(to, src, dst):
        i = next(number)
        copy = pltpu.make_async_remote_copy(
            src_ref=src,
            dst_ref=dst,
            send_sem=send_sem.at[i],
            recv_sem=recv_sem.at[i],
            device_id=here.device(to),
            device_id_type=MESH,
        )
        copy.start()
        return copy

    across = {dx: send("twin", b_ref.at[here.twin(dx)], sib.at[dx]) for dx in (2, 1, 3, 0)}

    def arrive(dx):
        across[dx].wait_recv()
        sib[dx] = sib[dx] + b_ref[here.index(dx)]

    def rows(h):
        return pl.ds(UPD[h][0], UPD[h][1] - UPD[h][0])

    def part(buf, h):
        return buf.at[h, pl.ds(0, UPD[h][1] - UPD[h][0])]

    arrive(2)
    far = [send(sign_of(h), sib.at[2, rows(h)], part(far_buf, h)) for h in range(2)]
    arrive(1)
    arrive(3)
    near = [send(-sign_of(h), sib.at[-sign_of(h) % NX, rows(h)], part(near_buf, h)) for h in range(2)]
    arrive(0)
    second = []
    for h in range(2):
        far[h].wait_recv()
        part(far_buf, h)[...] = part(far_buf, h)[...] + sib[sign_of(h) % NX, rows(h), :]
        second.append(send(sign_of(h), part(far_buf, h), part(second_buf, h)))
    totals = []
    for h in range(2):
        near[h].wait_recv()
        totals.append(sib[0, rows(h), :] + part(near_buf, h)[...])
    for h in range(2):
        second[h].wait_recv()
        totals[h] = totals[h] + part(second_buf, h)[...]
    total = jnp.concatenate(totals, axis=0)
    norm = jnp.broadcast_to(total[128:129], (128, 128)).T
    out_ref[...] = RELAX * total[:128] / norm
    for copy in [*across.values(), *far, *near, *second]:
        copy.wait_send()


def backward(code, turned, high, low, col):
    size = UPD[0][1]
    return pl.pallas_call(
        backward_kernel,
        out_shape=jax.ShapeDtypeStruct((128, S), jnp.float32),
        in_specs=[SM, VM, VM, VM, VM],
        out_specs=VM,
        scratch_shapes=[
            vmem(STEPS * BWD, BLK, S),
            vmem(NA, 136, S),
            vmem(NX, 136, S),
            vmem(2, size, S),
            vmem(2, size, S),
            vmem(2, size, S),
            pltpu.SemaphoreType.DMA((10,)),
            pltpu.SemaphoreType.DMA((10,)),
        ],
        compiler_params=pltpu.CompilerParams(
            collective_id=2, has_side_effects=True, vmem_limit_bytes=32 * MIB
        ),
        cost_estimate=cost(17),
        name="backward_and_sum",
    )(code, turned, high, low, col)


def shards(tiles, tile_ray, tile_pix, tile_count, ray_slot, image, measured):
    rows = tiles[0, 0].reshape(SLOTS // 8, 8, 32, 128).transpose(0, 2, 1, 3).reshape(SLOTS * 32, 128)
    used_tiles = jnp.broadcast_to(tile_count[0], (RB,))
    index = jnp.concatenate([tile_ray[0, 0], tile_pix[0, 0], ray_slot[0], used_tiles])[None]
    img, code = gather_image(index, image)
    p, col, turned = forward(code, rows, img)
    own, high, low = exchange(p, measured[0])
    return (image + backward(code, turned, high, low, col), own[None])


def solution(mesh):
    in_specs = (
        P("pix", "ang", None, None),
        P("pix", "ang", None),
        P("pix", "ang", None),
        P("pix", "ang"),
        P("ang", None),
        P(("pix", "ang"), None),
        P("ang", "pix", None),
    )
    out_specs = (P(("pix", "ang"), None), P("ang", "pix", None))
    return jax.shard_map(shards, mesh=mesh, in_specs=in_specs, out_specs=out_specs, check_vma=False)
```

```python
import functools

import jax
import jax.numpy as jnp
from jax import lax
from jax.experimental import pallas as pl
from jax.experimental.pallas import tpu as pltpu
from jax.sharding import PartitionSpec as P

MESH = pl.DeviceIdType.MESH
BLK, S, SLOTS, RB, QB = 64, 128, 512, 128, 16
RELAX = 0.9
NZ, NY, NX, NA = 8, 4, 4, 8
GRP = 4
NPOS = SLOTS + QB * (GRP - 1)
NPOS_PAD = 640
LIST = NPOS_PAD + 128
BWD = 12
STEPS = NPOS // GRP // BWD + 1
OWN = 256
CH = OWN + 8
VM = pl.BlockSpec(memory_space=pltpu.VMEM)
SM = pl.BlockSpec(memory_space=pltpu.SMEM)
MIB = 1024 * 1024


def cost(us):
    return pl.CostEstimate(flops=int(us * 1.15e9), bytes_accessed=0, transcendentals=0)


def vmem(*shape, dtype=jnp.float32):
    return pltpu.VMEM(shape, dtype)


def split_bf16(x):
    hi = x.astype(jnp.bfloat16)
    return hi, (x - hi.astype(jnp.float32)).astype(jnp.bfloat16)


def sign_of(i):
    return 1 if i % 2 == 0 else -1


class Ang:
    def __init__(self):
        self.pix, me = lax.axis_index("pix"), lax.axis_index("ang")
        self.me, self.x, self.core = me, me // 2, lax.rem(me, 2)

    def index(self, dx):
        return lax.rem(self.x + dx % NX, NX) * 2 + self.core

    def twin(self, dx=0):
        return lax.rem(self.x + dx % NX, NX) * 2 + (1 - self.core)

    def device(self, to):
        if to == "twin":
            return (self.pix, self.twin())
        return (self.pix, self.twin(to // 2) if to % 2 == 0 else self.index(to))

    def meet(self, others):
        barrier = pltpu.get_barrier_semaphore()
        for to in others:
            pl.semaphore_signal(barrier, inc=1, device_id=self.device(to), device_id_type=MESH)
        return lambda: pl.semaphore_wait(barrier, len(others))


def sort_tiles(ray, pix, used_tiles, table):
    f32 = jnp.float32
    both = jnp.broadcast_to((pix * RB + ray).astype(f32), (128, SLOTS)).T.astype(jnp.int32)
    lane = lax.broadcasted_iota(jnp.int32, (SLOTS, 128), 1)
    t = lax.broadcasted_iota(jnp.int32, (SLOTS, 128), 0)
    q = lax.shift_right_logical(both, 7)
    mine = jnp.where((q == lane) & (t < used_tiles), 1.0, 0.0).astype(f32)
    slot = jnp.sum(jnp.where((both & (RB - 1)) == lane, table.astype(f32), 0.0), axis=1, keepdims=True)
    earlier = lax.broadcasted_iota(jnp.int32, (SLOTS, SLOTS), 1) < lax.broadcasted_iota(jnp.int32, (SLOTS, SLOTS), 0)
    earlier = jnp.where(earlier, 1.0, 0.0).astype(jnp.bfloat16)
    before = jnp.dot(earlier, mine.astype(jnp.bfloat16), preferred_element_type=f32)
    counts = jnp.sum(mine, axis=0, keepdims=True).astype(jnp.int32)
    groups = lax.shift_right_logical(counts + (GRP - 1), 2).astype(f32)
    left_of = lax.broadcasted_iota(jnp.int32, (128, 128), 0) < lax.broadcasted_iota(jnp.int32, (128, 128), 1)
    left_of = jnp.where(left_of, 1.0, 0.0).astype(jnp.bfloat16)
    first = jnp.dot(jnp.broadcast_to(groups, (8, 128)).astype(jnp.bfloat16), left_of, preferred_element_type=f32)
    place = jnp.sum(mine * (before + GRP * first[:1]), axis=1, keepdims=True)
    place = jnp.where(t < used_tiles, place, -1.0)
    code = ((1 << 20) + q * (1 << 16) + t * RB).astype(f32) + slot
    parts = []
    for c in range(NPOS_PAD // 128):
        at = (lax.broadcasted_iota(jnp.int32, (1, 128), 1) + c * 128).astype(f32)
        part = jnp.sum(jnp.where(place == at, code, 0.0), axis=0, keepdims=True)
        parts.append(jnp.where(at == NPOS_PAD - 1, jnp.sum(groups, axis=1, keepdims=True), part))
    parts.append(jnp.where(groups > 0.0, first[:1] + groups - 1.0, -1.0))
    return jnp.concatenate(parts, axis=1).astype(jnp.int32)


def gather_kernel(
    index_ref, img_ref, out_ref, code_ref, send_sem, recv_sem
):
    here = Ang()
    here.meet(("twin", 1, -1, 2, -2))()
    number = iter(range(13))

    def send(to, dx, half, src=None):
        lo, size = (0, 128) if half is None else (64 * half, 64)
        rows = out_ref.at[pl.ds(pl.multiple_of(here.index(dx) * 128 + lo, 64), size)]
        i = next(number)
        copy = pltpu.make_async_remote_copy(
            src_ref=rows if src is None else src.at[pl.ds(lo, size)],
            dst_ref=rows,
            send_sem=send_sem.at[i],
            recv_sem=recv_sem.at[i],
            device_id=here.device(to),
            device_id_type=MESH,
        )
        copy.start()
        return copy

    far = [send(sign_of(h), 0, h, img_ref) for h in range(2)]
    near = [send(-sign_of(h), 0, h, img_ref) for h in range(2)]
    across = [send("twin", 0, None, img_ref)]
    out_ref[pl.ds(pl.multiple_of(here.me * 128, 128), 128), :] = img_ref[...]
    ray, pix = index_ref[:, :SLOTS], index_ref[:, SLOTS : 2 * SLOTS]
    table, used_tiles = index_ref[:, 2 * SLOTS : 2 * SLOTS + RB], index_ref[:, 2 * SLOTS + RB :]
    code_ref[...] = sort_tiles(ray, pix, used_tiles, table)
    second = []
    for h in range(2):
        far[h].wait_recv()
        second += [send(sign_of(h), -sign_of(h), h), send(2 * sign_of(h), -sign_of(h), h)]
        across.append(send("twin", -sign_of(h), h))
    for h in range(2):
        near[h].wait_recv()
        across.append(send("twin", sign_of(h), h))
    across += second
    for copy in across:
        copy.wait_recv()
    for copy in far + near + across:
        copy.wait_send()


def gather_image(index, image):
    return pl.pallas_call(
        gather_kernel,
        out_shape=(
            jax.ShapeDtypeStruct((NA * 128, S), jnp.float32),
            jax.ShapeDtypeStruct((1, LIST), jnp.int32),
        ),
        in_specs=[VM, VM],
        out_specs=(VM, VM),
        scratch_shapes=[
            pltpu.SemaphoreType.DMA((13,)),
            pltpu.SemaphoreType.DMA((13,)),
        ],
        compiler_params=pltpu.CompilerParams(
            collective_id=0, has_side_effects=True, vmem_limit_bytes=24 * MIB
        ),
        cost_estimate=cost(8),
        name="gather_image",
    )(index, image)


def tile_rows(tiles_ref, code):
    t = lax.shift_right_logical(code, 7) & (SLOTS - 1)
    start = lax.shift_right_logical(t, 3) * 256 + (t & 7)
    used = lax.shift_right_logical(code, 20).astype(jnp.float32)
    return tiles_ref[pl.ds(start, 32, stride=8), :] * used


FWD = 12


def forward_kernel(code_ref, tiles_ref, img_ref, p_ref, col_ref, turned_ref, w_ref, rowacc, colacc):
    zero = jnp.zeros((BLK, S), jnp.bfloat16)

    def weights(q, _):
        hi, lo = split_bf16(img_ref[pl.ds(pl.multiple_of(q * BLK, BLK), BLK), :])
        both = [jnp.concatenate([jnp.concatenate([x, zero], 1), jnp.concatenate([zero, x], 1)], 0) for x in (hi, lo)]
        w_ref[q] = jnp.concatenate([both[0], both[0], both[1]], axis=0)
        return _

    lax.fori_loop(0, QB, weights, 0, unroll=4)
    rowacc[...] = jnp.zeros_like(rowacc)
    colacc[...] = jnp.zeros_like(colacc)

    def clear(o, _):
        p_ref[o] = jnp.zeros((CH, S), jnp.float32)
        return _

    lax.fori_loop(0, NZ * NY, clear, 0, unroll=4)

    def place(slot):
        rows = pl.ds(pl.multiple_of((slot & 3) * BLK, BLK), BLK)
        return lax.shift_right_logical(slot, 2), rows, slice(None)

    def read(slot):
        return p_ref[place(slot)]

    def write(slot, value):
        p_ref[place(slot)] = value

    def read_rows(slot):
        return rowacc[slot]

    def write_rows(slot, value):
        rowacc[slot] = value

    def step(b, _):
        for i in range(FWD):
            codes = [code_ref[0, (b * FWD + i) * GRP + j] for j in range(GRP)]
            q = lax.shift_right_logical(codes[0], 16) & (QB - 1)
            slots = [c & (RB - 1) for c in codes]
            tiles = [tile_rows(tiles_ref, c) for c in codes]
            hi, lo = split_bf16(jnp.concatenate(tiles, axis=0))
            turned_ref[b * FWD + i] = jnp.concatenate([hi.T, lo.T], axis=1)
            out = jnp.dot(jnp.concatenate([hi, lo, hi], axis=1), w_ref[q], preferred_element_type=jnp.float32)
            terms = [
                jnp.concatenate([out[32 * j : 32 * j + 32, h * S : h * S + S] for h in range(2)], axis=0)
                for j in range(GRP)
            ]
            for k, v in zip(slots, tiles):
                rowacc[k] += v
            colacc[q] += (tiles[0] + tiles[1]) + (tiles[2] + tiles[3])
            for k, v in zip(slots, terms):
                write(k, read(k) + v)
        return _

    lax.fori_loop(0, (code_ref[0, NPOS_PAD - 1] + FWD - 1) // FWD, step, 0)

    lane = lax.broadcasted_iota(jnp.int32, (8, 256), 1)
    pick = lax.broadcasted_iota(jnp.int32, (8, 256), 0) == (lane & 127) // BLK
    pick = pick.astype(jnp.float32).astype(jnp.bfloat16)

    def row_sums(o, _):
        both = jnp.concatenate(split_bf16(rowacc[pl.ds(o * 8, 8)].reshape(256, 128)), axis=1)
        sums = lax.dot_general(pick, both, (((1,), (1,)), ((), ())), preferred_element_type=jnp.float32)
        p_ref[2 * o, OWN:CH, :] = sums[:, :128]
        p_ref[2 * o + 1, OWN:CH, :] = sums[:, 128:]
        return _

    lax.fori_loop(0, NZ * NY // 2, row_sums, 0, unroll=8)
    low = lax.broadcasted_iota(jnp.int32, (1, 128), 1) < BLK
    for o in range(NA):
        a = jnp.sum(colacc[2 * o], axis=0, keepdims=True)
        b = jnp.sum(colacc[2 * o + 1], axis=0, keepdims=True)
        a = a + pltpu.roll(a, BLK, 1)
        b = b + pltpu.roll(b, BLK, 1)
        col_ref[o] = jnp.broadcast_to(jnp.where(low, a, b), (8, 128))


def forward(code, tiles, img):
    return pl.pallas_call(
        forward_kernel,
        out_shape=(
            jax.ShapeDtypeStruct((NZ * NY, CH, S), jnp.float32),
            jax.ShapeDtypeStruct((NA, 8, 128), jnp.float32),
            jax.ShapeDtypeStruct((STEPS * BWD, 128, 2 * 128), jnp.bfloat16),
        ),
        in_specs=[SM, VM, VM],
        out_specs=(VM, VM, VM),
        scratch_shapes=[
            vmem(QB, 6 * BLK, 2 * S, dtype=jnp.bfloat16),
            vmem(RB, 32, 128),
            vmem(QB, 32, 128),
        ],
        compiler_params=pltpu.CompilerParams(vmem_limit_bytes=32 * MIB),
        cost_estimate=cost(13),
        name="forward_tiles",
    )(code, tiles, img)


def ring_steps(n, sign):
    return ((sign, n // 2), (-sign, n // 2 - 1))


class Task:
    def __init__(self, key, link, rows, needs):
        self.key, self.link, self.rows, self.needs = key, link, rows, needs


def schedule(tasks, latency, rate):
    by_key = {t.key: t for t in tasks}
    follow = {t.key: [] for t in tasks}
    for t in tasks:
        for k in t.needs:
            follow[k].append(t.key)
    tail = {}

    def tail_of(k):
        if k not in tail:
            t = by_key[k]
            tail[k] = t.rows / rate + latency + max([tail_of(f) for f in follow[k]], default=0.0)
        return tail[k]

    left, done, free, order = list(tasks), {}, {}, []
    while left:
        best = None
        for t in left:
            if all(k in done for k in t.needs):
                at = max([done[k] for k in t.needs], default=0.0)
                start = max(at, free.get(t.link, 0.0))
                rank = (start, -tail_of(t.key))
                if best is None or rank < best[0]:
                    best = (rank, t)
        (start, _), t = best
        free[t.link] = start + t.rows / rate
        done[t.key] = start + t.rows / rate + latency
        order.append((start, t.key))
        left.remove(t)
    return [k for _, k in sorted(order, key=lambda e: e[0])]


RATE = 95.0
LATENCY = 2.5

SUM_A = (0, 104)
SUM_B = (104, 264)
ALL_A = (0, 104)
ALL_B = (104, 256)


def halves(span):
    lo, hi = span
    mid = lo + ((hi - lo) // 2 + 7) // 8 * 8
    return ((lo, mid), (mid, hi))


def sum_tasks():
    tasks = []

    def ring(stage, n, axis, piece, sign, rows, local_needs):
        for chain, (d, steps) in enumerate(ring_steps(n, sign)):
            for s in range(1, steps + 1):
                off = (d * (steps - s + 1)) % n
                needs = [(stage, piece, chain, s - 1)] if s > 1 else []
                tasks.append(Task((stage, piece, chain, s), (axis, d), rows, needs + local_needs(off)))

    def last(stage, n, piece):
        return [(stage, piece, 0, n // 2), (stage, piece, 1, n // 2 - 1)]

    for yo in range(NY):
        ring("a1", NZ, "z", yo, sign_of(yo), SUM_A[1] - SUM_A[0], lambda off: [])
    for h, (lo, hi) in enumerate(halves(SUM_A)):
        ring("a2", NY, "y", h, sign_of(h), hi - lo, lambda off: last("a1", NZ, off))
    for zo in range(NZ):
        ring("b1", NY, "y", zo, sign_of(zo), SUM_B[1] - SUM_B[0], lambda off: [])
    for h, (lo, hi) in enumerate(halves(SUM_B)):
        ring("b2", NZ, "z", h, sign_of(h), hi - lo, lambda off: last("b1", NY, off))
    return tasks


def all_tasks():
    tasks = []

    def ring(stage, n, axis, piece, sign, rows, first_needs):
        for chain, (d, steps) in enumerate(ring_steps(n, sign)):
            for s in range(1, steps + 1):
                needs = [(stage, piece, chain, s - 1)] if s > 1 else first_needs
                tasks.append(Task((stage, piece, chain, s), (axis, d), rows, needs))

    def arrives(stage, n, piece, sign, off):
        for chain, (d, steps) in enumerate(ring_steps(n, sign)):
            for s in range(1, steps + 1):
                if (-d * s) % n == off:
                    return (stage, piece, chain, s)

    for h, (lo, hi) in enumerate(halves(ALL_A)):
        ring("c1", NY, "y", h, sign_of(h), hi - lo, [])
    for yo in range(NY):
        needs = [arrives("c1", NY, h, sign_of(h), yo) for h in range(2)] if yo else []
        ring("c2", NZ, "z", yo, sign_of(yo), ALL_A[1] - ALL_A[0], needs)
    for h, (lo, hi) in enumerate(halves(ALL_B)):
        ring("d1", NZ, "z", h, sign_of(h), hi - lo, [])
    for zo in range(NZ):
        needs = [arrives("d1", NZ, h, sign_of(h), zo) for h in range(2)] if zo else []
        ring("d2", NY, "y", zo, sign_of(zo), ALL_B[1] - ALL_B[0], needs)
    return tasks


AHEAD = 3


def exchange_kernel(
    p_ref, meas_ref, resid_ref, hi_ref, lo_ref, all_ref, ra1, ra2, rb1, rb2, own, send_sem, recv_sem
):
    pix, ang = lax.axis_index("pix"), lax.axis_index("ang")
    z, y = pix // NY, lax.rem(pix, NY)

    def at(zo, yo):
        return lax.rem(z + zo % NZ, NZ) * NY + lax.rem(y + yo % NY, NY)

    def device(link):
        axis, d = link
        return (at(d, 0) if axis == "z" else at(0, d), ang)

    barrier = pltpu.get_barrier_semaphore()
    for link in (("z", 1), ("z", -1), ("y", 1), ("y", -1)):
        pl.semaphore_signal(barrier, inc=1, device_id=device(link), device_id_type=MESH)
    pl.semaphore_wait(barrier, 4)

    tasks = sum_tasks() + all_tasks()
    number = {t.key: i for i, t in enumerate(tasks)}
    by_key = {t.key: t for t in tasks}
    sums = schedule(sum_tasks(), LATENCY, RATE)
    alls = schedule(all_tasks(), LATENCY, RATE)

    a_rows, b_rows = pl.ds(SUM_A[0], SUM_A[1] - SUM_A[0]), pl.ds(SUM_B[0], SUM_B[1] - SUM_B[0])
    slot_of = {}
    for stage, ref in (("a1", ra1), ("a2", ra2), ("b1", rb1), ("b2", rb2)):
        keys = [t.key for t in tasks if t.key[0] == stage]
        for i, k in enumerate(keys):
            slot_of[k] = ref.at[i, pl.ds(0, by_key[k].rows)]

    def chain_of(n, piece, chain):
        return ring_steps(n, sign_of(piece))[chain]

    def origin(key):
        stage, piece, chain, s = key
        if stage in ("c1", "d1"):
            n = NY if stage == "c1" else NZ
            d, _ = chain_of(n, piece, chain)
            off = -d * (s - 1)
            lo, hi = halves(ALL_A if stage == "c1" else ALL_B)[piece]
            return (at(0, off) if stage == "c1" else at(off, 0)), pl.ds(lo, hi - lo)
        n = NZ if stage == "c2" else NY
        d, _ = chain_of(n, piece, chain)
        off = -d * (s - 1)
        lo, hi = ALL_A if stage == "c2" else ALL_B
        return (at(off, piece) if stage == "c2" else at(piece, off)), pl.ds(lo, hi - lo)

    def source(key):
        stage, piece, chain, s = key
        if stage in ("c1", "c2", "d1", "d2"):
            owner, rows = origin(key)
            ref = all_ref.at[owner, rows]
            return ref, ref
        dst = slot_of[key]
        if s > 1:
            return slot_of[(stage, piece, chain, s - 1)], dst
        return local(key), dst

    def local(key):
        stage, piece, chain, s = key
        if stage in ("a1", "b1"):
            n = NZ if stage == "a1" else NY
            d, steps = chain_of(n, piece, chain)
            off = d * (steps - s + 1)
            return p_ref.at[at(off, piece), a_rows] if stage == "a1" else p_ref.at[at(piece, off), b_rows]
        n = NY if stage == "a2" else NZ
        d, steps = chain_of(n, piece, chain)
        off = (d * (steps - s + 1)) % n
        span = SUM_A if stage == "a2" else SUM_B
        lo, hi = halves(span)[piece]
        first = ("a1" if stage == "a2" else "b1", off, 0, n_first(stage) // 2)
        return slot_of[first].at[pl.ds(lo - span[0], hi - lo)]

    def n_first(stage):
        return NZ if stage == "a2" else NY

    copies = {}

    def copy_of(key):
        if key not in copies:
            src, dst = source(key)
            i = number[key]
            copies[key] = pltpu.make_async_remote_copy(
                src_ref=src,
                dst_ref=dst,
                send_sem=send_sem.at[i],
                recv_sem=recv_sem.at[i],
                device_id=device(by_key[key].link),
                device_id_type=MESH,
            )
        return copies[key]

    received, sent, waited, finished = set(), {}, set(), set()

    def receive(key):
        if key not in received:
            received.add(key)
            copy_of(key).wait_recv()

    def finish(stage, off):
        if (stage, off) in finished:
            return
        finished.add((stage, off))
        n = NZ if stage == "a1" else NY
        one, two = (stage, off, 0, n // 2), (stage, off, 1, n // 2 - 1)
        receive(one)
        receive(two)
        mine = p_ref.at[at(0, off), a_rows] if stage == "a1" else p_ref.at[at(off, 0), b_rows]
        slot_of[one][...] = slot_of[one][...] + slot_of[two][...] + mine[...]

    def issue(key):
        stage, piece, chain, s = key
        task = by_key[key]
        queue = sent.setdefault(task.link, [])
        if len(queue) >= AHEAD:
            old = queue[-AHEAD]
            if old not in waited:
                waited.add(old)
                copy_of(old).wait_send()
        for k in task.needs:
            if stage in ("a2", "b2") and k[0] in ("a1", "b1"):
                finish(k[0], k[1])
            else:
                receive(k)
        if s > 1 and stage in ("a1", "a2", "b1", "b2"):
            ref = slot_of[(stage, piece, chain, s - 1)]
            ref[...] = ref[...] + local(key)[...]
        copy_of(key).start()
        queue.append(key)

    for key in sums:
        issue(key)
    for stage, span, n, n1 in (("a2", SUM_A, NY, NZ), ("b2", SUM_B, NZ, NY)):
        first = "a1" if stage == "a2" else "b1"
        finish(first, 0)
        for h, (lo, hi) in enumerate(halves(span)):
            one, two = (stage, h, 0, n // 2), (stage, h, 1, n // 2 - 1)
            receive(one)
            receive(two)
            mine = slot_of[(first, 0, 0, n1 // 2)].at[pl.ds(lo - span[0], hi - lo)]
            own[lo:hi, :] = slot_of[one][...] + slot_of[two][...] + mine[...]

    norms = [jnp.broadcast_to(own[OWN + h : OWN + h + 1, :], (128, 128)).T for h in range(2)]
    for b in range(4):
        for h in range(2):
            natural = pl.ds(b * BLK + h, 32, stride=2)
            mine = slice(b * BLK + 32 * h, b * BLK + 32 * h + 32)
            value = (meas_ref[natural, :] - own[mine, :]) / norms[h][32 * b : 32 * b + 32]
            resid_ref[natural, :] = value
            all_ref[at(0, 0), mine, :] = value

    def place(key):
        stage, piece, chain, s = key
        d, _ = chain_of(NY if stage in ("c1", "d2") else NZ, piece, chain)
        off = -d * s
        if stage == "c1":
            return 0, off % NY
        if stage == "d1":
            return off % NZ, 0
        return (off % NZ, piece) if stage == "c2" else (piece, off % NY)

    parts = {}
    for key in alls:
        parts.setdefault(place(key), []).append(key)

    def split(where):
        o = at(*where)
        rows = pl.ds(pl.multiple_of(o * 8, 8), 8)
        hi_ref[rows], lo_ref[rows] = split_bf16(all_ref[o].reshape(8, 32, S))

    def split_whole():
        for where in list(parts):
            if all(k in received for k in parts[where]):
                del parts[where]
                split(where)

    for i, key in enumerate(alls):
        issue(key)
        if i == 8:
            split((0, 0))
        split_whole()
    for key in alls:
        receive(key)
        split_whole()
    for t in tasks:
        receive(t.key)
    for t in tasks:
        if t.key not in waited:
            copy_of(t.key).wait_send()


def exchange(p, measured):
    tasks = sum_tasks() + all_tasks()
    count = {}
    for t in tasks:
        count[t.key[0]] = count.get(t.key[0], 0) + 1
    most = {k: max(t.rows for t in tasks if t.key[0] == k) for k in count}
    return pl.pallas_call(
        exchange_kernel,
        out_shape=(
            jax.ShapeDtypeStruct((OWN, S), jnp.float32),
            jax.ShapeDtypeStruct((RB * 2, 32, S), jnp.bfloat16),
            jax.ShapeDtypeStruct((RB * 2, 32, S), jnp.bfloat16),
        ),
        in_specs=[VM, VM],
        out_specs=(VM, VM, VM),
        scratch_shapes=[vmem(NZ * NY, OWN, S)]
        + [vmem(count[k], most[k], S) for k in ("a1", "a2", "b1", "b2")]
        + [
            vmem(CH, S),
            pltpu.SemaphoreType.DMA((len(tasks),)),
            pltpu.SemaphoreType.DMA((len(tasks),)),
        ],
        compiler_params=pltpu.CompilerParams(
            collective_id=1, has_side_effects=True, vmem_limit_bytes=24 * MIB
        ),
        cost_estimate=cost(50),
        name="sum_and_spread",
    )(p, measured)


UPD = ((0, 72), (72, 136))


def backward_kernel(
    code_ref, turned_ref, hi_ref, lo_ref, col_ref, out_ref, run_ref, b_ref, sib, far_buf, near_buf, second_buf,
    send_sem, recv_sem,
):
    here = Ang()
    wait_for_others = here.meet(("twin", 1, -1))

    def pixel_block(g):
        return lax.shift_right_logical(code_ref[0, g * GRP], 16) & (QB - 1)

    def step(b, run):
        for i in range(BWD):
            g = b * BWD + i
            codes = [code_ref[0, g * GRP + j] for j in range(GRP)]
            hi, lo = turned_ref[g, :, :128], turned_ref[g, :, 128:]
            slots = [c & (RB - 1) for c in codes]

            def rays(ref):
                return [ref[slot * 2 + h] for h in range(2) for slot in slots]

            r_hi, r_lo = rays(hi_ref), rays(lo_ref)
            left = jnp.concatenate([hi[:BLK], hi[BLK:], lo[:BLK], lo[BLK:], hi[:BLK], hi[BLK:]], axis=1)
            right = jnp.concatenate(r_hi + r_hi + r_lo, axis=0)
            out = jnp.dot(left, right, preferred_element_type=jnp.float32)
            before = pixel_block(jnp.maximum(g - 1, 0))
            run = run * (before == pixel_block(g)).astype(jnp.float32) + out
            run_ref[g] = run
        return run

    lax.fori_loop(0, STEPS, step, jnp.zeros((BLK, S), jnp.float32))
    for q in range(QB):
        last = code_ref[0, NPOS_PAD + q]
        total = run_ref[jnp.maximum(last, 0)]
        b_ref[q // 2, q % 2 * BLK : q % 2 * BLK + BLK, :] = total * (last >= 0).astype(jnp.float32)
    for o in range(NA):
        b_ref[o, 128:136, :] = col_ref[o]

    wait_for_others()
    number = iter(range(10))

    def send(to, src, dst):
        i = next(number)
        copy = pltpu.make_async_remote_copy(
            src_ref=src,
            dst_ref=dst,
            send_sem=send_sem.at[i],
            recv_sem=recv_sem.at[i],
            device_id=here.device(to),
            device_id_type=MESH,
        )
        copy.start()
        return copy

    across = {dx: send("twin", b_ref.at[here.twin(dx)], sib.at[dx]) for dx in (2, 1, 3, 0)}

    def arrive(dx):
        across[dx].wait_recv()
        sib[dx] = sib[dx] + b_ref[here.index(dx)]

    def rows(h):
        return pl.ds(UPD[h][0], UPD[h][1] - UPD[h][0])

    def part(buf, h):
        return buf.at[h, pl.ds(0, UPD[h][1] - UPD[h][0])]

    arrive(2)
    far = [send(sign_of(h), sib.at[2, rows(h)], part(far_buf, h)) for h in range(2)]
    arrive(1)
    arrive(3)
    near = [send(-sign_of(h), sib.at[-sign_of(h) % NX, rows(h)], part(near_buf, h)) for h in range(2)]
    arrive(0)
    second = []
    for h in range(2):
        far[h].wait_recv()
        part(far_buf, h)[...] = part(far_buf, h)[...] + sib[sign_of(h) % NX, rows(h), :]
        second.append(send(sign_of(h), part(far_buf, h), part(second_buf, h)))
    totals = []
    for h in range(2):
        near[h].wait_recv()
        totals.append(sib[0, rows(h), :] + part(near_buf, h)[...])
    for h in range(2):
        second[h].wait_recv()
        totals[h] = totals[h] + part(second_buf, h)[...]
    total = jnp.concatenate(totals, axis=0)
    norm = jnp.broadcast_to(total[128:129], (128, 128)).T
    out_ref[...] = RELAX * total[:128] / norm
    for copy in [*across.values(), *far, *near, *second]:
        copy.wait_send()


def backward(code, turned, high, low, col):
    size = UPD[0][1]
    return pl.pallas_call(
        backward_kernel,
        out_shape=jax.ShapeDtypeStruct((128, S), jnp.float32),
        in_specs=[SM, VM, VM, VM, VM],
        out_specs=VM,
        scratch_shapes=[
            vmem(STEPS * BWD, BLK, S),
            vmem(NA, 136, S),
            vmem(NX, 136, S),
            vmem(2, size, S),
            vmem(2, size, S),
            vmem(2, size, S),
            pltpu.SemaphoreType.DMA((10,)),
            pltpu.SemaphoreType.DMA((10,)),
        ],
        compiler_params=pltpu.CompilerParams(
            collective_id=2, has_side_effects=True, vmem_limit_bytes=32 * MIB
        ),
        cost_estimate=cost(17),
        name="backward_and_sum",
    )(code, turned, high, low, col)


def finish_kernel(image_ref, step_ref, own_ref, new_ref, resid_ref):
    resid_ref[...] = own_ref[...]
    new_ref[...] = image_ref[...] + step_ref[...]


def finish(image, step, own):
    return pl.pallas_call(
        finish_kernel,
        out_shape=(
            jax.ShapeDtypeStruct((128, S), jnp.float32),
            jax.ShapeDtypeStruct((OWN, S), jnp.float32),
        ),
        in_specs=[VM, VM, VM],
        out_specs=(VM, VM),
        compiler_params=pltpu.CompilerParams(vmem_limit_bytes=24 * MIB),
        cost_estimate=cost(1),
        name="new_image",
    )(image, step, own)


def shards(tiles, tile_ray, tile_pix, tile_count, ray_slot, image, measured):
    rows = tiles[0, 0].reshape(SLOTS // 8, 8, 32, 128).transpose(0, 2, 1, 3).reshape(SLOTS * 32, 128)
    used_tiles = jnp.broadcast_to(tile_count[0], (RB,))
    index = jnp.concatenate([tile_ray[0, 0], tile_pix[0, 0], ray_slot[0], used_tiles])[None]
    img, code = gather_image(index, image)
    p, col, turned = forward(code, rows, img)
    own, high, low = exchange(p, measured[0])
    new_image, resid = finish(image, backward(code, turned, high, low, col), own)
    return (new_image, resid[None])


def solution(mesh):
    in_specs = (
        P("pix", "ang", None, None),
        P("pix", "ang", None),
        P("pix", "ang", None),
        P("pix", "ang"),
        P("ang", None),
        P(("pix", "ang"), None),
        P("ang", "pix", None),
    )
    out_specs = (P(("pix", "ang"), None), P("ang", "pix", None))
    return jax.shard_map(shards, mesh=mesh, in_specs=in_specs, out_specs=out_specs, check_vma=False)
```

```python
import functools

import jax
import jax.numpy as jnp
from jax import lax
from jax.experimental import pallas as pl
from jax.experimental.pallas import tpu as pltpu
from jax.sharding import PartitionSpec as P

MESH = pl.DeviceIdType.MESH
BLK, S, SLOTS, RB, QB = 64, 128, 512, 128, 16
RELAX = 0.9
NZ, NY, NX, NA = 8, 4, 4, 8
GRP = 4
NPOS = SLOTS + QB * (GRP - 1)
NPOS_PAD = 640
LIST = NPOS_PAD + 128
BWD = 18
STEPS = NPOS // GRP // BWD + 1
OWN = 256
CH = OWN + 8
VM = pl.BlockSpec(memory_space=pltpu.VMEM)
SM = pl.BlockSpec(memory_space=pltpu.SMEM)
MIB = 1024 * 1024


def cost(us):
    return pl.CostEstimate(flops=int(us * 1.15e9), bytes_accessed=0, transcendentals=0)


def vmem(*shape, dtype=jnp.float32):
    return pltpu.VMEM(shape, dtype)


def split_bf16(x):
    hi = x.astype(jnp.bfloat16)
    return hi, (x - hi.astype(jnp.float32)).astype(jnp.bfloat16)


def sign_of(i):
    return 1 if i % 2 == 0 else -1


class Ang:
    def __init__(self):
        self.pix, me = lax.axis_index("pix"), lax.axis_index("ang")
        self.me, self.x, self.core = me, me // 2, lax.rem(me, 2)

    def index(self, dx):
        return lax.rem(self.x + dx % NX, NX) * 2 + self.core

    def twin(self, dx=0):
        return lax.rem(self.x + dx % NX, NX) * 2 + (1 - self.core)

    def device(self, to):
        if to == "twin":
            return (self.pix, self.twin())
        return (self.pix, self.twin(to // 2) if to % 2 == 0 else self.index(to))

    def meet(self, others):
        barrier = pltpu.get_barrier_semaphore()
        for to in others:
            pl.semaphore_signal(barrier, inc=1, device_id=self.device(to), device_id_type=MESH)
        return lambda: pl.semaphore_wait(barrier, len(others))


def sort_tiles(ray, pix, used_tiles, table):
    f32 = jnp.float32
    both = jnp.broadcast_to((pix * RB + ray).astype(f32), (128, SLOTS)).T.astype(jnp.int32)
    lane = lax.broadcasted_iota(jnp.int32, (SLOTS, 128), 1)
    t = lax.broadcasted_iota(jnp.int32, (SLOTS, 128), 0)
    q = lax.shift_right_logical(both, 7)
    mine = jnp.where((q == lane) & (t < used_tiles), 1.0, 0.0).astype(f32)
    slot = jnp.sum(jnp.where((both & (RB - 1)) == lane, table.astype(f32), 0.0), axis=1, keepdims=True)
    earlier = lax.broadcasted_iota(jnp.int32, (SLOTS, SLOTS), 1) < lax.broadcasted_iota(jnp.int32, (SLOTS, SLOTS), 0)
    earlier = jnp.where(earlier, 1.0, 0.0).astype(jnp.bfloat16)
    before = jnp.dot(earlier, mine.astype(jnp.bfloat16), preferred_element_type=f32)
    counts = jnp.sum(mine, axis=0, keepdims=True).astype(jnp.int32)
    groups = lax.shift_right_logical(counts + (GRP - 1), 2).astype(f32)
    left_of = lax.broadcasted_iota(jnp.int32, (128, 128), 0) < lax.broadcasted_iota(jnp.int32, (128, 128), 1)
    left_of = jnp.where(left_of, 1.0, 0.0).astype(jnp.bfloat16)
    first = jnp.dot(jnp.broadcast_to(groups, (8, 128)).astype(jnp.bfloat16), left_of, preferred_element_type=f32)
    place = jnp.sum(mine * (before + GRP * first[:1]), axis=1, keepdims=True)
    place = jnp.where(t < used_tiles, place, -1.0)
    code = ((1 << 20) + q * (1 << 16) + t * RB).astype(f32) + slot
    parts = []
    for c in range(NPOS_PAD // 128):
        at = (lax.broadcasted_iota(jnp.int32, (1, 128), 1) + c * 128).astype(f32)
        part = jnp.sum(jnp.where(place == at, code, 0.0), axis=0, keepdims=True)
        parts.append(jnp.where(at == NPOS_PAD - 1, jnp.sum(groups, axis=1, keepdims=True), part))
    parts.append(jnp.where(groups > 0.0, first[:1] + groups - 1.0, -1.0))
    return jnp.concatenate(parts, axis=1).astype(jnp.int32)


def gather_kernel(
    index_ref, img_ref, out_ref, code_ref, send_sem, recv_sem
):
    here = Ang()
    here.meet(("twin", 1, -1, 2, -2))()
    number = iter(range(13))

    def send(to, dx, half, src=None):
        lo, size = (0, 128) if half is None else (64 * half, 64)
        rows = out_ref.at[pl.ds(pl.multiple_of(here.index(dx) * 128 + lo, 64), size)]
        i = next(number)
        copy = pltpu.make_async_remote_copy(
            src_ref=rows if src is None else src.at[pl.ds(lo, size)],
            dst_ref=rows,
            send_sem=send_sem.at[i],
            recv_sem=recv_sem.at[i],
            device_id=here.device(to),
            device_id_type=MESH,
        )
        copy.start()
        return copy

    far = [send(sign_of(h), 0, h, img_ref) for h in range(2)]
    near = [send(-sign_of(h), 0, h, img_ref) for h in range(2)]
    across = [send("twin", 0, None, img_ref)]
    out_ref[pl.ds(pl.multiple_of(here.me * 128, 128), 128), :] = img_ref[...]
    ray, pix = index_ref[:, :SLOTS], index_ref[:, SLOTS : 2 * SLOTS]
    table, used_tiles = index_ref[:, 2 * SLOTS : 2 * SLOTS + RB], index_ref[:, 2 * SLOTS + RB :]
    code_ref[...] = sort_tiles(ray, pix, used_tiles, table)
    second = []
    for h in range(2):
        far[h].wait_recv()
        second += [send(sign_of(h), -sign_of(h), h), send(2 * sign_of(h), -sign_of(h), h)]
        across.append(send("twin", -sign_of(h), h))
    for h in range(2):
        near[h].wait_recv()
        across.append(send("twin", sign_of(h), h))
    across += second
    for copy in across:
        copy.wait_recv()
    for copy in far + near + across:
        copy.wait_send()


def gather_image(index, image):
    return pl.pallas_call(
        gather_kernel,
        out_shape=(
            jax.ShapeDtypeStruct((NA * 128, S), jnp.float32),
            jax.ShapeDtypeStruct((1, LIST), jnp.int32),
        ),
        in_specs=[VM, VM],
        out_specs=(VM, VM),
        scratch_shapes=[
            pltpu.SemaphoreType.DMA((13,)),
            pltpu.SemaphoreType.DMA((13,)),
        ],
        compiler_params=pltpu.CompilerParams(
            collective_id=0, has_side_effects=True, vmem_limit_bytes=24 * MIB
        ),
        cost_estimate=cost(8),
        name="gather_image",
    )(index, image)


def tile_rows(tiles_ref, code):
    t = lax.shift_right_logical(code, 7) & (SLOTS - 1)
    start = lax.shift_right_logical(t, 3) * 256 + (t & 7)
    used = lax.shift_right_logical(code, 20).astype(jnp.float32)
    return tiles_ref[pl.ds(start, 32, stride=8), :] * used


FWD = 16


def forward_kernel(code_ref, tiles_ref, img_ref, p_ref, col_ref, turned_ref, w_ref, rowacc, colacc):
    zero = jnp.zeros((BLK, S), jnp.bfloat16)

    def weights(q, _):
        hi, lo = split_bf16(img_ref[pl.ds(pl.multiple_of(q * BLK, BLK), BLK), :])
        both = [jnp.concatenate([jnp.concatenate([x, zero], 1), jnp.concatenate([zero, x], 1)], 0) for x in (hi, lo)]
        w_ref[q] = jnp.concatenate([both[0], both[0], both[1]], axis=0)
        return _

    lax.fori_loop(0, QB, weights, 0, unroll=4)
    rowacc[...] = jnp.zeros_like(rowacc)
    colacc[...] = jnp.zeros_like(colacc)

    def clear(o, _):
        p_ref[o] = jnp.zeros((CH, S), jnp.float32)
        return _

    lax.fori_loop(0, NZ * NY, clear, 0, unroll=4)

    def place(slot):
        rows = pl.ds(pl.multiple_of((slot & 3) * BLK, BLK), BLK)
        return lax.shift_right_logical(slot, 2), rows, slice(None)

    def read(slot):
        return p_ref[place(slot)]

    def write(slot, value):
        p_ref[place(slot)] = value

    def read_rows(slot):
        return rowacc[slot]

    def write_rows(slot, value):
        rowacc[slot] = value

    def step(b, _):
        for i in range(FWD):
            codes = [code_ref[0, (b * FWD + i) * GRP + j] for j in range(GRP)]
            q = lax.shift_right_logical(codes[0], 16) & (QB - 1)
            slots = [c & (RB - 1) for c in codes]
            tiles = [tile_rows(tiles_ref, c) for c in codes]
            hi, lo = split_bf16(jnp.concatenate(tiles, axis=0))
            turned_ref[b * FWD + i] = jnp.concatenate([hi.T, lo.T], axis=1)
            out = jnp.dot(jnp.concatenate([hi, lo, hi], axis=1), w_ref[q], preferred_element_type=jnp.float32)
            terms = [
                jnp.concatenate([out[32 * j : 32 * j + 32, h * S : h * S + S] for h in range(2)], axis=0)
                for j in range(GRP)
            ]
            for k, v in zip(slots, tiles):
                rowacc[k] += v
            colacc[q] += (tiles[0] + tiles[1]) + (tiles[2] + tiles[3])
            for k, v in zip(slots, terms):
                write(k, read(k) + v)
        return _

    lax.fori_loop(0, (code_ref[0, NPOS_PAD - 1] + FWD - 1) // FWD, step, 0)

    lane = lax.broadcasted_iota(jnp.int32, (8, 256), 1)
    pick = lax.broadcasted_iota(jnp.int32, (8, 256), 0) == (lane & 127) // BLK
    pick = pick.astype(jnp.float32).astype(jnp.bfloat16)

    def row_sums(o, _):
        both = jnp.concatenate(split_bf16(rowacc[pl.ds(o * 8, 8)].reshape(256, 128)), axis=1)
        sums = lax.dot_general(pick, both, (((1,), (1,)), ((), ())), preferred_element_type=jnp.float32)
        p_ref[2 * o, OWN:CH, :] = sums[:, :128]
        p_ref[2 * o + 1, OWN:CH, :] = sums[:, 128:]
        return _

    lax.fori_loop(0, NZ * NY // 2, row_sums, 0, unroll=8)
    low = lax.broadcasted_iota(jnp.int32, (1, 128), 1) < BLK
    for o in range(NA):
        a = jnp.sum(colacc[2 * o], axis=0, keepdims=True)
        b = jnp.sum(colacc[2 * o + 1], axis=0, keepdims=True)
        a = a + pltpu.roll(a, BLK, 1)
        b = b + pltpu.roll(b, BLK, 1)
        col_ref[o] = jnp.broadcast_to(jnp.where(low, a, b), (8, 128))


def forward(code, tiles, img):
    return pl.pallas_call(
        forward_kernel,
        out_shape=(
            jax.ShapeDtypeStruct((NZ * NY, CH, S), jnp.float32),
            jax.ShapeDtypeStruct((NA, 8, 128), jnp.float32),
            jax.ShapeDtypeStruct((STEPS * BWD, 128, 2 * 128), jnp.bfloat16),
        ),
        in_specs=[SM, VM, VM],
        out_specs=(VM, VM, VM),
        scratch_shapes=[
            vmem(QB, 6 * BLK, 2 * S, dtype=jnp.bfloat16),
            vmem(RB, 32, 128),
            vmem(QB, 32, 128),
        ],
        compiler_params=pltpu.CompilerParams(vmem_limit_bytes=32 * MIB),
        cost_estimate=cost(13),
        name="forward_tiles",
    )(code, tiles, img)


def ring_steps(n, sign):
    return ((sign, n // 2), (-sign, n // 2 - 1))


class Task:
    def __init__(self, key, link, rows, needs):
        self.key, self.link, self.rows, self.needs = key, link, rows, needs


def schedule(tasks, latency, rate):
    by_key = {t.key: t for t in tasks}
    follow = {t.key: [] for t in tasks}
    for t in tasks:
        for k in t.needs:
            follow[k].append(t.key)
    tail = {}

    def tail_of(k):
        if k not in tail:
            t = by_key[k]
            tail[k] = t.rows / rate + latency + max([tail_of(f) for f in follow[k]], default=0.0)
        return tail[k]

    left, done, free, order = list(tasks), {}, {}, []
    while left:
        best = None
        for t in left:
            if all(k in done for k in t.needs):
                at = max([done[k] for k in t.needs], default=0.0)
                start = max(at, free.get(t.link, 0.0))
                rank = (start, -tail_of(t.key))
                if best is None or rank < best[0]:
                    best = (rank, t)
        (start, _), t = best
        free[t.link] = start + t.rows / rate
        done[t.key] = start + t.rows / rate + latency
        order.append((start, t.key))
        left.remove(t)
    return [k for _, k in sorted(order, key=lambda e: e[0])]


RATE = 95.0
LATENCY = 2.5

SUM_A = (0, 104)
SUM_B = (104, 264)
ALL_A = (0, 104)
ALL_B = (104, 256)


def halves(span):
    lo, hi = span
    mid = lo + ((hi - lo) // 2 + 7) // 8 * 8
    return ((lo, mid), (mid, hi))


def sum_tasks():
    tasks = []

    def ring(stage, n, axis, piece, sign, rows, local_needs):
        for chain, (d, steps) in enumerate(ring_steps(n, sign)):
            for s in range(1, steps + 1):
                off = (d * (steps - s + 1)) % n
                needs = [(stage, piece, chain, s - 1)] if s > 1 else []
                tasks.append(Task((stage, piece, chain, s), (axis, d), rows, needs + local_needs(off)))

    def last(stage, n, piece):
        return [(stage, piece, 0, n // 2), (stage, piece, 1, n // 2 - 1)]

    for yo in range(NY):
        ring("a1", NZ, "z", yo, sign_of(yo), SUM_A[1] - SUM_A[0], lambda off: [])
    for h, (lo, hi) in enumerate(halves(SUM_A)):
        ring("a2", NY, "y", h, sign_of(h), hi - lo, lambda off: last("a1", NZ, off))
    for zo in range(NZ):
        ring("b1", NY, "y", zo, sign_of(zo), SUM_B[1] - SUM_B[0], lambda off: [])
    for h, (lo, hi) in enumerate(halves(SUM_B)):
        ring("b2", NZ, "z", h, sign_of(h), hi - lo, lambda off: last("b1", NY, off))
    return tasks


def all_tasks():
    tasks = []

    def ring(stage, n, axis, piece, sign, rows, first_needs):
        for chain, (d, steps) in enumerate(ring_steps(n, sign)):
            for s in range(1, steps + 1):
                needs = [(stage, piece, chain, s - 1)] if s > 1 else first_needs
                tasks.append(Task((stage, piece, chain, s), (axis, d), rows, needs))

    def arrives(stage, n, piece, sign, off):
        for chain, (d, steps) in enumerate(ring_steps(n, sign)):
            for s in range(1, steps + 1):
                if (-d * s) % n == off:
                    return (stage, piece, chain, s)

    for h, (lo, hi) in enumerate(halves(ALL_A)):
        ring("c1", NY, "y", h, sign_of(h), hi - lo, [])
    for yo in range(NY):
        needs = [arrives("c1", NY, h, sign_of(h), yo) for h in range(2)] if yo else []
        ring("c2", NZ, "z", yo, sign_of(yo), ALL_A[1] - ALL_A[0], needs)
    for h, (lo, hi) in enumerate(halves(ALL_B)):
        ring("d1", NZ, "z", h, sign_of(h), hi - lo, [])
    for zo in range(NZ):
        needs = [arrives("d1", NZ, h, sign_of(h), zo) for h in range(2)] if zo else []
        ring("d2", NY, "y", zo, sign_of(zo), ALL_B[1] - ALL_B[0], needs)
    return tasks


AHEAD = 3


def exchange_kernel(
    p_ref, meas_ref, resid_ref, hi_ref, lo_ref, all_ref, ra1, ra2, rb1, rb2, own, send_sem, recv_sem
):
    pix, ang = lax.axis_index("pix"), lax.axis_index("ang")
    z, y = pix // NY, lax.rem(pix, NY)

    def at(zo, yo):
        return lax.rem(z + zo % NZ, NZ) * NY + lax.rem(y + yo % NY, NY)

    def device(link):
        axis, d = link
        return (at(d, 0) if axis == "z" else at(0, d), ang)

    barrier = pltpu.get_barrier_semaphore()
    for link in (("z", 1), ("z", -1), ("y", 1), ("y", -1)):
        pl.semaphore_signal(barrier, inc=1, device_id=device(link), device_id_type=MESH)
    pl.semaphore_wait(barrier, 4)

    tasks = sum_tasks() + all_tasks()
    number = {t.key: i for i, t in enumerate(tasks)}
    by_key = {t.key: t for t in tasks}
    sums = schedule(sum_tasks(), LATENCY, RATE)
    alls = schedule(all_tasks(), LATENCY, RATE)

    a_rows, b_rows = pl.ds(SUM_A[0], SUM_A[1] - SUM_A[0]), pl.ds(SUM_B[0], SUM_B[1] - SUM_B[0])
    slot_of = {}
    for stage, ref in (("a1", ra1), ("a2", ra2), ("b1", rb1), ("b2", rb2)):
        keys = [t.key for t in tasks if t.key[0] == stage]
        for i, k in enumerate(keys):
            slot_of[k] = ref.at[i, pl.ds(0, by_key[k].rows)]

    def chain_of(n, piece, chain):
        return ring_steps(n, sign_of(piece))[chain]

    def origin(key):
        stage, piece, chain, s = key
        if stage in ("c1", "d1"):
            n = NY if stage == "c1" else NZ
            d, _ = chain_of(n, piece, chain)
            off = -d * (s - 1)
            lo, hi = halves(ALL_A if stage == "c1" else ALL_B)[piece]
            return (at(0, off) if stage == "c1" else at(off, 0)), pl.ds(lo, hi - lo)
        n = NZ if stage == "c2" else NY
        d, _ = chain_of(n, piece, chain)
        off = -d * (s - 1)
        lo, hi = ALL_A if stage == "c2" else ALL_B
        return (at(off, piece) if stage == "c2" else at(piece, off)), pl.ds(lo, hi - lo)

    def source(key):
        stage, piece, chain, s = key
        if stage in ("c1", "c2", "d1", "d2"):
            owner, rows = origin(key)
            ref = all_ref.at[owner, rows]
            return ref, ref
        dst = slot_of[key]
        if s > 1:
            return slot_of[(stage, piece, chain, s - 1)], dst
        return local(key), dst

    def local(key):
        stage, piece, chain, s = key
        if stage in ("a1", "b1"):
            n = NZ if stage == "a1" else NY
            d, steps = chain_of(n, piece, chain)
            off = d * (steps - s + 1)
            return p_ref.at[at(off, piece), a_rows] if stage == "a1" else p_ref.at[at(piece, off), b_rows]
        n = NY if stage == "a2" else NZ
        d, steps = chain_of(n, piece, chain)
        off = (d * (steps - s + 1)) % n
        span = SUM_A if stage == "a2" else SUM_B
        lo, hi = halves(span)[piece]
        first = ("a1" if stage == "a2" else "b1", off, 0, n_first(stage) // 2)
        return slot_of[first].at[pl.ds(lo - span[0], hi - lo)]

    def n_first(stage):
        return NZ if stage == "a2" else NY

    copies = {}

    def copy_of(key):
        if key not in copies:
            src, dst = source(key)
            i = number[key]
            copies[key] = pltpu.make_async_remote_copy(
                src_ref=src,
                dst_ref=dst,
                send_sem=send_sem.at[i],
                recv_sem=recv_sem.at[i],
                device_id=device(by_key[key].link),
                device_id_type=MESH,
            )
        return copies[key]

    received, sent, waited, finished = set(), {}, set(), set()

    def receive(key):
        if key not in received:
            received.add(key)
            copy_of(key).wait_recv()

    def finish(stage, off):
        if (stage, off) in finished:
            return
        finished.add((stage, off))
        n = NZ if stage == "a1" else NY
        one, two = (stage, off, 0, n // 2), (stage, off, 1, n // 2 - 1)
        receive(one)
        receive(two)
        mine = p_ref.at[at(0, off), a_rows] if stage == "a1" else p_ref.at[at(off, 0), b_rows]
        slot_of[one][...] = slot_of[one][...] + slot_of[two][...] + mine[...]

    def issue(key):
        stage, piece, chain, s = key
        task = by_key[key]
        queue = sent.setdefault(task.link, [])
        if len(queue) >= AHEAD:
            old = queue[-AHEAD]
            if old not in waited:
                waited.add(old)
                copy_of(old).wait_send()
        for k in task.needs:
            if stage in ("a2", "b2") and k[0] in ("a1", "b1"):
                finish(k[0], k[1])
            else:
                receive(k)
        if s > 1 and stage in ("a1", "a2", "b1", "b2"):
            ref = slot_of[(stage, piece, chain, s - 1)]
            ref[...] = ref[...] + local(key)[...]
        copy_of(key).start()
        queue.append(key)

    for key in sums:
        issue(key)
    for stage, span, n, n1 in (("a2", SUM_A, NY, NZ), ("b2", SUM_B, NZ, NY)):
        first = "a1" if stage == "a2" else "b1"
        finish(first, 0)
        for h, (lo, hi) in enumerate(halves(span)):
            one, two = (stage, h, 0, n // 2), (stage, h, 1, n // 2 - 1)
            receive(one)
            receive(two)
            mine = slot_of[(first, 0, 0, n1 // 2)].at[pl.ds(lo - span[0], hi - lo)]
            own[lo:hi, :] = slot_of[one][...] + slot_of[two][...] + mine[...]

    norms = [jnp.broadcast_to(own[OWN + h : OWN + h + 1, :], (128, 128)).T for h in range(2)]
    for b in range(4):
        for h in range(2):
            natural = pl.ds(b * BLK + h, 32, stride=2)
            mine = slice(b * BLK + 32 * h, b * BLK + 32 * h + 32)
            value = (meas_ref[natural, :] - own[mine, :]) / norms[h][32 * b : 32 * b + 32]
            resid_ref[natural, :] = value
            all_ref[at(0, 0), mine, :] = value

    def place(key):
        stage, piece, chain, s = key
        d, _ = chain_of(NY if stage in ("c1", "d2") else NZ, piece, chain)
        off = -d * s
        if stage == "c1":
            return 0, off % NY
        if stage == "d1":
            return off % NZ, 0
        return (off % NZ, piece) if stage == "c2" else (piece, off % NY)

    parts = {}
    for key in alls:
        parts.setdefault(place(key), []).append(key)

    def split(where):
        o = at(*where)
        rows = pl.ds(pl.multiple_of(o * 8, 8), 8)
        hi_ref[rows], lo_ref[rows] = split_bf16(all_ref[o].reshape(8, 32, S))

    def split_whole():
        for where in list(parts):
            if all(k in received for k in parts[where]):
                del parts[where]
                split(where)

    for i, key in enumerate(alls):
        issue(key)
        if i == 8:
            split((0, 0))
        split_whole()
    for key in alls:
        receive(key)
        split_whole()
    for t in tasks:
        receive(t.key)
    for t in tasks:
        if t.key not in waited:
            copy_of(t.key).wait_send()


def exchange(p, measured):
    tasks = sum_tasks() + all_tasks()
    count = {}
    for t in tasks:
        count[t.key[0]] = count.get(t.key[0], 0) + 1
    most = {k: max(t.rows for t in tasks if t.key[0] == k) for k in count}
    return pl.pallas_call(
        exchange_kernel,
        out_shape=(
            jax.ShapeDtypeStruct((OWN, S), jnp.float32),
            jax.ShapeDtypeStruct((RB * 2, 32, S), jnp.bfloat16),
            jax.ShapeDtypeStruct((RB * 2, 32, S), jnp.bfloat16),
        ),
        in_specs=[VM, VM],
        out_specs=(VM, VM, VM),
        scratch_shapes=[vmem(NZ * NY, OWN, S)]
        + [vmem(count[k], most[k], S) for k in ("a1", "a2", "b1", "b2")]
        + [
            vmem(CH, S),
            pltpu.SemaphoreType.DMA((len(tasks),)),
            pltpu.SemaphoreType.DMA((len(tasks),)),
        ],
        compiler_params=pltpu.CompilerParams(
            collective_id=1, has_side_effects=True, vmem_limit_bytes=24 * MIB
        ),
        cost_estimate=cost(50),
        name="sum_and_spread",
    )(p, measured)


UPD = ((0, 72), (72, 136))


def backward_kernel(
    code_ref, turned_ref, hi_ref, lo_ref, col_ref, out_ref, run_ref, b_ref, sib, far_buf, near_buf, second_buf,
    send_sem, recv_sem,
):
    here = Ang()
    wait_for_others = here.meet(("twin", 1, -1))

    def pixel_block(g):
        return lax.shift_right_logical(code_ref[0, g * GRP], 16) & (QB - 1)

    def step(b, run):
        for i in range(BWD):
            g = b * BWD + i
            codes = [code_ref[0, g * GRP + j] for j in range(GRP)]
            hi, lo = turned_ref[g, :, :128], turned_ref[g, :, 128:]
            slots = [c & (RB - 1) for c in codes]

            def rays(ref):
                return [ref[slot * 2 + h] for h in range(2) for slot in slots]

            r_hi, r_lo = rays(hi_ref), rays(lo_ref)
            left = jnp.concatenate([hi[:BLK], hi[BLK:], lo[:BLK], lo[BLK:], hi[:BLK], hi[BLK:]], axis=1)
            right = jnp.concatenate(r_hi + r_hi + r_lo, axis=0)
            out = jnp.dot(left, right, preferred_element_type=jnp.float32)
            before = pixel_block(jnp.maximum(g - 1, 0))
            run = run * (before == pixel_block(g)).astype(jnp.float32) + out
            run_ref[g] = run
        return run

    lax.fori_loop(0, STEPS, step, jnp.zeros((BLK, S), jnp.float32))
    for q in range(QB):
        last = code_ref[0, NPOS_PAD + q]
        total = run_ref[jnp.maximum(last, 0)]
        b_ref[q // 2, q % 2 * BLK : q % 2 * BLK + BLK, :] = total * (last >= 0).astype(jnp.float32)
    for o in range(NA):
        b_ref[o, 128:136, :] = col_ref[o]

    wait_for_others()
    number = iter(range(10))

    def send(to, src, dst):
        i = next(number)
        copy = pltpu.make_async_remote_copy(
            src_ref=src,
            dst_ref=dst,
            send_sem=send_sem.at[i],
            recv_sem=recv_sem.at[i],
            device_id=here.device(to),
            device_id_type=MESH,
        )
        copy.start()
        return copy

    across = {dx: send("twin", b_ref.at[here.twin(dx)], sib.at[dx]) for dx in (2, 1, 3, 0)}

    def arrive(dx):
        across[dx].wait_recv()
        sib[dx] = sib[dx] + b_ref[here.index(dx)]

    def rows(h):
        return pl.ds(UPD[h][0], UPD[h][1] - UPD[h][0])

    def part(buf, h):
        return buf.at[h, pl.ds(0, UPD[h][1] - UPD[h][0])]

    arrive(2)
    far = [send(sign_of(h), sib.at[2, rows(h)], part(far_buf, h)) for h in range(2)]
    arrive(1)
    arrive(3)
    near = [send(-sign_of(h), sib.at[-sign_of(h) % NX, rows(h)], part(near_buf, h)) for h in range(2)]
    arrive(0)
    second = []
    for h in range(2):
        far[h].wait_recv()
        part(far_buf, h)[...] = part(far_buf, h)[...] + sib[sign_of(h) % NX, rows(h), :]
        second.append(send(sign_of(h), part(far_buf, h), part(second_buf, h)))
    totals = []
    for h in range(2):
        near[h].wait_recv()
        totals.append(sib[0, rows(h), :] + part(near_buf, h)[...])
    for h in range(2):
        second[h].wait_recv()
        totals[h] = totals[h] + part(second_buf, h)[...]
    total = jnp.concatenate(totals, axis=0)
    norm = jnp.broadcast_to(total[128:129], (128, 128)).T
    out_ref[...] = RELAX * total[:128] / norm
    for copy in [*across.values(), *far, *near, *second]:
        copy.wait_send()


def backward(code, turned, high, low, col):
    size = UPD[0][1]
    return pl.pallas_call(
        backward_kernel,
        out_shape=jax.ShapeDtypeStruct((128, S), jnp.float32),
        in_specs=[SM, VM, VM, VM, VM],
        out_specs=VM,
        scratch_shapes=[
            vmem(STEPS * BWD, BLK, S),
            vmem(NA, 136, S),
            vmem(NX, 136, S),
            vmem(2, size, S),
            vmem(2, size, S),
            vmem(2, size, S),
            pltpu.SemaphoreType.DMA((10,)),
            pltpu.SemaphoreType.DMA((10,)),
        ],
        compiler_params=pltpu.CompilerParams(
            collective_id=2, has_side_effects=True, vmem_limit_bytes=32 * MIB
        ),
        cost_estimate=cost(17),
        name="backward_and_sum",
    )(code, turned, high, low, col)


def finish_kernel(image_ref, step_ref, own_ref, new_ref, resid_ref):
    resid_ref[...] = own_ref[...]
    new_ref[...] = image_ref[...] + step_ref[...]


def finish(image, step, own):
    return pl.pallas_call(
        finish_kernel,
        out_shape=(
            jax.ShapeDtypeStruct((128, S), jnp.float32),
            jax.ShapeDtypeStruct((OWN, S), jnp.float32),
        ),
        in_specs=[VM, VM, VM],
        out_specs=(VM, VM),
        compiler_params=pltpu.CompilerParams(vmem_limit_bytes=24 * MIB),
        cost_estimate=cost(1),
        name="new_image",
    )(image, step, own)


def shards(tiles, tile_ray, tile_pix, tile_count, ray_slot, image, measured):
    rows = tiles[0, 0].reshape(SLOTS // 8, 8, 32, 128).transpose(0, 2, 1, 3).reshape(SLOTS * 32, 128)
    used_tiles = jnp.broadcast_to(tile_count[0], (RB,))
    index = jnp.concatenate([tile_ray[0, 0], tile_pix[0, 0], ray_slot[0], used_tiles])[None]
    img, code = gather_image(index, image)
    p, col, turned = forward(code, rows, img)
    own, high, low = exchange(p, measured[0])
    new_image, resid = finish(image, backward(code, turned, high, low, col), own)
    return (new_image, resid[None])


def solution(mesh):
    in_specs = (
        P("pix", "ang", None, None),
        P("pix", "ang", None),
        P("pix", "ang", None),
        P("pix", "ang"),
        P("ang", None),
        P(("pix", "ang"), None),
        P("ang", "pix", None),
    )
    out_specs = (P(("pix", "ang"), None), P("ang", "pix", None))
    return jax.shard_map(shards, mesh=mesh, in_specs=in_specs, out_specs=out_specs, check_vma=False)
```

```python
import functools

import jax
import jax.numpy as jnp
from jax import lax
from jax.experimental import pallas as pl
from jax.experimental.pallas import tpu as pltpu
from jax.sharding import PartitionSpec as P

MESH = pl.DeviceIdType.MESH
BLK, S, SLOTS, RB, QB = 64, 128, 512, 128, 16
RELAX = 0.9
NZ, NY, NX, NA = 8, 4, 4, 8
GRP = 4
NPOS = SLOTS + QB * (GRP - 1)
NPOS_PAD = 640
LIST = NPOS_PAD + 128
BWD = 36
STEPS = NPOS // GRP // BWD + 1
OWN = 256
CH = OWN + 8
VM = pl.BlockSpec(memory_space=pltpu.VMEM)
SM = pl.BlockSpec(memory_space=pltpu.SMEM)
MIB = 1024 * 1024


def cost(us):
    return pl.CostEstimate(flops=int(us * 1.15e9), bytes_accessed=0, transcendentals=0)


def vmem(*shape, dtype=jnp.float32):
    return pltpu.VMEM(shape, dtype)


def split_bf16(x):
    hi = x.astype(jnp.bfloat16)
    return hi, (x - hi.astype(jnp.float32)).astype(jnp.bfloat16)


def sign_of(i):
    return 1 if i % 2 == 0 else -1


class Ang:
    def __init__(self):
        self.pix, me = lax.axis_index("pix"), lax.axis_index("ang")
        self.me, self.x, self.core = me, me // 2, lax.rem(me, 2)

    def index(self, dx):
        return lax.rem(self.x + dx % NX, NX) * 2 + self.core

    def twin(self, dx=0):
        return lax.rem(self.x + dx % NX, NX) * 2 + (1 - self.core)

    def device(self, to):
        if to == "twin":
            return (self.pix, self.twin())
        return (self.pix, self.twin(to // 2) if to % 2 == 0 else self.index(to))

    def meet(self, others):
        barrier = pltpu.get_barrier_semaphore()
        for to in others:
            pl.semaphore_signal(barrier, inc=1, device_id=self.device(to), device_id_type=MESH)
        return lambda: pl.semaphore_wait(barrier, len(others))


def sort_tiles(ray, pix, used_tiles, table):
    f32 = jnp.float32
    both = jnp.broadcast_to((pix * RB + ray).astype(f32), (128, SLOTS)).T.astype(jnp.int32)
    lane = lax.broadcasted_iota(jnp.int32, (SLOTS, 128), 1)
    t = lax.broadcasted_iota(jnp.int32, (SLOTS, 128), 0)
    q = lax.shift_right_logical(both, 7)
    mine = jnp.where((q == lane) & (t < used_tiles), 1.0, 0.0).astype(f32)
    slot = jnp.sum(jnp.where((both & (RB - 1)) == lane, table.astype(f32), 0.0), axis=1, keepdims=True)
    earlier = lax.broadcasted_iota(jnp.int32, (SLOTS, SLOTS), 1) < lax.broadcasted_iota(jnp.int32, (SLOTS, SLOTS), 0)
    earlier = jnp.where(earlier, 1.0, 0.0).astype(jnp.bfloat16)
    before = jnp.dot(earlier, mine.astype(jnp.bfloat16), preferred_element_type=f32)
    counts = jnp.sum(mine, axis=0, keepdims=True).astype(jnp.int32)
    groups = lax.shift_right_logical(counts + (GRP - 1), 2).astype(f32)
    left_of = lax.broadcasted_iota(jnp.int32, (128, 128), 0) < lax.broadcasted_iota(jnp.int32, (128, 128), 1)
    left_of = jnp.where(left_of, 1.0, 0.0).astype(jnp.bfloat16)
    first = jnp.dot(jnp.broadcast_to(groups, (8, 128)).astype(jnp.bfloat16), left_of, preferred_element_type=f32)
    place = jnp.sum(mine * (before + GRP * first[:1]), axis=1, keepdims=True)
    place = jnp.where(t < used_tiles, place, -1.0)
    code = ((1 << 20) + q * (1 << 16) + t * RB).astype(f32) + slot
    parts = []
    for c in range(NPOS_PAD // 128):
        at = (lax.broadcasted_iota(jnp.int32, (1, 128), 1) + c * 128).astype(f32)
        part = jnp.sum(jnp.where(place == at, code, 0.0), axis=0, keepdims=True)
        parts.append(jnp.where(at == NPOS_PAD - 1, jnp.sum(groups, axis=1, keepdims=True), part))
    parts.append(jnp.where(groups > 0.0, first[:1] + groups - 1.0, -1.0))
    return jnp.concatenate(parts, axis=1).astype(jnp.int32)


def gather_kernel(
    index_ref, img_ref, out_ref, code_ref, send_sem, recv_sem
):
    here = Ang()
    here.meet(("twin", 1, -1, 2, -2))()
    number = iter(range(13))

    def send(to, dx, half, src=None):
        lo, size = (0, 128) if half is None else (64 * half, 64)
        rows = out_ref.at[pl.ds(pl.multiple_of(here.index(dx) * 128 + lo, 64), size)]
        i = next(number)
        copy = pltpu.make_async_remote_copy(
            src_ref=rows if src is None else src.at[pl.ds(lo, size)],
            dst_ref=rows,
            send_sem=send_sem.at[i],
            recv_sem=recv_sem.at[i],
            device_id=here.device(to),
            device_id_type=MESH,
        )
        copy.start()
        return copy

    far = [send(sign_of(h), 0, h, img_ref) for h in range(2)]
    near = [send(-sign_of(h), 0, h, img_ref) for h in range(2)]
    across = [send("twin", 0, None, img_ref)]
    out_ref[pl.ds(pl.multiple_of(here.me * 128, 128), 128), :] = img_ref[...]
    ray, pix = index_ref[:, :SLOTS], index_ref[:, SLOTS : 2 * SLOTS]
    table, used_tiles = index_ref[:, 2 * SLOTS : 2 * SLOTS + RB], index_ref[:, 2 * SLOTS + RB :]
    code_ref[...] = sort_tiles(ray, pix, used_tiles, table)
    second = []
    for h in range(2):
        far[h].wait_recv()
        second += [send(sign_of(h), -sign_of(h), h), send(2 * sign_of(h), -sign_of(h), h)]
        across.append(send("twin", -sign_of(h), h))
    for h in range(2):
        near[h].wait_recv()
        across.append(send("twin", sign_of(h), h))
    across += second
    for copy in across:
        copy.wait_recv()
    for copy in far + near + across:
        copy.wait_send()


def gather_image(index, image):
    return pl.pallas_call(
        gather_kernel,
        out_shape=(
            jax.ShapeDtypeStruct((NA * 128, S), jnp.float32),
            jax.ShapeDtypeStruct((1, LIST), jnp.int32),
        ),
        in_specs=[VM, VM],
        out_specs=(VM, VM),
        scratch_shapes=[
            pltpu.SemaphoreType.DMA((13,)),
            pltpu.SemaphoreType.DMA((13,)),
        ],
        compiler_params=pltpu.CompilerParams(
            collective_id=0, has_side_effects=True, vmem_limit_bytes=24 * MIB
        ),
        cost_estimate=cost(8),
        name="gather_image",
    )(index, image)


def tile_rows(tiles_ref, code):
    t = lax.shift_right_logical(code, 7) & (SLOTS - 1)
    start = lax.shift_right_logical(t, 3) * 256 + (t & 7)
    used = lax.shift_right_logical(code, 20).astype(jnp.float32)
    return tiles_ref[pl.ds(start, 32, stride=8), :] * used


FWD = 24


def forward_kernel(code_ref, tiles_ref, img_ref, p_ref, col_ref, turned_ref, w_ref, rowacc, colacc):
    zero = jnp.zeros((BLK, S), jnp.bfloat16)

    def weights(q, _):
        hi, lo = split_bf16(img_ref[pl.ds(pl.multiple_of(q * BLK, BLK), BLK), :])
        both = [jnp.concatenate([jnp.concatenate([x, zero], 1), jnp.concatenate([zero, x], 1)], 0) for x in (hi, lo)]
        w_ref[q] = jnp.concatenate([both[0], both[0], both[1]], axis=0)
        return _

    lax.fori_loop(0, QB, weights, 0, unroll=4)
    rowacc[...] = jnp.zeros_like(rowacc)
    colacc[...] = jnp.zeros_like(colacc)

    def clear(o, _):
        p_ref[o] = jnp.zeros((CH, S), jnp.float32)
        return _

    lax.fori_loop(0, NZ * NY, clear, 0, unroll=4)

    def place(slot):
        rows = pl.ds(pl.multiple_of((slot & 3) * BLK, BLK), BLK)
        return lax.shift_right_logical(slot, 2), rows, slice(None)

    def read(slot):
        return p_ref[place(slot)]

    def write(slot, value):
        p_ref[place(slot)] = value

    def read_rows(slot):
        return rowacc[slot]

    def write_rows(slot, value):
        rowacc[slot] = value

    def step(b, _):
        for i in range(FWD):
            codes = [code_ref[0, (b * FWD + i) * GRP + j] for j in range(GRP)]
            q = lax.shift_right_logical(codes[0], 16) & (QB - 1)
            slots = [c & (RB - 1) for c in codes]
            tiles = [tile_rows(tiles_ref, c) for c in codes]
            hi, lo = split_bf16(jnp.concatenate(tiles, axis=0))
            turned_ref[b * FWD + i] = jnp.concatenate([hi.T, lo.T], axis=1)
            out = jnp.dot(jnp.concatenate([hi, lo, hi], axis=1), w_ref[q], preferred_element_type=jnp.float32)
            terms = [
                jnp.concatenate([out[32 * j : 32 * j + 32, h * S : h * S + S] for h in range(2)], axis=0)
                for j in range(GRP)
            ]
            for k, v in zip(slots, tiles):
                rowacc[k] += v
            colacc[q] += (tiles[0] + tiles[1]) + (tiles[2] + tiles[3])
            for k, v in zip(slots, terms):
                write(k, read(k) + v)
        return _

    lax.fori_loop(0, (code_ref[0, NPOS_PAD - 1] + FWD - 1) // FWD, step, 0)

    lane = lax.broadcasted_iota(jnp.int32, (8, 256), 1)
    pick = lax.broadcasted_iota(jnp.int32, (8, 256), 0) == (lane & 127) // BLK
    pick = pick.astype(jnp.float32).astype(jnp.bfloat16)

    def row_sums(o, _):
        both = jnp.concatenate(split_bf16(rowacc[pl.ds(o * 8, 8)].reshape(256, 128)), axis=1)
        sums = lax.dot_general(pick, both, (((1,), (1,)), ((), ())), preferred_element_type=jnp.float32)
        p_ref[2 * o, OWN:CH, :] = sums[:, :128]
        p_ref[2 * o + 1, OWN:CH, :] = sums[:, 128:]
        return _

    lax.fori_loop(0, NZ * NY // 2, row_sums, 0, unroll=8)
    low = lax.broadcasted_iota(jnp.int32, (1, 128), 1) < BLK
    for o in range(NA):
        a = jnp.sum(colacc[2 * o], axis=0, keepdims=True)
        b = jnp.sum(colacc[2 * o + 1], axis=0, keepdims=True)
        a = a + pltpu.roll(a, BLK, 1)
        b = b + pltpu.roll(b, BLK, 1)
        col_ref[o] = jnp.broadcast_to(jnp.where(low, a, b), (8, 128))


def forward(code, tiles, img):
    return pl.pallas_call(
        forward_kernel,
        out_shape=(
            jax.ShapeDtypeStruct((NZ * NY, CH, S), jnp.float32),
            jax.ShapeDtypeStruct((NA, 8, 128), jnp.float32),
            jax.ShapeDtypeStruct((STEPS * BWD, 128, 2 * 128), jnp.bfloat16),
        ),
        in_specs=[SM, VM, VM],
        out_specs=(VM, VM, VM),
        scratch_shapes=[
            vmem(QB, 6 * BLK, 2 * S, dtype=jnp.bfloat16),
            vmem(RB, 32, 128),
            vmem(QB, 32, 128),
        ],
        compiler_params=pltpu.CompilerParams(vmem_limit_bytes=32 * MIB),
        cost_estimate=cost(13),
        name="forward_tiles",
    )(code, tiles, img)


def ring_steps(n, sign):
    return ((sign, n // 2), (-sign, n // 2 - 1))


class Task:
    def __init__(self, key, link, rows, needs):
        self.key, self.link, self.rows, self.needs = key, link, rows, needs


def schedule(tasks, latency, rate):
    by_key = {t.key: t for t in tasks}
    follow = {t.key: [] for t in tasks}
    for t in tasks:
        for k in t.needs:
            follow[k].append(t.key)
    tail = {}

    def tail_of(k):
        if k not in tail:
            t = by_key[k]
            tail[k] = t.rows / rate + latency + max([tail_of(f) for f in follow[k]], default=0.0)
        return tail[k]

    left, done, free, order = list(tasks), {}, {}, []
    while left:
        best = None
        for t in left:
            if all(k in done for k in t.needs):
                at = max([done[k] for k in t.needs], default=0.0)
                start = max(at, free.get(t.link, 0.0))
                rank = (start, -tail_of(t.key))
                if best is None or rank < best[0]:
                    best = (rank, t)
        (start, _), t = best
        free[t.link] = start + t.rows / rate
        done[t.key] = start + t.rows / rate + latency
        order.append((start, t.key))
        left.remove(t)
    return [k for _, k in sorted(order, key=lambda e: e[0])]


RATE = 95.0
LATENCY = 2.5

SUM_A = (0, 104)
SUM_B = (104, 264)
ALL_A = (0, 104)
ALL_B = (104, 256)


def halves(span):
    lo, hi = span
    mid = lo + ((hi - lo) // 2 + 7) // 8 * 8
    return ((lo, mid), (mid, hi))


def sum_tasks():
    tasks = []

    def ring(stage, n, axis, piece, sign, rows, local_needs):
        for chain, (d, steps) in enumerate(ring_steps(n, sign)):
            for s in range(1, steps + 1):
                off = (d * (steps - s + 1)) % n
                needs = [(stage, piece, chain, s - 1)] if s > 1 else []
                tasks.append(Task((stage, piece, chain, s), (axis, d), rows, needs + local_needs(off)))

    def last(stage, n, piece):
        return [(stage, piece, 0, n // 2), (stage, piece, 1, n // 2 - 1)]

    for yo in range(NY):
        ring("a1", NZ, "z", yo, sign_of(yo), SUM_A[1] - SUM_A[0], lambda off: [])
    for h, (lo, hi) in enumerate(halves(SUM_A)):
        ring("a2", NY, "y", h, sign_of(h), hi - lo, lambda off: last("a1", NZ, off))
    for zo in range(NZ):
        ring("b1", NY, "y", zo, sign_of(zo), SUM_B[1] - SUM_B[0], lambda off: [])
    for h, (lo, hi) in enumerate(halves(SUM_B)):
        ring("b2", NZ, "z", h, sign_of(h), hi - lo, lambda off: last("b1", NY, off))
    return tasks


def all_tasks():
    tasks = []

    def ring(stage, n, axis, piece, sign, rows, first_needs):
        for chain, (d, steps) in enumerate(ring_steps(n, sign)):
            for s in range(1, steps + 1):
                needs = [(stage, piece, chain, s - 1)] if s > 1 else first_needs
                tasks.append(Task((stage, piece, chain, s), (axis, d), rows, needs))

    def arrives(stage, n, piece, sign, off):
        for chain, (d, steps) in enumerate(ring_steps(n, sign)):
            for s in range(1, steps + 1):
                if (-d * s) % n == off:
                    return (stage, piece, chain, s)

    for h, (lo, hi) in enumerate(halves(ALL_A)):
        ring("c1", NY, "y", h, sign_of(h), hi - lo, [])
    for yo in range(NY):
        needs = [arrives("c1", NY, h, sign_of(h), yo) for h in range(2)] if yo else []
        ring("c2", NZ, "z", yo, sign_of(yo), ALL_A[1] - ALL_A[0], needs)
    for h, (lo, hi) in enumerate(halves(ALL_B)):
        ring("d1", NZ, "z", h, sign_of(h), hi - lo, [])
    for zo in range(NZ):
        needs = [arrives("d1", NZ, h, sign_of(h), zo) for h in range(2)] if zo else []
        ring("d2", NY, "y", zo, sign_of(zo), ALL_B[1] - ALL_B[0], needs)
    return tasks


AHEAD = 3


def exchange_kernel(
    p_ref, meas_ref, resid_ref, hi_ref, lo_ref, all_ref, ra1, ra2, rb1, rb2, own, send_sem, recv_sem
):
    pix, ang = lax.axis_index("pix"), lax.axis_index("ang")
    z, y = pix // NY, lax.rem(pix, NY)

    def at(zo, yo):
        return lax.rem(z + zo % NZ, NZ) * NY + lax.rem(y + yo % NY, NY)

    def device(link):
        axis, d = link
        return (at(d, 0) if axis == "z" else at(0, d), ang)

    barrier = pltpu.get_barrier_semaphore()
    for link in (("z", 1), ("z", -1), ("y", 1), ("y", -1)):
        pl.semaphore_signal(barrier, inc=1, device_id=device(link), device_id_type=MESH)
    pl.semaphore_wait(barrier, 4)

    tasks = sum_tasks() + all_tasks()
    number = {t.key: i for i, t in enumerate(tasks)}
    by_key = {t.key: t for t in tasks}
    sums = schedule(sum_tasks(), LATENCY, RATE)
    alls = schedule(all_tasks(), LATENCY, RATE)

    a_rows, b_rows = pl.ds(SUM_A[0], SUM_A[1] - SUM_A[0]), pl.ds(SUM_B[0], SUM_B[1] - SUM_B[0])
    slot_of = {}
    for stage, ref in (("a1", ra1), ("a2", ra2), ("b1", rb1), ("b2", rb2)):
        keys = [t.key for t in tasks if t.key[0] == stage]
        for i, k in enumerate(keys):
            slot_of[k] = ref.at[i, pl.ds(0, by_key[k].rows)]

    def chain_of(n, piece, chain):
        return ring_steps(n, sign_of(piece))[chain]

    def origin(key):
        stage, piece, chain, s = key
        if stage in ("c1", "d1"):
            n = NY if stage == "c1" else NZ
            d, _ = chain_of(n, piece, chain)
            off = -d * (s - 1)
            lo, hi = halves(ALL_A if stage == "c1" else ALL_B)[piece]
            return (at(0, off) if stage == "c1" else at(off, 0)), pl.ds(lo, hi - lo)
        n = NZ if stage == "c2" else NY
        d, _ = chain_of(n, piece, chain)
        off = -d * (s - 1)
        lo, hi = ALL_A if stage == "c2" else ALL_B
        return (at(off, piece) if stage == "c2" else at(piece, off)), pl.ds(lo, hi - lo)

    def source(key):
        stage, piece, chain, s = key
        if stage in ("c1", "c2", "d1", "d2"):
            owner, rows = origin(key)
            ref = all_ref.at[owner, rows]
            return ref, ref
        dst = slot_of[key]
        if s > 1:
            return slot_of[(stage, piece, chain, s - 1)], dst
        return local(key), dst

    def local(key):
        stage, piece, chain, s = key
        if stage in ("a1", "b1"):
            n = NZ if stage == "a1" else NY
            d, steps = chain_of(n, piece, chain)
            off = d * (steps - s + 1)
            return p_ref.at[at(off, piece), a_rows] if stage == "a1" else p_ref.at[at(piece, off), b_rows]
        n = NY if stage == "a2" else NZ
        d, steps = chain_of(n, piece, chain)
        off = (d * (steps - s + 1)) % n
        span = SUM_A if stage == "a2" else SUM_B
        lo, hi = halves(span)[piece]
        first = ("a1" if stage == "a2" else "b1", off, 0, n_first(stage) // 2)
        return slot_of[first].at[pl.ds(lo - span[0], hi - lo)]

    def n_first(stage):
        return NZ if stage == "a2" else NY

    copies = {}

    def copy_of(key):
        if key not in copies:
            src, dst = source(key)
            i = number[key]
            copies[key] = pltpu.make_async_remote_copy(
                src_ref=src,
                dst_ref=dst,
                send_sem=send_sem.at[i],
                recv_sem=recv_sem.at[i],
                device_id=device(by_key[key].link),
                device_id_type=MESH,
            )
        return copies[key]

    received, sent, waited, finished = set(), {}, set(), set()

    def receive(key):
        if key not in received:
            received.add(key)
            copy_of(key).wait_recv()

    def finish(stage, off):
        if (stage, off) in finished:
            return
        finished.add((stage, off))
        n = NZ if stage == "a1" else NY
        one, two = (stage, off, 0, n // 2), (stage, off, 1, n // 2 - 1)
        receive(one)
        receive(two)
        mine = p_ref.at[at(0, off), a_rows] if stage == "a1" else p_ref.at[at(off, 0), b_rows]
        slot_of[one][...] = slot_of[one][...] + slot_of[two][...] + mine[...]

    def issue(key):
        stage, piece, chain, s = key
        task = by_key[key]
        queue = sent.setdefault(task.link, [])
        if len(queue) >= AHEAD:
            old = queue[-AHEAD]
            if old not in waited:
                waited.add(old)
                copy_of(old).wait_send()
        for k in task.needs:
            if stage in ("a2", "b2") and k[0] in ("a1", "b1"):
                finish(k[0], k[1])
            else:
                receive(k)
        if s > 1 and stage in ("a1", "a2", "b1", "b2"):
            ref = slot_of[(stage, piece, chain, s - 1)]
            ref[...] = ref[...] + local(key)[...]
        copy_of(key).start()
        queue.append(key)

    for key in sums:
        issue(key)
    for stage, span, n, n1 in (("a2", SUM_A, NY, NZ), ("b2", SUM_B, NZ, NY)):
        first = "a1" if stage == "a2" else "b1"
        finish(first, 0)
        for h, (lo, hi) in enumerate(halves(span)):
            one, two = (stage, h, 0, n // 2), (stage, h, 1, n // 2 - 1)
            receive(one)
            receive(two)
            mine = slot_of[(first, 0, 0, n1 // 2)].at[pl.ds(lo - span[0], hi - lo)]
            own[lo:hi, :] = slot_of[one][...] + slot_of[two][...] + mine[...]

    norms = [jnp.broadcast_to(own[OWN + h : OWN + h + 1, :], (128, 128)).T for h in range(2)]
    for b in range(4):
        for h in range(2):
            natural = pl.ds(b * BLK + h, 32, stride=2)
            mine = slice(b * BLK + 32 * h, b * BLK + 32 * h + 32)
            value = (meas_ref[natural, :] - own[mine, :]) / norms[h][32 * b : 32 * b + 32]
            resid_ref[natural, :] = value
            all_ref[at(0, 0), mine, :] = value

    def place(key):
        stage, piece, chain, s = key
        d, _ = chain_of(NY if stage in ("c1", "d2") else NZ, piece, chain)
        off = -d * s
        if stage == "c1":
            return 0, off % NY
        if stage == "d1":
            return off % NZ, 0
        return (off % NZ, piece) if stage == "c2" else (piece, off % NY)

    parts = {}
    for key in alls:
        parts.setdefault(place(key), []).append(key)

    def split(where):
        o = at(*where)
        rows = pl.ds(pl.multiple_of(o * 8, 8), 8)
        hi_ref[rows], lo_ref[rows] = split_bf16(all_ref[o].reshape(8, 32, S))

    def split_whole():
        for where in list(parts):
            if all(k in received for k in parts[where]):
                del parts[where]
                split(where)

    for i, key in enumerate(alls):
        issue(key)
        if i == 8:
            split((0, 0))
        split_whole()
    for key in alls:
        receive(key)
        split_whole()
    for t in tasks:
        receive(t.key)
    for t in tasks:
        if t.key not in waited:
            copy_of(t.key).wait_send()


def exchange(p, measured):
    tasks = sum_tasks() + all_tasks()
    count = {}
    for t in tasks:
        count[t.key[0]] = count.get(t.key[0], 0) + 1
    most = {k: max(t.rows for t in tasks if t.key[0] == k) for k in count}
    return pl.pallas_call(
        exchange_kernel,
        out_shape=(
            jax.ShapeDtypeStruct((OWN, S), jnp.float32),
            jax.ShapeDtypeStruct((RB * 2, 32, S), jnp.bfloat16),
            jax.ShapeDtypeStruct((RB * 2, 32, S), jnp.bfloat16),
        ),
        in_specs=[VM, VM],
        out_specs=(VM, VM, VM),
        scratch_shapes=[vmem(NZ * NY, OWN, S)]
        + [vmem(count[k], most[k], S) for k in ("a1", "a2", "b1", "b2")]
        + [
            vmem(CH, S),
            pltpu.SemaphoreType.DMA((len(tasks),)),
            pltpu.SemaphoreType.DMA((len(tasks),)),
        ],
        compiler_params=pltpu.CompilerParams(
            collective_id=1, has_side_effects=True, vmem_limit_bytes=24 * MIB
        ),
        cost_estimate=cost(50),
        name="sum_and_spread",
    )(p, measured)


UPD = ((0, 72), (72, 136))


def backward_kernel(
    code_ref, turned_ref, hi_ref, lo_ref, col_ref, out_ref, run_ref, b_ref, sib, far_buf, near_buf, second_buf,
    send_sem, recv_sem,
):
    here = Ang()
    wait_for_others = here.meet(("twin", 1, -1))

    def pixel_block(g):
        return lax.shift_right_logical(code_ref[0, g * GRP], 16) & (QB - 1)

    def step(b, run):
        for i in range(BWD):
            g = b * BWD + i
            codes = [code_ref[0, g * GRP + j] for j in range(GRP)]
            hi, lo = turned_ref[g, :, :128], turned_ref[g, :, 128:]
            slots = [c & (RB - 1) for c in codes]

            def rays(ref):
                return [ref[slot * 2 + h] for h in range(2) for slot in slots]

            r_hi, r_lo = rays(hi_ref), rays(lo_ref)
            left = jnp.concatenate([hi[:BLK], hi[BLK:], lo[:BLK], lo[BLK:], hi[:BLK], hi[BLK:]], axis=1)
            right = jnp.concatenate(r_hi + r_hi + r_lo, axis=0)
            out = jnp.dot(left, right, preferred_element_type=jnp.float32)
            before = pixel_block(jnp.maximum(g - 1, 0))
            run = run * (before == pixel_block(g)).astype(jnp.float32) + out
            run_ref[g] = run
        return run

    lax.fori_loop(0, STEPS, step, jnp.zeros((BLK, S), jnp.float32))
    for q in range(QB):
        last = code_ref[0, NPOS_PAD + q]
        total = run_ref[jnp.maximum(last, 0)]
        b_ref[q // 2, q % 2 * BLK : q % 2 * BLK + BLK, :] = total * (last >= 0).astype(jnp.float32)
    for o in range(NA):
        b_ref[o, 128:136, :] = col_ref[o]

    wait_for_others()
    number = iter(range(10))

    def send(to, src, dst):
        i = next(number)
        copy = pltpu.make_async_remote_copy(
            src_ref=src,
            dst_ref=dst,
            send_sem=send_sem.at[i],
            recv_sem=recv_sem.at[i],
            device_id=here.device(to),
            device_id_type=MESH,
        )
        copy.start()
        return copy

    across = {dx: send("twin", b_ref.at[here.twin(dx)], sib.at[dx]) for dx in (2, 1, 3, 0)}

    def arrive(dx):
        across[dx].wait_recv()
        sib[dx] = sib[dx] + b_ref[here.index(dx)]

    def rows(h):
        return pl.ds(UPD[h][0], UPD[h][1] - UPD[h][0])

    def part(buf, h):
        return buf.at[h, pl.ds(0, UPD[h][1] - UPD[h][0])]

    arrive(2)
    far = [send(sign_of(h), sib.at[2, rows(h)], part(far_buf, h)) for h in range(2)]
    arrive(1)
    arrive(3)
    near = [send(-sign_of(h), sib.at[-sign_of(h) % NX, rows(h)], part(near_buf, h)) for h in range(2)]
    arrive(0)
    second = []
    for h in range(2):
        far[h].wait_recv()
        part(far_buf, h)[...] = part(far_buf, h)[...] + sib[sign_of(h) % NX, rows(h), :]
        second.append(send(sign_of(h), part(far_buf, h), part(second_buf, h)))
    totals = []
    for h in range(2):
        near[h].wait_recv()
        totals.append(sib[0, rows(h), :] + part(near_buf, h)[...])
    for h in range(2):
        second[h].wait_recv()
        totals[h] = totals[h] + part(second_buf, h)[...]
    total = jnp.concatenate(totals, axis=0)
    norm = jnp.broadcast_to(total[128:129], (128, 128)).T
    out_ref[...] = RELAX * total[:128] / norm
    for copy in [*across.values(), *far, *near, *second]:
        copy.wait_send()


def backward(code, turned, high, low, col):
    size = UPD[0][1]
    return pl.pallas_call(
        backward_kernel,
        out_shape=jax.ShapeDtypeStruct((128, S), jnp.float32),
        in_specs=[SM, VM, VM, VM, VM],
        out_specs=VM,
        scratch_shapes=[
            vmem(STEPS * BWD, BLK, S),
            vmem(NA, 136, S),
            vmem(NX, 136, S),
            vmem(2, size, S),
            vmem(2, size, S),
            vmem(2, size, S),
            pltpu.SemaphoreType.DMA((10,)),
            pltpu.SemaphoreType.DMA((10,)),
        ],
        compiler_params=pltpu.CompilerParams(
            collective_id=2, has_side_effects=True, vmem_limit_bytes=32 * MIB
        ),
        cost_estimate=cost(17),
        name="backward_and_sum",
    )(code, turned, high, low, col)


def finish_kernel(image_ref, step_ref, own_ref, new_ref, resid_ref):
    resid_ref[...] = own_ref[...]
    new_ref[...] = image_ref[...] + step_ref[...]


def finish(image, step, own):
    return pl.pallas_call(
        finish_kernel,
        out_shape=(
            jax.ShapeDtypeStruct((128, S), jnp.float32),
            jax.ShapeDtypeStruct((OWN, S), jnp.float32),
        ),
        in_specs=[VM, VM, VM],
        out_specs=(VM, VM),
        compiler_params=pltpu.CompilerParams(vmem_limit_bytes=24 * MIB),
        cost_estimate=cost(1),
        name="new_image",
    )(image, step, own)


def shards(tiles, tile_ray, tile_pix, tile_count, ray_slot, image, measured):
    rows = tiles[0, 0].reshape(SLOTS // 8, 8, 32, 128).transpose(0, 2, 1, 3).reshape(SLOTS * 32, 128)
    used_tiles = jnp.broadcast_to(tile_count[0], (RB,))
    index = jnp.concatenate([tile_ray[0, 0], tile_pix[0, 0], ray_slot[0], used_tiles])[None]
    img, code = gather_image(index, image)
    p, col, turned = forward(code, rows, img)
    own, high, low = exchange(p, measured[0])
    new_image, resid = finish(image, backward(code, turned, high, low, col), own)
    return (new_image, resid[None])


def solution(mesh):
    in_specs = (
        P("pix", "ang", None, None),
        P("pix", "ang", None),
        P("pix", "ang", None),
        P("pix", "ang"),
        P("ang", None),
        P(("pix", "ang"), None),
        P("ang", "pix", None),
    )
    out_specs = (P(("pix", "ang"), None), P("ang", "pix", None))
    return jax.shard_map(shards, mesh=mesh, in_specs=in_specs, out_specs=out_specs, check_vma=False)
```
